128 devices in a mesh: grp: 4 (over z_hi, core), dom: 32 (over x, y, z_lo).
Axes of the slice: x: 4, y: 4, z: 4 (z_hi: 2, z_lo: 2; z = z_hi * 2 + z_lo), core: 2. Of those that a mesh axis runs over, the one named last changes fastest.
Arguments:
- state: float32 [4, 3, 32, 65536], P('grp', None, None, 'dom'), may hold values from -4 to 4, as said below
- kappa: float32 [4, 65536], P('grp', 'dom'), may hold values from 0.02 to 0.3
- neighbours: int32 [4, 3, 65536], P('grp', None, 'dom'), may hold values from 0 to 2111, as said below
- parent: int32 [4, 65536], P('grp', 'dom'), may hold values from 0 to 511, as said below
- cos_zenith: float32 [4, 16384], P('grp', 'dom'), may hold values from -1 to 1
- routes: int32 [128, 32, 1], P(('grp', 'dom')), may hold values from 0 to 31; in each aligned block of 32 rows (0 to 31, 32 to 63, ..., all dimensions but the last counted through in order) at most 2 rows name the same one
- rad_albedo: float32 [4, 98304], P('grp', 'dom'), may hold values from 0.05 to 0.8
- aerosol_depth: float32 [4, 32, 14, 98304], P('grp', None, None, 'dom'), may hold values from 0.01 to 0.5
- aerosol_ssa: float32 [4, 32, 14, 98304], P('grp', None, None, 'dom'), may hold values from 0.3 to 0.99
- gas_table: float32 [112, 32], replicated, may hold values from 0.002 to 0.3
- cloud_ext: float32 [112], replicated, may hold values from 0.05 to 1
- cloud_ssa: float32 [112], replicated, may hold values from 0.5 to 0.99
- rayleigh: float32 [112], replicated, may hold values from 0.01 to 0.25
- solar_weight: float32 [112], replicated, may hold values from 0.1 to 1
Outputs:
- new_state: float32 [4, 3, 32, 65536], P('grp', None, None, 'dom')
The draws below stay inside these ranges and needn't reach their ends.
Inputs may be any that keep to these rules, and one draw needn't show every extreme that they name: `state`: field 0 is a temperature anomaly; fields 1 and 2 are positive. `neighbours`: every neighbour lies within 32 cells of the cell's own position. Within each domain every coarse column is the parent of exactly four fine cells. `routes`: among the blocks of one device at most 2 go to one radiation domain.
All inputs are finite; a program needn't handle non-finite values.
Results may differ from the reference program's by a relative error of at most 0.0001.
Values sent between devices are 32-bit elements; how exact they have to be, the bound alone decides.
No kernel may reach another device: no remote copies, remote signals or barrier semaphores. Data moves between devices by JAX's collectives and lax.ppermute only.
A program may use at most 192 MiB of HBM per device.

```python
import math
import jax
import jax.numpy as jnp
import numpy as np
from jax import lax

FIELDS = 3
LEV = 32
GPOINTS = 112
BANDS = 14
NODES = 32
CELL_DEV = 2048
HALO = 32
BLOCKS = 32
COARSE_DEV = 512
BLOCK_COLS = 16
BLOCK_MOST = 2
SLOT_COLS = 32
RAD_COLS = 3072
RAD_SLOTS = 98304
CELLS = 65536
COARSE = 16384
N_GRP = 4
N_DOM = 32


def draw_state(key, part):
    key = jax.random.fold_in(key, 5)
    starting_seed_handle, second_key, third_key = jax.random.split(key, 3)
    tensor_extents = (N_GRP, 1, LEV, CELLS)
    thermal_state_kelvin = jnp.clip(jax.random.normal(starting_seed_handle, tensor_extents, jnp.float32), -4.0, 4.0)
    humidity_mixing_ratio = jnp.exp(jax.random.uniform(second_key, tensor_extents, jnp.float32, math.log(0.2), math.log(2.0)))
    droplet_mixing_ratio = jnp.exp(jax.random.uniform(third_key, tensor_extents, jnp.float32, math.log(0.02), math.log(1.0)))
    return jnp.concatenate([thermal_state_kelvin, humidity_mixing_ratio, droplet_mixing_ratio], axis=1).astype(jnp.float32)


def draw_neighbours(key, part):
    key = jax.random.fold_in(key, 11)
    domains = CELLS // CELL_DEV
    offsets = jax.random.randint(key, (N_GRP, 3, domains, CELL_DEV), -HALO, HALO + 1, dtype=jnp.int32)
    cell_ids = jnp.arange(CELL_DEV, dtype=jnp.int32)
    entries = HALO + cell_ids[None, None, None, :] + offsets
    entries = entries.at[:, 0, :, 0].set(0)
    entries = entries.at[:, 2, :, CELL_DEV - 1].set(CELL_DEV + 2 * HALO - 1)
    return entries.reshape(N_GRP, 3, CELLS).astype(jnp.int32)


def draw_parent(key, part):
    key = jax.random.fold_in(key, 17)
    domains = CELLS // CELL_DEV
    keys = jax.random.split(key, N_GRP * domains)
    orders = jax.vmap(lambda single_key: jax.random.permutation(single_key, CELL_DEV))(keys)
    return (orders.astype(jnp.int32) // 4).reshape(N_GRP, CELLS)


def block_scale(key, shape, cuts, least, high):
    level = 1.0
    for dim, parts in cuts:
        heights = jax.random.uniform(jax.random.fold_in(jax.random.fold_in(key, 6), dim), (parts,), jnp.float32, least / len(cuts), high / len(cuts))
        level = level * jnp.repeat(jnp.exp(heights), shape[dim] // parts).reshape((-1,) + (1,) * (len(shape) - 1 - dim))
    return level


def deal_out(own_key, own, number, rows, number_of, top, reach, slope):
    ranking = jax.random.permutation(own_key, number_of)
    crowded, ordinary = load_shares(number_of, rows * top, reach, slope, True), load_shares(number_of, rows * top, reach, slope, False)
    places = jnp.arange(number_of)

    def named(tallies, offset_by):
        used = int((tallies > 0).sum())
        fixed = max(1, used // 4)
        moved = fixed + (places - fixed + offset_by * (used - fixed)) % max(1, number_of - fixed)
        return jnp.zeros((number_of,), jnp.int32).at[ranking[jnp.where(places < fixed, places, moved)]].set(jnp.asarray(tallies, jnp.int32))

    tallies = jnp.where(number % 4 == 0, named(crowded, number // 4), named(ordinary, number - number // 4 - 1))
    mixed = jax.random.permutation(jax.random.fold_in(own, 3), number_of)
    donor, receiver = mixed[0:number_of // 2 * 2:2], mixed[1:number_of // 2 * 2:2]
    room = jnp.minimum(tallies[donor] - 1, reach - tallies[receiver]) // 2
    room = jnp.where((donor == ranking[0]) | (receiver == ranking[0]) | (tallies[receiver] == 0), 0, jnp.maximum(room, 0))
    moved = jax.random.randint(jax.random.fold_in(own, 4), (number_of // 2,), 0, 1 << 20) % (room + 1)
    tallies = tallies.at[donor].add(-moved).at[receiver].add(moved)
    items = jnp.searchsorted(jnp.cumsum(tallies), jnp.arange(rows * top), side="right").astype(jnp.int32)
    grid = items.reshape(top, rows).T
    grid = grid[jax.random.permutation(jax.random.fold_in(own, 1), rows)]
    offset_by = jax.random.randint(jax.random.fold_in(own, 2), (rows, 1), 0, top)
    return jnp.take_along_axis(grid, (jnp.arange(top)[None, :] + offset_by) % top, axis=1)


def load_shares(number_of, total, reach, lean, full):
    loads = [(1 << 20) // math.isqrt(grade ** lean) + 1 for grade in range(1, number_of + 1)]
    largest = reach if full else min(reach, max(-(-total // number_of), total * loads[0] // sum(loads)))
    least = 1 if total - largest >= number_of - 1 else 0
    given, rest = [largest] + [least] * (number_of - 1), total - largest - least * (number_of - 1)
    while rest > 0:
        candidates = [i for i in range(1, number_of) if given[i] < largest] or [i for i in range(1, number_of) if given[i] < reach]
        whole, budget = sum([loads[i] for i in candidates]), rest
        for i in candidates:
            more = min(reach - given[i], max(1, budget * loads[i] // whole), rest)
            given[i] = given[i] + more
            rest = rest - more
    return np.array(given)


def setup_inputs(seed: int = 0) -> dict:
    streams_of = jax.random.split(jax.random.key(seed), 15)
    state = draw_state(jax.random.fold_in(streams_of[14], 71), 0)
    kappa = jnp.clip(jnp.exp(math.log(0.3) - 2.7080503 * jax.random.uniform(streams_of[1], (N_GRP, CELLS), jnp.float32) ** block_scale(streams_of[1], (N_GRP, CELLS), ((0, 4), (1, 32)), -0.2, 0.2)), 0.02, 0.3)
    neighbours = draw_neighbours(jax.random.fold_in(streams_of[14], 71), 0)
    parent = draw_parent(jax.random.fold_in(streams_of[14], 71), 0)
    cos_zenith = jnp.clip(jax.random.uniform(streams_of[4], (N_GRP, COARSE), jnp.float32, -1.0, 1.0) * block_scale(streams_of[4], (N_GRP, COARSE), ((0, 4), (1, 32)), -0.4, 0.0), -1.0, 1.0)
    routes_keys = jax.random.split(jax.random.fold_in(streams_of[5], 1), (N_GRP * N_DOM) * BLOCKS // BLOCKS)
    routes_turns = jax.random.permutation(jax.random.fold_in(streams_of[5], 3), (N_GRP * N_DOM) * BLOCKS // BLOCKS)
    routes = jax.vmap(lambda own, number: deal_out(jax.random.fold_in(streams_of[5], 2), own, number, BLOCKS, N_DOM, 1, BLOCK_MOST, 2))(routes_keys, routes_turns).reshape((N_GRP * N_DOM, BLOCKS, 1))
    rad_albedo = jnp.clip(0.05 + 0.75 * jax.random.uniform(streams_of[6], (N_GRP, RAD_SLOTS), jnp.float32) ** block_scale(streams_of[6], (N_GRP, RAD_SLOTS), ((0, 4), (1, 32)), -0.2, 0.2), 0.05, 0.8)
    aerosol_depth = jnp.clip(jnp.exp(math.log(0.5) - 3.912023 * jax.random.uniform(streams_of[7], (N_GRP, LEV, BANDS, RAD_SLOTS), jnp.float32) ** block_scale(streams_of[7], (N_GRP, LEV, BANDS, RAD_SLOTS), ((0, 4), (3, 32)), -0.2, 0.2)), 0.01, 0.5)
    aerosol_ssa = jnp.clip(0.3 + 0.69 * jax.random.uniform(streams_of[8], (N_GRP, LEV, BANDS, RAD_SLOTS), jnp.float32) ** block_scale(streams_of[8], (N_GRP, LEV, BANDS, RAD_SLOTS), ((0, 4), (3, 32)), -0.2, 0.2), 0.3, 0.99)
    gas_table = jnp.clip(jnp.exp(jax.random.uniform(streams_of[9], (GPOINTS, NODES), jnp.float32, math.log(0.002), math.log(0.3))), 0.002, 0.3)
    cloud_ext = jnp.clip(jnp.exp(jax.random.uniform(streams_of[10], (GPOINTS,), jnp.float32, math.log(0.05), math.log(1.0))), 0.05, 1.0)
    cloud_ssa = jnp.clip(jax.random.uniform(streams_of[11], (GPOINTS,), jnp.float32, 0.5, 0.99), 0.5, 0.99)
    rayleigh = jnp.clip(jnp.exp(jax.random.uniform(streams_of[12], (GPOINTS,), jnp.float32, math.log(0.01), math.log(0.25))), 0.01, 0.25)
    solar_weight = jnp.clip(jnp.exp(jax.random.uniform(streams_of[13], (GPOINTS,), jnp.float32, math.log(0.1), math.log(1.0))), 0.1, 1.0)
    return {"state": state, "kappa": kappa, "neighbours": neighbours, "parent": parent, "cos_zenith": cos_zenith, "routes": routes, "rad_albedo": rad_albedo, "aerosol_depth": aerosol_depth, "aerosol_ssa": aerosol_ssa, "gas_table": gas_table, "cloud_ext": cloud_ext, "cloud_ssa": cloud_ssa, "rayleigh": rayleigh, "solar_weight": solar_weight}


def substep(fields, extended, rates, index):
    near = jnp.take(extended, index.reshape(-1), axis=2)
    near = near.reshape(fields.shape[0], fields.shape[1], 3, fields.shape[2])
    return fields + rates * (jnp.sum(near, axis=2) - 3.0 * fields)


def radiate(stacked_layer_values, sun_cosine, albedo, aero_depth, aero_ssa, gas_table, cloud_ext, cloud_ssa, rayleigh, solar_weight):
    thermal_state_kelvin = stacked_layer_values[0]
    humidity_mixing_ratio = stacked_layer_values[1]
    droplet_mixing_ratio = stacked_layer_values[2]
    levels = stacked_layer_values.shape[1]
    band_count = gas_table.shape[0]
    node_count = gas_table.shape[1]
    per_band = band_count // aero_depth.shape[1]
    aero_wide = jnp.repeat(aero_depth, per_band, axis=1)
    aero_scatter = jnp.repeat(aero_ssa, per_band, axis=1) * aero_wide
    mesh_spacing = 8.0 / (node_count - 1)
    polygon_midpoints = -4.0 + mesh_spacing * jnp.arange(node_count).astype(jnp.float32)
    quadrature_multipliers = jnp.maximum(0.0, 1.0 - jnp.abs(thermal_state_kelvin[:, None, :] - polygon_midpoints[None, :, None]) / mesh_spacing)
    basis = humidity_mixing_ratio[:, None, :] * quadrature_multipliers
    gas_depth = jnp.einsum("gb,lbn->lgn", gas_table, basis, precision=lax.Precision.HIGHEST)
    cloud_depth = cloud_ext[None, :, None] * droplet_mixing_ratio[:, None, :]
    optical = gas_depth + cloud_depth + rayleigh[None, :, None] + aero_wide
    single_albedo = (cloud_ssa[None, :, None] * cloud_depth + rayleigh[None, :, None] + aero_scatter) / optical
    path_cosine = jnp.maximum(sun_cosine, 0.1)
    direct = jnp.exp(-optical / path_cosine[None, None, :])
    spread = 0.5 * single_albedo * (1.0 - direct)
    diffuse = jnp.exp(-1.66 * optical * (1.0 - single_albedo))
    incoming = jnp.broadcast_to(jnp.maximum(sun_cosine, 0.0)[None, :], direct.shape[1:])

    def downward(carry, layer_in):
        direct_flux, diffuse_flux = carry
        through, spread_layer, diffuse_layer = layer_in
        return (direct_flux * through, diffuse_flux * diffuse_layer + direct_flux * spread_layer), (direct_flux, diffuse_flux)

    (direct_floor, diffuse_floor), (direct_fluxes, diffuse_fluxes) = lax.scan(
        downward, (incoming, jnp.zeros_like(incoming)), (direct, spread, diffuse))
    ground = albedo[None, :] * (direct_floor + diffuse_floor)

    def upward(rising, layer_in):
        direct_layer, spread_layer, diffuse_layer = layer_in
        updated = rising * diffuse_layer + direct_layer * spread_layer
        return updated, updated

    top_rising, risings = lax.scan(upward, ground, (direct_fluxes, spread, diffuse), reverse=True)
    net_upper = direct_fluxes + diffuse_fluxes - risings
    net_floor = direct_floor + diffuse_floor - ground
    net_lower = jnp.concatenate([net_upper[1:], net_floor[None]], axis=0)
    absorbed = net_upper - net_lower
    return (levels / band_count) * jnp.einsum("g,lgn->ln", solar_weight, absorbed, precision=lax.Precision.HIGHEST)


def reference(state, kappa, neighbours, parent, cos_zenith, routes, rad_albedo, aerosol_depth, aerosol_ssa, gas_table, cloud_ext, cloud_ssa, rayleigh, solar_weight):
    cycle_len = N_DOM * CELL_DEV
    position = jnp.arange(cycle_len, dtype=jnp.int32)
    leading = (position // CELL_DEV) * CELL_DEV
    ordinal = jnp.arange(BLOCKS, dtype=jnp.int32)
    results = []
    for group_slot in range(N_GRP - 1):
        fields = state[group_slot]
        cycle_index = (leading[None, :] + neighbours[group_slot] - HALO) % cycle_len
        current = fields
        for substep_no in range(2):
            current = substep(current, current, kappa[group_slot], cycle_index.astype(jnp.int32))
        owner_ids = ((position // CELL_DEV) * COARSE_DEV + parent[group_slot]).astype(jnp.int32)
        coarse = jnp.zeros((FIELDS, LEV, N_DOM * COARSE_DEV), jnp.float32).at[:, :, owner_ids].add(fields) * 0.25
        target = routes[group_slot * N_DOM:(group_slot + 1) * N_DOM, :, 0]
        earlier = (target[:, :, None] == target[:, None, :]) & (ordinal[None, None, :] < ordinal[None, :, None])
        arrival = jnp.sum(earlier.astype(jnp.int32), axis=2)
        sender = group_slot * N_DOM + jnp.arange(N_DOM, dtype=jnp.int32)
        offset_base = target * RAD_COLS + sender[:, None] * SLOT_COLS + arrival * BLOCK_COLS
        slot_index = offset_base[:, :, None] + jnp.arange(BLOCK_COLS, dtype=jnp.int32)[None, None, :]
        flat_slots = slot_index.reshape(N_DOM, COARSE_DEV).astype(jnp.int32)
        albedo = rad_albedo[N_GRP - 1][flat_slots]
        aero_cols = jnp.transpose(aerosol_depth[N_GRP - 1][:, :, flat_slots], (2, 0, 1, 3))
        aero_ssa_cols = jnp.transpose(aerosol_ssa[N_GRP - 1][:, :, flat_slots], (2, 0, 1, 3))
        profiles = jnp.transpose(coarse.reshape(FIELDS, LEV, N_DOM, COARSE_DEV), (2, 0, 1, 3))
        sun_cosine = cos_zenith[group_slot].reshape(N_DOM, COARSE_DEV)
        heating = lax.map(lambda operand: radiate(operand[0], operand[1], operand[2], operand[3], operand[4], gas_table, cloud_ext, cloud_ssa, rayleigh, solar_weight), (profiles, sun_cosine, albedo, aero_cols, aero_ssa_cols))
        local_parent = parent[group_slot].reshape(N_DOM, CELL_DEV)
        fine_heating = jax.vmap(lambda column_heat, lineage: jnp.take(column_heat, lineage, axis=1))(heating, local_parent)
        fine_heating = jnp.transpose(fine_heating, (1, 0, 2)).reshape(LEV, cycle_len)
        warmed = jnp.concatenate([(current[0] + 0.5 * fine_heating)[None], current[1:]], axis=0)
        results.append(warmed)
    results.append(jnp.zeros_like(state[0]))
    return jnp.stack(results)
```

```python
import jax
import jax.numpy as jnp
from jax import lax
from jax.experimental import pallas as pl
from jax.experimental.pallas import tpu as pltpu
from jax.sharding import PartitionSpec as P

F32 = jnp.float32
BF16 = jnp.bfloat16
I32 = jnp.int32
HALO = 32
FIELDS, LEVELS, GPOINTS, BANDS, NODES = 3, 32, 112, 14, 32
ROWS = FIELDS * LEVELS
CELLS, COARSE = 2048, 512
BLOCKS, BLOCK_COLS, MOST = 32, 16, 2
DOMAINS, SLOTS = 32, 4
SLOT_COLS = BLOCK_COLS * MOST
LANES = 128
PER_TILE = LANES // SLOT_COLS
TILES = CELLS // LANES
UNIT = 256
UNIT_SENDERS = UNIT // SLOT_COLS
KEPT = 16
LEVEL_BLOCK = 8
LOG2E = 1.4426950408889634
VMEM_LIMIT = 56 * 1024 * 1024


def halves(x):
    high = x.astype(BF16)
    return high, (x - high.astype(F32)).astype(BF16)


def thirds(x):
    high = x.astype(BF16)
    rest = x - high.astype(F32)
    middle = rest.astype(BF16)
    return high, middle, (rest - middle.astype(F32)).astype(BF16)


def exact_dot(x, chosen, contract):
    rows = x.shape[0]
    stacked = jnp.concatenate(thirds(x), axis=0)
    product = lax.dot_general(
        stacked, chosen, (((1,), (contract,)), ((), ())), preferred_element_type=F32
    )
    return product[:rows] + product[rows : 2 * rows] + product[2 * rows :]


def iota(shape, dim):
    return lax.broadcasted_iota(I32, shape, dim)


def ones_where(mask):
    return jnp.where(mask, 1.0, 0.0).astype(BF16)


def regroup(pieces, shift_of):
    group = iota(pieces[0].shape, 1) // SLOT_COLS
    result = None
    for k, piece in enumerate(pieces):
        shift = (shift_of(k) % PER_TILE) * SLOT_COLS
        moved = pltpu.roll(piece, shift, 1) if shift else piece
        result = moved if result is None else jnp.where(group == k, moved, result)
    return result


def column(row):
    n = row.shape[1]
    return jnp.sum(jnp.where(iota((n, n), 0) == iota((n, n), 1), row, 0.0), axis=1, keepdims=True)


def coarsen_kernel(
    routes, state, parent, sun, kappa, near, gas, ext, ssa, ray, solar,
    message, edges, slots_out, weights, solar_out,
):
    block = iota((1, COARSE), 1) // BLOCK_COLS
    target = jnp.zeros((1, COARSE), I32)
    for b in range(BLOCKS):
        target = jnp.where(block == b, routes[0, b, 0], target)
    arrival = jnp.zeros((1, COARSE), I32)
    for b in range(BLOCKS):
        same = (target == routes[0, b, 0]) & (block > b)
        arrival = arrival + jnp.where(same, 1, 0)
    place = (target * MOST + arrival) * BLOCK_COLS + iota((1, COARSE), 1) % BLOCK_COLS
    slots_out[...] = place

    lineage = ones_where(iota((COARSE, CELLS), 0) == parent[...])
    coarse = 0.25 * exact_dot(state[...], lineage, 1)
    sun_rows = jnp.where(iota((8, COARSE), 0) == 0, sun[...], 0.0)
    columns = jnp.concatenate([coarse, sun_rows], axis=0)
    placed = ones_where(iota((DOMAINS * SLOT_COLS, COARSE), 0) == place)
    packed = exact_dot(columns, placed, 1)
    span = ROWS // PER_TILE
    for tile in range(DOMAINS // PER_TILE):
        part = packed[:, tile * LANES : (tile + 1) * LANES]
        for e in range(PER_TILE):
            pieces = [part[a * span : (a + 1) * span] for a in range(PER_TILE)]
            message[tile * PER_TILE + e, 0:span, :] = regroup(pieces, lambda a: a - e)
            moved = pltpu.roll(part[ROWS:], ((-e) % PER_TILE) * SLOT_COLS, 1) if e else part[ROWS:]
            message[tile * PER_TILE + e, span : span + 8, :] = moved

    for side, start in ((0, CELLS - LANES), (1, 0)):
        edges[side, 0:ROWS, :] = state[:, start : start + LANES]
        edges[side, ROWS : ROWS + 8, :] = jnp.concatenate(
            [
                kappa[:, start : start + LANES],
                near[:, start : start + LANES].astype(F32),
                jnp.zeros((4, LANES), F32),
            ],
            axis=0,
        )

    band = jnp.where(iota((GPOINTS, 16), 0) // 8 == iota((GPOINTS, 16), 1), 1.0, 0.0)
    spot = iota((GPOINTS, 16), 1)
    ext_col, ssa_col, ray_col = column(ext[...]), column(ssa[...]), column(ray[...])
    scatter_w = jnp.where(spot == BANDS, ray_col, jnp.where(spot == BANDS + 1, ssa_col * ext_col, 0.0))
    optical_w = jnp.where(spot == BANDS, ray_col, jnp.where(spot == BANDS + 1, ext_col, band))
    gas_hi, gas_lo = halves(gas[...])
    opt_hi, opt_lo = halves(optical_w)
    sca_hi, sca_lo = halves(scatter_w)
    none = jnp.zeros((GPOINTS, 16), F32)
    wide = jnp.zeros((GPOINTS, NODES), F32)
    upper = [gas_hi, gas_lo, gas_hi, opt_hi, opt_lo, opt_hi, none, none]
    lower = [wide, wide, wide, sca_hi, sca_lo, sca_hi, band, band]
    weights[0:GPOINTS, :] = (-jnp.concatenate([p.astype(F32) for p in upper], axis=1)).astype(BF16)
    weights[GPOINTS:, :] = jnp.concatenate([p.astype(F32) for p in lower], axis=1).astype(BF16)
    solar_out[...] = jnp.broadcast_to(column(solar[...]), (GPOINTS, LANES))


def diffuse_kernel(role, state, kappa, near, left, right, out, fields, rates, goal, chosen):
    for ref, start, width, shift in (
        (left, 0, LANES, LANES - HALO - CELLS),
        (right, LANES + CELLS, LANES, LANES - HALO + CELLS),
    ):
        fields[:, start : start + width] = ref[0:ROWS, :]
        rates[:, start : start + width] = ref[ROWS : ROWS + 1, :]
        goal[0:3, start : start + width] = ref[ROWS + 1 : ROWS + 4, :].astype(I32) + shift
    fields[:, LANES : LANES + CELLS] = state[...]
    rates[:, LANES : LANES + CELLS] = kappa[...]
    goal[0:3, LANES : LANES + CELLS] = near[...] + (LANES - HALO)
    window = 3 * LANES
    rows = iota((window, LANES), 0)

    def spread(tile):
        first = min(max(tile - 1, 0), TILES - 1)
        return first * LANES

    results = []
    for tile in range(TILES + 2):
        here = slice(tile * LANES, (tile + 1) * LANES)
        place = rows + spread(tile)
        count = jnp.zeros((window, LANES), F32)
        for n in range(3):
            count = count + jnp.where(place == goal[n : n + 1, here], 1.0, 0.0)
        picked = count.astype(BF16)
        chosen[tile] = picked
        own = fields[:, here]
        total = exact_dot(fields[:, spread(tile) : spread(tile) + window], picked, 0)
        results.append(own + rates[:, here] * (total - 3.0 * own))
    for tile, value in enumerate(results):
        fields[:, tile * LANES : (tile + 1) * LANES] = value
    dynamic = role[0] != SLOTS - 1
    for tile in range(1, TILES + 1):
        here = slice(tile * LANES, (tile + 1) * LANES)
        own = fields[:, here]
        total = exact_dot(fields[:, spread(tile) : spread(tile) + window], chosen[tile], 0)
        value = own + rates[:, here] * (total - 3.0 * own)
        out[:, (tile - 1) * LANES : tile * LANES] = jnp.where(dynamic, value, 0.0)


def radiation_kernel(
    role, weights, solar, received, from_first, from_second, depth, ssa, albedo,
    aero_two, aero_first, aero_second, out,
    profile, columns, aero, optics, scatter_q, decay, beam, glow, net, sems,
):
    step = pl.program_id(0)
    steps = pl.num_programs(0)
    is_first, is_second, is_third, is_last = (role[0] == k for k in range(4))
    kept = KEPT // UNIT_SENDERS
    active = (step < kept) | is_third | is_last

    def copies(unit, slot):
        lanes = pl.ds(pl.multiple_of(unit * UNIT, UNIT), UNIT)
        begin = jnp.where(unit < kept, KEPT * SLOT_COLS, 2 * KEPT * SLOT_COLS)
        own = pl.ds(pl.multiple_of(begin + unit * UNIT, UNIT), UNIT)
        target = aero.at[slot]
        return (
            (is_first, [pltpu.make_async_copy(aero_first.at[:, :, lanes], target, sems.at[slot, 0])]),
            (is_second, [pltpu.make_async_copy(aero_second.at[:, :, lanes], target, sems.at[slot, 0])]),
            (is_third, [pltpu.make_async_copy(aero_two.at[:, :, lanes], target, sems.at[slot, 0])]),
            (
                is_last,
                [
                    pltpu.make_async_copy(
                        depth.at[0, :, :, own], target.at[pl.ds(0, LEVELS)], sems.at[slot, 0]
                    ),
                    pltpu.make_async_copy(
                        ssa.at[0, :, :, own], target.at[pl.ds(LEVELS, LEVELS)], sems.at[slot, 1]
                    ),
                    pltpu.make_async_copy(
                        albedo.at[:, own], target.at[2 * LEVELS, pl.ds(0, 1)], sems.at[slot, 2]
                    ),
                ],
            ),
        )

    def has(unit):
        return (unit < kept) | is_third | is_last

    def begin(unit, slot):
        for chosen, descriptors in copies(unit, slot):
            @pl.when(chosen & has(unit))
            def _():
                for descriptor in descriptors:
                    descriptor.start()

    slot = step % 2

    @pl.when(step == 0)
    def _():
        begin(step, slot)

    @pl.when(step + 1 < steps)
    def _():
        begin(step + 1, 1 - slot)

    for chosen, ref in (
        (~is_last, received),
        (is_last & (step < kept), from_first),
        (is_last & (step >= kept), from_second),
    ):
        @pl.when(chosen)
        def _():
            profile[...] = ref[...]

    @pl.when(jnp.logical_not(active))
    def _():
        out[...] = jnp.zeros_like(out)

    @pl.when(active)
    def _():
        span = ROWS // PER_TILE
        for tile in range(UNIT // LANES):
            lanes = slice(tile * LANES, (tile + 1) * LANES)
            parts = [profile[tile * PER_TILE + e] for e in range(PER_TILE)]
            for a in range(PER_TILE):
                pieces = [part[0:span] for part in parts]
                columns[a * span : (a + 1) * span, lanes] = regroup(pieces, lambda e: e - a)
            pieces = [part[span : span + 8] for part in parts]
            columns[ROWS : ROWS + 8, lanes] = regroup(pieces, lambda e: e)
        for chosen, descriptors in copies(step, slot):
            @pl.when(chosen)
            def _():
                for descriptor in descriptors:
                    descriptor.wait()
        radiate(weights, solar, columns, aero, slot, optics, scatter_q, decay, beam, glow, net)
        heat = (net[0:LEVELS] - net[1 : LEVELS + 1]).sum(axis=1) * (LEVELS / GPOINTS)
        span = LEVELS // PER_TILE
        for tile in range(UNIT // LANES):
            part = heat[:, tile * LANES : (tile + 1) * LANES]
            for e in range(PER_TILE):
                pieces = [part[a * span : (a + 1) * span] for a in range(PER_TILE)]
                out[tile * PER_TILE + e] = regroup(pieces, lambda a: a - e)


def radiate(weights, solar, columns, aero, slot, optics, scatter_q, decay, beam, glow, net):
    cosine = columns[ROWS : ROWS + 1, :]
    path = jnp.maximum(cosine, 0.1)
    scale = LOG2E / path
    beam[...] = solar[:, 0:1] * (0.5 * jnp.maximum(cosine, 0.0))
    glow[...] = jnp.zeros_like(glow)
    node = iota((NODES, UNIT), 0).astype(F32)
    half = GPOINTS // 2

    def down(block, _):
        first = block * LEVEL_BLOCK
        for j in range(LEVEL_BLOCK):
            level = first + j
            warmth = (columns[pl.ds(level, 1), :] + 4.0) * ((NODES - 1) / 8.0)
            vapour = columns[pl.ds(level + LEVELS, 1), :] * scale
            cloud = columns[pl.ds(level + 2 * LEVELS, 1), :] * scale
            hat = jnp.maximum(0.0, 1.0 - jnp.abs(warmth - node)) * vapour
            depth = aero[slot, level] * scale
            share = depth * aero[slot, level + LEVELS]
            hat_hi, hat_lo = halves(hat)
            opt_hi, opt_lo = halves(jnp.concatenate([depth, scale, cloud], axis=0))
            sca_hi, sca_lo = halves(jnp.concatenate([share, jnp.zeros((2, UNIT), F32)], axis=0))
            stacked = jnp.concatenate(
                [hat_hi, hat_hi, hat_lo, opt_hi, opt_hi, opt_lo, sca_hi, sca_lo], axis=0
            )
            optics[j] = jnp.dot(weights[...], stacked, preferred_element_type=F32)
        for lane in range(0, UNIT, LANES):
            lanes = slice(lane, lane + LANES)
            back = jnp.broadcast_to(1.66 * path[:, lanes], (half, LANES))
            for row in range(0, GPOINTS, half):
                rows = slice(row, row + half)
                straight = beam[rows, lanes]
                spread = glow[rows, lanes]
                for j in range(LEVEL_BLOCK):
                    loss = optics[j, rows, lanes]
                    part = optics[j, GPOINTS + row : GPOINTS + row + half, lanes]
                    through = straight * jnp.exp2(loss)
                    kept = jnp.exp2(back * (loss + part))
                    source = (through - straight) * (part * pl.reciprocal(loss, approx=True))
                    scatter_q[first + j, rows, lanes] = source
                    decay[first + j, rows, lanes] = kept
                    total = (straight + straight + spread).reshape(half // 8, 8, LANES).sum(axis=0)
                    if row == 0:
                        net[first + j, :, lanes] = total
                    else:
                        net[first + j, :, lanes] += total
                    spread = spread * kept + source
                    straight = through
                beam[rows, lanes] = straight
                glow[rows, lanes] = spread
        return 0

    lax.fori_loop(0, LEVELS // LEVEL_BLOCK, down, 0)
    ground = aero[slot, 2 * LEVELS, 0:1, :]
    for lane in range(0, UNIT, LANES):
        lanes = slice(lane, lane + LANES)
        floor = 2.0 * beam[:, lanes] + glow[:, lanes]
        rising = ground[:, lanes] * floor
        net[LEVELS, :, lanes] = (floor - rising).reshape(GPOINTS // 8, 8, LANES).sum(axis=0)

        def up(i, rising):
            for k in range(4):
                level = LEVELS - 1 - (i * 4 + k)
                rising = rising * decay[level, :, lanes] + scatter_q[level, :, lanes]
                net[level, :, lanes] -= rising.reshape(GPOINTS // 8, 8, LANES).sum(axis=0)
            return rising

        lax.fori_loop(0, LEVELS // 4, up, rising)


def warm_kernel(role, mine, parent, slots_in, stepped, out):
    span = LEVELS // PER_TILE
    tiles = []
    for tile in range(DOMAINS // PER_TILE):
        parts = [mine[tile * PER_TILE + e] for e in range(PER_TILE)]
        tiles.append(
            jnp.concatenate([regroup(parts, lambda e: e - a) for a in range(PER_TILE)], axis=0)
        )
    heat = jnp.concatenate(tiles, axis=1)
    placed = ones_where(iota((DOMAINS * SLOT_COLS, COARSE), 0) == slots_in[...])
    coarse = exact_dot(heat, placed, 0)
    lineage = ones_where(iota((COARSE, CELLS), 0) == parent[...])
    fine = exact_dot(coarse, lineage, 0)
    out[...] = jnp.where(role[0] != SLOTS - 1, stepped[...] + 0.5 * fine, 0.0)


def params():
    return pltpu.CompilerParams(vmem_limit_bytes=VMEM_LIMIT)


SMEM = pl.BlockSpec(memory_space=pltpu.SMEM)
VMEM = pl.BlockSpec(memory_space=pltpu.VMEM)
HBM = pl.BlockSpec(memory_space=pl.ANY)


def per_device(
    state, kappa, neighbours, parent, cos_zenith, routes, rad_albedo, aerosol_depth, aerosol_ssa,
    gas_table, cloud_ext, cloud_ssa, rayleigh, solar_weight,
):
    fields = state.reshape(ROWS, CELLS)
    near = neighbours[0]
    slot = lax.axis_index("grp").astype(I32).reshape(1)
    last = SLOTS - 1

    def aerosol(begin, count):
        cut = slice(begin, begin + count)
        ground = jnp.broadcast_to(rad_albedo[0, cut], (1, BANDS, count))
        return jnp.concatenate(
            [aerosol_depth[0, :, :, cut], aerosol_ssa[0, :, :, cut], ground], axis=0
        )

    slot_span = DOMAINS * SLOT_COLS
    kept_cols = KEPT * SLOT_COLS
    aero_first = lax.ppermute(aerosol(0, kept_cols), "grp", [(last, 0)])
    aero_second = lax.ppermute(aerosol(slot_span, kept_cols), "grp", [(last, 1)])
    aero_two = lax.ppermute(aerosol(2 * slot_span, slot_span), "grp", [(last, 2)])

    message, edges, places, weights, solar = pl.pallas_call(
        coarsen_kernel,
        in_specs=[SMEM] + [VMEM] * 10,
        out_specs=[VMEM] * 5,
        out_shape=[
            jax.ShapeDtypeStruct((DOMAINS, 32, LANES), F32),
            jax.ShapeDtypeStruct((2, ROWS + 8, LANES), F32),
            jax.ShapeDtypeStruct((1, COARSE), I32),
            jax.ShapeDtypeStruct((2 * GPOINTS, 176), BF16),
            jax.ShapeDtypeStruct((GPOINTS, LANES), F32),
        ],
        compiler_params=params(),
        name="coarsen",
    )(
        routes, fields, parent, cos_zenith, kappa, near, gas_table, cloud_ext[None],
        cloud_ssa[None], rayleigh[None], solar_weight[None],
    )

    forward = [(i, (i + 1) % DOMAINS) for i in range(DOMAINS)]
    backward = [(target, source) for source, target in forward]
    left = lax.ppermute(edges[0], "dom", forward)
    right = lax.ppermute(edges[1], "dom", backward)
    received = lax.all_to_all(message, "dom", 0, 0, tiled=True)
    beyond = received[KEPT:]
    from_first = lax.ppermute(beyond, "grp", [(0, last)])
    from_second = lax.ppermute(beyond, "grp", [(1, last)])

    extended = CELLS + 2 * LANES
    stepped = pl.pallas_call(
        diffuse_kernel,
        in_specs=[SMEM] + [VMEM] * 5,
        out_specs=VMEM,
        out_shape=jax.ShapeDtypeStruct((ROWS, CELLS), F32),
        scratch_shapes=[
            pltpu.VMEM((ROWS, extended), F32),
            pltpu.VMEM((1, extended), F32),
            pltpu.VMEM((8, extended), I32),
            pltpu.VMEM((TILES + 2, 3 * LANES, LANES), BF16),
        ],
        compiler_params=params(),
        name="diffuse",
    )(slot, fields, kappa, near, left, right)

    units = DOMAINS // UNIT_SENDERS
    kept = KEPT // UNIT_SENDERS
    prof_block = (UNIT_SENDERS, 32, LANES)

    def own_block(i, role):
        return (jnp.where(role[0] == last, 0, jnp.where(role[0] < 2, jnp.minimum(i, kept - 1), i)), 0, 0)

    def first_block(i, role):
        return (jnp.where(role[0] == last, jnp.minimum(i, kept - 1), 0), 0, 0)

    def second_block(i, role):
        return (jnp.where(role[0] == last, jnp.maximum(i - kept, 0), 0), 0, 0)

    heat = pl.pallas_call(
        radiation_kernel,
        grid_spec=pltpu.PrefetchScalarGridSpec(
            num_scalar_prefetch=1,
            grid=(units,),
            in_specs=[
                pl.BlockSpec((2 * GPOINTS, 176), lambda i, role: (0, 0)),
                pl.BlockSpec((GPOINTS, LANES), lambda i, role: (0, 0)),
                pl.BlockSpec(prof_block, own_block),
                pl.BlockSpec(prof_block, first_block),
                pl.BlockSpec(prof_block, second_block),
                HBM, HBM, HBM, HBM, HBM, HBM,
            ],
            out_specs=pl.BlockSpec((UNIT_SENDERS, 8, LANES), lambda i, role: (i, 0, 0)),
            scratch_shapes=[
                pltpu.VMEM(prof_block, F32),
                pltpu.VMEM((ROWS + 8, UNIT), F32),
                pltpu.VMEM((2, 2 * LEVELS + 1, BANDS, UNIT), F32),
                pltpu.VMEM((LEVEL_BLOCK, 2 * GPOINTS, UNIT), F32),
                pltpu.VMEM((LEVELS, GPOINTS, UNIT), F32),
                pltpu.VMEM((LEVELS, GPOINTS, UNIT), F32),
                pltpu.VMEM((GPOINTS, UNIT), F32),
                pltpu.VMEM((GPOINTS, UNIT), F32),
                pltpu.VMEM((LEVELS + 1, 8, UNIT), F32),
                pltpu.SemaphoreType.DMA((2, 3)),
            ],
        ),
        out_shape=jax.ShapeDtypeStruct((DOMAINS, 8, LANES), F32),
        compiler_params=params(),
        name="radiation",
    )(
        slot, weights, solar, received, from_first, from_second, aerosol_depth, aerosol_ssa,
        rad_albedo, aero_two, aero_first, aero_second,
    )

    to_first = lax.ppermute(heat[:KEPT], "grp", [(last, 0)])
    to_second = lax.ppermute(heat[KEPT:], "grp", [(last, 1)])
    returning = jnp.concatenate([heat[:KEPT], heat[KEPT:] + (to_first + to_second)], axis=0)
    mine = lax.all_to_all(returning, "dom", 0, 0, tiled=True)

    warmed = pl.pallas_call(
        warm_kernel,
        grid=(1,),
        in_specs=[
            SMEM,
            pl.BlockSpec((DOMAINS, 8, LANES), lambda i: (0, 0, 0)),
            pl.BlockSpec((1, CELLS), lambda i: (0, 0)),
            pl.BlockSpec((1, COARSE), lambda i: (0, 0)),
            pl.BlockSpec((LEVELS, CELLS), lambda i: (0, 0)),
        ],
        out_specs=pl.BlockSpec((LEVELS, CELLS), lambda i: (0, 0)),
        out_shape=jax.ShapeDtypeStruct((ROWS, CELLS), F32),
        input_output_aliases={4: 0},
        compiler_params=params(),
        name="warm",
    )(slot, mine, parent, places, stepped)
    return warmed.reshape(1, FIELDS, LEVELS, CELLS)


def solution(mesh):
    return jax.shard_map(
        per_device,
        mesh=mesh,
        in_specs=(
            P("grp", None, None, "dom"),
            P("grp", "dom"),
            P("grp", None, "dom"),
            P("grp", "dom"),
            P("grp", "dom"),
            P(("grp", "dom"), None, None),
            P("grp", "dom"),
            P("grp", None, None, "dom"),
            P("grp", None, None, "dom"),
            P(),
            P(),
            P(),
            P(),
            P(),
        ),
        out_specs=P("grp", None, None, "dom"),
        check_vma=False,
    )
```

```python
import jax
import jax.numpy as jnp
from jax import lax
from jax.experimental import pallas as pl
from jax.experimental.pallas import tpu as pltpu
from jax.sharding import PartitionSpec as P

F32 = jnp.float32
BF16 = jnp.bfloat16
I32 = jnp.int32
HALO = 32
FIELDS, LEVELS, GPOINTS, BANDS, NODES = 3, 32, 112, 14, 32
ROWS = FIELDS * LEVELS
CELLS, COARSE = 2048, 512
BLOCKS, BLOCK_COLS, MOST = 32, 16, 2
DOMAINS, SLOTS = 32, 4
SLOT_COLS = BLOCK_COLS * MOST
LANES = 128
PER_TILE = LANES // SLOT_COLS
TILES = CELLS // LANES
UNIT = 256
UNIT_SENDERS = UNIT // SLOT_COLS
STAY = 16
MOVED = DOMAINS - STAY
LEVEL_BLOCK = 8
LOG2E = 1.4426950408889634
VMEM_LIMIT = 28 * 1024 * 1024


def halves(x):
    high = x.astype(BF16)
    return high, (x - high.astype(F32)).astype(BF16)


def thirds(x):
    high = x.astype(BF16)
    rest = x - high.astype(F32)
    middle = rest.astype(BF16)
    return high, middle, (rest - middle.astype(F32)).astype(BF16)


def exact_dot(x, chosen, contract):
    rows = x.shape[0]
    stacked = jnp.concatenate(thirds(x), axis=0)
    product = lax.dot_general(
        stacked, chosen, (((1,), (contract,)), ((), ())), preferred_element_type=F32
    )
    return product[:rows] + product[rows : 2 * rows] + product[2 * rows :]


def iota(shape, dim):
    return lax.broadcasted_iota(I32, shape, dim)


def ones_where(mask):
    return jnp.where(mask, 1.0, 0.0).astype(BF16)


def regroup(pieces, shift_of):
    group = iota(pieces[0].shape, 1) // SLOT_COLS
    result = None
    for k, piece in enumerate(pieces):
        shift = (shift_of(k) % PER_TILE) * SLOT_COLS
        moved = pltpu.roll(piece, shift, 1) if shift else piece
        result = moved if result is None else jnp.where(group == k, moved, result)
    return result


def column(row):
    n = row.shape[1]
    return jnp.sum(jnp.where(iota((n, n), 0) == iota((n, n), 1), row, 0.0), axis=1, keepdims=True)


def aerosol_copies(depth, ssa, albedo, target, begin, count, sems):
    lanes = pl.ds(begin, count)
    height = BANDS * LEVELS
    return [
        pltpu.make_async_copy(depth.at[:, lanes], target.at[pl.ds(0, height)], sems.at[0]),
        pltpu.make_async_copy(ssa.at[:, lanes], target.at[pl.ds(height, height)], sems.at[1]),
        pltpu.make_async_copy(albedo.at[:, lanes], target.at[pl.ds(2 * height, 1)], sems.at[2]),
    ]


def edge_kernel(role, low_state, low_kappa, low_near, high_state, high_kappa, high_near, low, high):
    @pl.when(role[0] != SLOTS - 1)
    def _():
        for state, kappa, near, edge in (
            (low_state, low_kappa, low_near, low), (high_state, high_kappa, high_near, high)
        ):
            edge[0:ROWS, :] = state[...]
            others = [near[n].astype(F32) for n in range(3)]
            edge[ROWS : ROWS + 8, :] = jnp.concatenate(
                [kappa[...]] + others + [jnp.zeros((4, LANES), F32)], axis=0
            )


def stage_kernel(
    role, gas, ext, ssa, ray, solar, aero_depth, aero_ssa, albedo,
    weights, solar_out, aero_two, staged, sems,
):
    is_last = role[0] == SLOTS - 1
    tail = (DOMAINS + MOVED) * SLOT_COLS
    total = (SLOTS - 1) * DOMAINS * SLOT_COLS
    copies = aerosol_copies(aero_depth, aero_ssa, albedo, staged, total - tail, tail, sems)
    onward = pltpu.make_async_copy(staged, aero_two, sems.at[3])

    @pl.when(is_last)
    def _():
        for copy in copies:
            copy.start()

    @pl.when(role[0] >= SLOTS - 2)
    def _():
        radiation_weights(gas, ext, ssa, ray, solar, weights, solar_out)

    @pl.when(is_last)
    def _():
        for copy in copies:
            copy.wait()
        onward.start()
        onward.wait()


def coarsen_kernel(role, routes, state, parent, sun, _, message, slots_out):
    @pl.when(role[0] != SLOTS - 1)
    def _():
        pack_columns(routes, state, parent, sun, message, slots_out)


def pack_columns(routes, state, parent, sun, message, slots_out):
    block = iota((1, COARSE), 1) // BLOCK_COLS
    target = jnp.zeros((1, COARSE), I32)
    for b in range(BLOCKS):
        target = jnp.where(block == b, routes[0, 0, b], target)
    arrival = jnp.zeros((1, COARSE), I32)
    for b in range(BLOCKS):
        same = (target == routes[0, 0, b]) & (block > b)
        arrival = arrival + jnp.where(same, 1, 0)
    place = (target * MOST + arrival) * BLOCK_COLS + iota((1, COARSE), 1) % BLOCK_COLS
    slots_out[...] = place

    lineage = ones_where(iota((COARSE, CELLS), 0) == parent[...])
    coarse = 0.25 * exact_dot(state[...], lineage, 1)
    sun_rows = jnp.where(iota((8, COARSE), 0) == 0, sun[...], 0.0)
    columns = jnp.concatenate([coarse, sun_rows], axis=0)
    placed = ones_where(iota((DOMAINS * SLOT_COLS, COARSE), 0) == place)
    packed = exact_dot(columns, placed, 1)
    span = ROWS // PER_TILE
    for tile in range(DOMAINS // PER_TILE):
        part = packed[:, tile * LANES : (tile + 1) * LANES]
        for e in range(PER_TILE):
            pieces = [part[a * span : (a + 1) * span] for a in range(PER_TILE)]
            message[tile * PER_TILE + e, 0:span, :] = regroup(pieces, lambda a: a - e)
            moved = pltpu.roll(part[ROWS:], ((-e) % PER_TILE) * SLOT_COLS, 1) if e else part[ROWS:]
            message[tile * PER_TILE + e, span : span + 8, :] = moved


def radiation_weights(gas, ext, ssa, ray, solar, weights, solar_out):
    band = jnp.where(iota((GPOINTS, 16), 0) // 8 == iota((GPOINTS, 16), 1), 1.0, 0.0)
    spot = iota((GPOINTS, 16), 1)
    ext_col, ssa_col, ray_col = column(ext[...]), column(ssa[...]), column(ray[...])
    scatter_w = jnp.where(spot == BANDS, ray_col, jnp.where(spot == BANDS + 1, ssa_col * ext_col, 0.0))
    optical_w = jnp.where(spot == BANDS, ray_col, jnp.where(spot == BANDS + 1, ext_col, band))
    gas_hi, gas_lo = halves(gas[...].T)
    opt_hi, opt_lo = halves(optical_w)
    sca_hi, sca_lo = halves(scatter_w)
    none = jnp.zeros((GPOINTS, 16), F32)
    wide = jnp.zeros((GPOINTS, NODES), F32)
    upper = [gas_hi, gas_lo, gas_hi, opt_hi, opt_lo, opt_hi, none, none]
    lower = [wide, wide, wide, sca_hi, sca_lo, sca_hi, band, band]
    weights[0:GPOINTS, :] = (-jnp.concatenate([p.astype(F32) for p in upper], axis=1)).astype(BF16)
    weights[GPOINTS:, :] = jnp.concatenate([p.astype(F32) for p in lower], axis=1).astype(BF16)
    solar_out[...] = jnp.broadcast_to(column(solar[...]), (GPOINTS, LANES))


def diffuse_kernel(role, state, kappa, near, left, right, _, out, fields, rates, goal, chosen):
    @pl.when(role[0] == SLOTS - 1)
    def _():
        out[...] = jnp.zeros_like(out)

    @pl.when(role[0] != SLOTS - 1)
    def _():
        for ref, start, width, shift in (
            (left, 0, LANES, LANES - HALO - CELLS),
            (right, LANES + CELLS, LANES, LANES - HALO + CELLS),
        ):
            fields[:, start : start + width] = ref[0:ROWS, :]
            rates[:, start : start + width] = ref[ROWS : ROWS + 1, :]
            goal[0:3, start : start + width] = ref[ROWS + 1 : ROWS + 4, :].astype(I32) + shift
        fields[:, LANES : LANES + CELLS] = state[...]
        rates[:, LANES : LANES + CELLS] = kappa[...]
        for n in range(3):
            goal[n : n + 1, LANES : LANES + CELLS] = near[n] + (LANES - HALO)
        window = 3 * LANES
        rows = iota((window, LANES), 0)

        def spread(tile):
            first = min(max(tile - 1, 0), TILES - 1)
            return first * LANES

        results = []
        for tile in range(TILES + 2):
            here = slice(tile * LANES, (tile + 1) * LANES)
            place = rows + spread(tile)
            count = jnp.zeros((window, LANES), F32)
            for n in range(3):
                count = count + jnp.where(place == goal[n : n + 1, here], 1.0, 0.0)
            picked = count.astype(BF16)
            chosen[tile] = picked
            own = fields[:, here]
            total = exact_dot(fields[:, spread(tile) : spread(tile) + window], picked, 0)
            results.append(own + rates[:, here] * (total - 3.0 * own))
        for tile, value in enumerate(results):
            fields[:, tile * LANES : (tile + 1) * LANES] = value
        for tile in range(1, TILES + 1):
            here = slice(tile * LANES, (tile + 1) * LANES)
            own = fields[:, here]
            total = exact_dot(fields[:, spread(tile) : spread(tile) + window], chosen[tile], 0)
            value = own + rates[:, here] * (total - 3.0 * own)
            out[:, (tile - 1) * LANES : tile * LANES] = value


def radiation_kernel(
    role, weights, solar, received, from_first, from_second, from_moved, _left, _right, depth, ssa, albedo,
    aero_two, early, late,
    profile, columns, aero, optics, scatter_q, decay, beam, glow, net, sems,
):
    step = pl.program_id(0)
    steps = pl.num_programs(0)
    is_third, is_last = role[0] == SLOTS - 2, role[0] == SLOTS - 1
    ahead = DOMAINS // UNIT_SENDERS
    active = is_third | is_last

    def copies(unit, slot):
        two = jnp.where(unit < ahead, unit + MOVED // UNIT_SENDERS, unit - ahead) * UNIT
        third, fourth = [], []
        for tile in range(UNIT // LANES):
            lanes = pl.ds(pl.multiple_of(two + tile * LANES, LANES), LANES)
            third.append(
                pltpu.make_async_copy(
                    aero_two.at[:, lanes],
                    aero.at[slot, tile, pl.ds(0, 2 * BANDS * LEVELS + 8)],
                    sems.at[slot, tile, 0],
                )
            )
            fourth += aerosol_copies(
                depth, ssa, albedo, aero.at[slot, tile],
                pl.multiple_of(unit * UNIT + tile * LANES, LANES), LANES, sems.at[slot, tile],
            )
        return (is_third, third), (is_last, fourth)

    def begin(unit, slot):
        for chosen, descriptors in copies(unit, slot):
            @pl.when(chosen)
            def _():
                for descriptor in descriptors:
                    descriptor.start()

    slot = step % 2

    @pl.when(step == 0)
    def _():
        begin(step, slot)

    @pl.when(step + 1 < steps)
    def _():
        begin(step + 1, 1 - slot)

    for chosen, ref, first in (
        (is_third & (step < ahead), received, 0),
        (is_last & (step < ahead), from_first, 0),
        (is_last & (step >= ahead), from_second, ahead),
        (is_third & (step >= ahead), from_moved, ahead),
    ):
        @pl.when(chosen)
        def _():
            profile[...] = ref[pl.ds((step - first) * UNIT_SENDERS, UNIT_SENDERS)]

    @pl.when(active)
    def _():
        span = ROWS // PER_TILE
        for tile in range(UNIT // LANES):
            lanes = slice(tile * LANES, (tile + 1) * LANES)
            parts = [profile[tile * PER_TILE + e] for e in range(PER_TILE)]
            for a in range(PER_TILE):
                pieces = [part[0:span] for part in parts]
                columns[a * span : (a + 1) * span, lanes] = regroup(pieces, lambda e: e - a)
            pieces = [part[span : span + 8] for part in parts]
            columns[ROWS : ROWS + 8, lanes] = regroup(pieces, lambda e: e)
        for chosen, descriptors in copies(step, slot):
            @pl.when(chosen)
            def _():
                for descriptor in descriptors:
                    descriptor.wait()
        radiate(weights, solar, columns, aero, slot, optics, scatter_q, decay, beam, glow, net)
        heat = (net[0:LEVELS] - net[1 : LEVELS + 1]).sum(axis=1) * (LEVELS / GPOINTS)
        span = LEVELS // PER_TILE
        messages = []
        for tile in range(UNIT // LANES):
            part = heat[:, tile * LANES : (tile + 1) * LANES]
            pieces = [part[a * span : (a + 1) * span] for a in range(PER_TILE)]
            messages += [regroup(pieces, lambda a: a - e) for e in range(PER_TILE)]

        @pl.when(step < ahead)
        def _():
            for e, message in enumerate(messages):
                early[e] = message

        @pl.when(step >= ahead)
        def _():
            for e, message in enumerate(messages):
                late[e] = message


def radiate(weights, solar, columns, aero, slot, optics, scatter_q, decay, beam, glow, net):
    cosine = columns[ROWS : ROWS + 1, :]
    path = jnp.maximum(cosine, 0.1)
    scale = LOG2E / path
    beam[...] = solar[:, 0:1] * (0.5 * jnp.maximum(cosine, 0.0))
    glow[...] = jnp.zeros_like(glow)
    node = iota((NODES, UNIT), 0).astype(F32)
    spot = iota((16, UNIT), 0)
    half = GPOINTS // 2

    def bands_of(first):
        tiles = range(UNIT // LANES)
        rows = pl.ds(first, 16, stride=LEVELS)
        return jnp.concatenate([aero[slot, tile, rows, :] for tile in tiles], axis=1)

    def down(block, _):
        first = block * LEVEL_BLOCK
        for j in range(LEVEL_BLOCK):
            level = first + j
            warmth = (columns[pl.ds(level, 1), :] + 4.0) * ((NODES - 1) / 8.0)
            vapour = columns[pl.ds(level + LEVELS, 1), :] * scale
            cloud = columns[pl.ds(level + 2 * LEVELS, 1), :] * scale
            hat = jnp.maximum(0.0, 1.0 - jnp.abs(warmth - node)) * vapour
            depth = bands_of(level) * scale
            share = depth * bands_of(level + BANDS * LEVELS)
            hat_hi, hat_lo = halves(hat)
            opt_hi, opt_lo = halves(
                jnp.where(spot < BANDS, depth, jnp.where(spot == BANDS, scale, cloud))
            )
            sca_hi, sca_lo = halves(jnp.where(spot < BANDS, share, 0.0))
            stacked = jnp.concatenate(
                [hat_hi, hat_hi, hat_lo, opt_hi, opt_hi, opt_lo, sca_hi, sca_lo], axis=0
            )
            optics[j] = jnp.dot(weights[...], stacked, preferred_element_type=F32)
        for lane in range(0, UNIT, LANES):
            lanes = slice(lane, lane + LANES)
            back = jnp.broadcast_to(1.66 * path[:, lanes], (half, LANES))
            for row in range(0, GPOINTS, half):
                rows = slice(row, row + half)
                straight = beam[rows, lanes]
                spread = glow[rows, lanes]
                for j in range(LEVEL_BLOCK):
                    loss = optics[j, rows, lanes]
                    part = optics[j, GPOINTS + row : GPOINTS + row + half, lanes]
                    through = straight * jnp.exp2(loss)
                    kept = jnp.exp2(back * (loss + part))
                    source = (through - straight) * (part * pl.reciprocal(loss, approx=True))
                    scatter_q[first + j, rows, lanes] = source
                    decay[first + j, rows, lanes] = kept
                    total = (straight + straight + spread).reshape(half // 8, 8, LANES).sum(axis=0)
                    if row == 0:
                        net[first + j, :, lanes] = total
                    else:
                        net[first + j, :, lanes] += total
                    spread = spread * kept + source
                    straight = through
                beam[rows, lanes] = straight
                glow[rows, lanes] = spread
        return 0

    lax.fori_loop(0, LEVELS // LEVEL_BLOCK, down, 0)
    for lane in range(0, UNIT, LANES):
        lanes = slice(lane, lane + LANES)
        floor = 2.0 * beam[:, lanes] + glow[:, lanes]
        ground = 2 * BANDS * LEVELS
        rising = aero[slot, lane // LANES, ground : ground + 1, :] * floor
        net[LEVELS, :, lanes] = (floor - rising).reshape(GPOINTS // 8, 8, LANES).sum(axis=0)

        def up(i, rising):
            for k in range(4):
                level = LEVELS - 1 - (i * 4 + k)
                rising = rising * decay[level, :, lanes] + scatter_q[level, :, lanes]
                net[level, :, lanes] -= rising.reshape(GPOINTS // 8, 8, LANES).sum(axis=0)
            return rising

        lax.fori_loop(0, LEVELS // 4, up, rising)


def rad_scratch():
    return [
        pltpu.VMEM((ROWS + 8, UNIT), F32),
        pltpu.VMEM((2, UNIT // LANES, (2 * BANDS + 2) * LEVELS, LANES), F32),
        pltpu.VMEM((LEVEL_BLOCK, 2 * GPOINTS, UNIT), F32),
        pltpu.VMEM((LEVELS, GPOINTS, UNIT), F32),
        pltpu.VMEM((LEVELS, GPOINTS, UNIT), F32),
        pltpu.VMEM((GPOINTS, UNIT), F32),
        pltpu.VMEM((GPOINTS, UNIT), F32),
        pltpu.VMEM((LEVELS + 1, 8, UNIT), F32),
    ]


def warm_kernel(role, mine, parent, slots_in, stepped, out):
    span = LEVELS // PER_TILE
    tiles = []
    for tile in range(DOMAINS // PER_TILE):
        parts = [mine[tile * PER_TILE + e] for e in range(PER_TILE)]
        tiles.append(
            jnp.concatenate([regroup(parts, lambda e: e - a) for a in range(PER_TILE)], axis=0)
        )
    heat = jnp.concatenate(tiles, axis=1)
    placed = ones_where(iota((DOMAINS * SLOT_COLS, COARSE), 0) == slots_in[...])
    coarse = exact_dot(heat, placed, 0)
    lineage = ones_where(iota((COARSE, CELLS), 0) == parent[...])
    fine = exact_dot(coarse, lineage, 0)
    out[...] = jnp.where(role[0] != SLOTS - 1, stepped[...] + 0.5 * fine, 0.0)


def near_core(x):
    return pltpu.with_memory_space_constraint(x, pltpu.VMEM)


def far(x):
    return pltpu.with_memory_space_constraint(x, pltpu.HBM)


def params():
    return pltpu.CompilerParams(vmem_limit_bytes=VMEM_LIMIT)


SMEM = pl.BlockSpec(memory_space=pltpu.SMEM)
VMEM = pl.BlockSpec(memory_space=pltpu.VMEM)
HBM = pl.BlockSpec(memory_space=pl.ANY)


def per_device(
    state, kappa, neighbours, parent, cos_zenith, routes, rad_albedo, aerosol_depth, aerosol_ssa,
    gas_table, cloud_ext, cloud_ssa, rayleigh, solar_weight,
):
    fields = state.reshape(ROWS, CELLS)
    near = jnp.transpose(neighbours, (1, 0, 2))
    slot = lax.axis_index("grp").astype(I32).reshape(1)
    last = SLOTS - 1
    depth = jnp.transpose(aerosol_depth[0], (1, 0, 2)).reshape(BANDS * LEVELS, -1)
    ssa = jnp.transpose(aerosol_ssa[0], (1, 0, 2)).reshape(BANDS * LEVELS, -1)
    aero_rows = 2 * BANDS * LEVELS + 8

    def edges(tile):
        return [
            pl.BlockSpec((ROWS, LANES), lambda i: (0, tile)),
            pl.BlockSpec((1, LANES), lambda i: (0, tile)),
            pl.BlockSpec((3, 1, LANES), lambda i: (0, 0, tile)),
        ]

    edge_low, edge_high = pl.pallas_call(
        edge_kernel,
        grid=(1,),
        in_specs=[SMEM] + edges(0) + edges(TILES - 1),
        out_specs=[pl.BlockSpec((ROWS + 8, LANES), lambda i: (0, 0))] * 2,
        out_shape=[jax.ShapeDtypeStruct((ROWS + 8, LANES), F32)] * 2,
        compiler_params=params(),
        name="edge",
    )(slot, far(fields), far(kappa), far(near), far(fields), far(kappa), far(near))
    forward = [
        (s * DOMAINS + i, s * DOMAINS + (i + 1) % DOMAINS) for s in range(last) for i in range(DOMAINS)
    ]
    backward = [(target, source) for source, target in forward]
    left = lax.ppermute(edge_high, ("grp", "dom"), forward)
    right = lax.ppermute(edge_low, ("grp", "dom"), backward)

    weights, solar, aero_two = pl.pallas_call(
        stage_kernel,
        in_specs=[SMEM] + [VMEM] * 5 + [HBM] * 3,
        out_specs=[VMEM] * 2 + [HBM],
        out_shape=[
            jax.ShapeDtypeStruct((2 * GPOINTS, 176), BF16),
            jax.ShapeDtypeStruct((GPOINTS, LANES), F32),
            jax.ShapeDtypeStruct((aero_rows, (DOMAINS + MOVED) * SLOT_COLS), F32),
        ],
        scratch_shapes=[
            pltpu.VMEM((aero_rows, (DOMAINS + MOVED) * SLOT_COLS), F32),
            pltpu.SemaphoreType.DMA((4,)),
        ],
        compiler_params=params(),
        name="stage",
    )(
        slot, far(gas_table.T), far(cloud_ext[None]), far(cloud_ssa[None]), far(rayleigh[None]),
        far(solar_weight[None]), far(depth), far(ssa), far(rad_albedo),
    )
    aero_two = lax.ppermute(aero_two, "grp", [(last, last - 1)])

    message, places = pl.pallas_call(
        coarsen_kernel,
        in_specs=[SMEM, SMEM] + [VMEM] * 3 + [HBM],
        out_specs=[VMEM] * 2,
        out_shape=[
            jax.ShapeDtypeStruct((DOMAINS, 32, LANES), F32),
            jax.ShapeDtypeStruct((1, COARSE), I32),
        ],
        compiler_params=params(),
        name="coarsen",
    )(slot, far(jnp.transpose(routes, (0, 2, 1))), far(fields), far(parent), far(cos_zenith), weights)
    received = lax.all_to_all(message, "dom", 0, 0, tiled=True)
    from_first = lax.ppermute(received, "grp", [(0, last)])
    from_second = lax.ppermute(received[:STAY], "grp", [(1, last)])
    from_moved = lax.ppermute(received[STAY:], "grp", [(1, 2)])

    ahead = DOMAINS // UNIT_SENDERS
    units = ahead + STAY // UNIT_SENDERS

    early, late = pl.pallas_call(
        radiation_kernel,
        grid_spec=pltpu.PrefetchScalarGridSpec(
            num_scalar_prefetch=1,
            grid=(units,),
            in_specs=[
                pl.BlockSpec((2 * GPOINTS, 176), lambda i, role: (0, 0)),
                pl.BlockSpec((GPOINTS, LANES), lambda i, role: (0, 0)),
                VMEM, VMEM, VMEM, VMEM, VMEM, VMEM, HBM, HBM, HBM, VMEM,
            ],
            out_specs=[
                pl.BlockSpec(
                    (UNIT_SENDERS, 8, LANES), lambda i, role: (jnp.minimum(i, ahead - 1), 0, 0)
                ),
                pl.BlockSpec(
                    (UNIT_SENDERS, 8, LANES), lambda i, role: (jnp.maximum(i - ahead, 0), 0, 0)
                ),
            ],
            scratch_shapes=[
                pltpu.VMEM((UNIT_SENDERS, 32, LANES), F32),
                *rad_scratch(),
                pltpu.SemaphoreType.DMA((2, UNIT // LANES, 3)),
            ],
        ),
        out_shape=[
            jax.ShapeDtypeStruct((ahead * UNIT_SENDERS, 8, LANES), F32),
            jax.ShapeDtypeStruct(((units - ahead) * UNIT_SENDERS, 8, LANES), F32),
        ],
        compiler_params=params(),
        name="radiation",
    )(
        slot, weights, solar, near_core(received), near_core(from_first), near_core(from_second),
        near_core(from_moved), near_core(left), near_core(right), far(depth), far(ssa), far(rad_albedo),
        near_core(aero_two),
    )

    extended = CELLS + 2 * LANES
    stepped = pl.pallas_call(
        diffuse_kernel,
        in_specs=[SMEM] + [VMEM] * 5 + [HBM],
        out_specs=VMEM,
        out_shape=jax.ShapeDtypeStruct((ROWS, CELLS), F32),
        scratch_shapes=[
            pltpu.VMEM((ROWS, extended), F32),
            pltpu.VMEM((1, extended), F32),
            pltpu.VMEM((8, extended), I32),
            pltpu.VMEM((TILES + 2, 3 * LANES, LANES), BF16),
        ],
        compiler_params=params(),
        name="diffuse",
    )(slot, far(fields), far(kappa), far(near), near_core(left), near_core(right), early)

    to_first = lax.ppermute(early, "grp", [(last, 0)])
    to_second = lax.ppermute(late, "grp", [(last, 1)])
    moved_back = lax.ppermute(late, "grp", [(2, 1)])
    away = to_first + jnp.concatenate([to_second, moved_back], axis=0)
    returning = jnp.where(slot[0] == last - 1, early, away)
    mine = lax.all_to_all(returning, "dom", 0, 0, tiled=True)

    warmed = pl.pallas_call(
        warm_kernel,
        grid=(1,),
        in_specs=[
            SMEM,
            VMEM,
            pl.BlockSpec((1, CELLS), lambda i: (0, 0)),
            pl.BlockSpec((1, COARSE), lambda i: (0, 0)),
            pl.BlockSpec((LEVELS, CELLS), lambda i: (0, 0)),
        ],
        out_specs=pl.BlockSpec((LEVELS, CELLS), lambda i: (0, 0)),
        out_shape=jax.ShapeDtypeStruct((ROWS, CELLS), F32),
        input_output_aliases={4: 0},
        compiler_params=params(),
        name="warm",
    )(slot, near_core(mine), far(parent), places, stepped)
    return warmed.reshape(1, FIELDS, LEVELS, CELLS)


def solution(mesh):
    return jax.shard_map(
        per_device,
        mesh=mesh,
        in_specs=(
            P("grp", None, None, "dom"),
            P("grp", "dom"),
            P("grp", None, "dom"),
            P("grp", "dom"),
            P("grp", "dom"),
            P(("grp", "dom"), None, None),
            P("grp", "dom"),
            P("grp", None, None, "dom"),
            P("grp", None, None, "dom"),
            P(),
            P(),
            P(),
            P(),
            P(),
        ),
        out_specs=P("grp", None, None, "dom"),
        check_vma=False,
    )
```

```python
import jax
import jax.numpy as jnp
from jax import lax
from jax.experimental import pallas as pl
from jax.experimental.pallas import tpu as pltpu
from jax.sharding import PartitionSpec as P

F32 = jnp.float32
BF16 = jnp.bfloat16
I32 = jnp.int32
HALO = 32
FIELDS, LEVELS, GPOINTS, BANDS, NODES = 3, 32, 112, 14, 32
ROWS = FIELDS * LEVELS
CELLS, COARSE = 2048, 512
LANES = 128
BLOCKS, BLOCK_COLS, MOST = 32, 16, 2
DOMAINS, SLOTS = 32, 4
SLOT_COLS = BLOCK_COLS * MOST
SPAN = ROWS // (LANES // SLOT_COLS)
LINES = SPAN + 1
PER_TILE = LANES // SLOT_COLS
TILES = CELLS // LANES
UNIT = 256
UNIT_SENDERS = UNIT // SLOT_COLS
STAY = 24
MOVED = DOMAINS - STAY
LEVEL_BLOCK = 8
AERO = 2 * BANDS + 2
PITCH = LEVELS + 8
LOG2E = 1.4426950408889634
VMEM_LIMIT = 28 * 1024 * 1024


def halves(x):
    high = x.astype(BF16)
    return high, (x - high.astype(F32)).astype(BF16)


def thirds(x):
    high = x.astype(BF16)
    rest = x - high.astype(F32)
    middle = rest.astype(BF16)
    return high, middle, (rest - middle.astype(F32)).astype(BF16)


def exact_dot(x, chosen, contract):
    rows = x.shape[0]
    stacked = jnp.concatenate(thirds(x), axis=0)
    product = lax.dot_general(
        stacked, chosen, (((1,), (contract,)), ((), ())), preferred_element_type=F32
    )
    return product[:rows] + product[rows : 2 * rows] + product[2 * rows :]


def iota(shape, dim):
    return lax.broadcasted_iota(I32, shape, dim)


def ones_where(mask):
    return jnp.where(mask, 1.0, 0.0).astype(BF16)


def regroup(pieces, shift_of):
    group = iota(pieces[0].shape, 1) // SLOT_COLS
    result = None
    for k, piece in enumerate(pieces):
        shift = (shift_of(k) % PER_TILE) * SLOT_COLS
        moved = pltpu.roll(piece, shift, 1) if shift else piece
        result = moved if result is None else jnp.where(group == k, moved, result)
    return result


def column(row):
    n = row.shape[1]
    return jnp.sum(jnp.where(iota((n, n), 0) == iota((n, n), 1), row, 0.0), axis=1, keepdims=True)


def aerosol_copies(depth, ssa, albedo, target, begin, count, sems):
    lanes = pl.ds(begin, count)
    levels = pl.ds(0, LEVELS)
    return [
        pltpu.make_async_copy(
            depth.at[:, :, lanes], target.at[pl.ds(0, BANDS), levels], sems.at[0]
        ),
        pltpu.make_async_copy(
            ssa.at[:, :, lanes], target.at[pl.ds(BANDS, BANDS), levels], sems.at[1]
        ),
        pltpu.make_async_copy(
            albedo.at[:, lanes], target.at[2 * BANDS, pl.ds(0, 1)], sems.at[2]
        ),
    ]


def first_kernel(
    role, routes, state, parent, sun, kappa, near, gas, ext, ssa, ray, solar,
    aero_depth, aero_ssa, albedo,
    message, slots_out, edge_low, edge_high, weights, solar_out, aero_two, sems,
):
    is_last = role[0] == SLOTS - 1

    @pl.when(jnp.logical_not(is_last))
    def _():
        for edge, start in ((edge_high, CELLS - LANES), (edge_low, 0)):
            here = slice(start, start + LANES)
            edge[0:ROWS, :] = state[:, here]
            others = [near[n, :, here].astype(F32) for n in range(3)]
            edge[ROWS : ROWS + 8, :] = jnp.concatenate(
                [kappa[:, here]] + others + [jnp.zeros((4, LANES), F32)], axis=0
            )
        pack_columns(routes, state, parent, sun, message, slots_out)

    @pl.when(role[0] == SLOTS - 2)
    def _():
        radiation_weights(gas, ext, ssa, ray, solar, weights, solar_out)

    @pl.when(is_last)
    def _():
        tail = (DOMAINS + MOVED) * SLOT_COLS
        total = (SLOTS - 1) * DOMAINS * SLOT_COLS
        copies = aerosol_copies(aero_depth, aero_ssa, albedo, aero_two, total - tail, tail, sems)
        for copy in copies:
            copy.start()
        radiation_weights(gas, ext, ssa, ray, solar, weights, solar_out)
        for copy in copies:
            copy.wait()


def pack_columns(routes, state, parent, sun, message, slots_out):
    block = iota((1, COARSE), 1) // BLOCK_COLS
    target = jnp.zeros((1, COARSE), I32)
    for b in range(BLOCKS):
        target = jnp.where(block == b, routes[0, 0, b], target)
    arrival = jnp.zeros((1, COARSE), I32)
    for b in range(BLOCKS):
        same = (target == routes[0, 0, b]) & (block > b)
        arrival = arrival + jnp.where(same, 1, 0)
    place = (target * MOST + arrival) * BLOCK_COLS + iota((1, COARSE), 1) % BLOCK_COLS
    slots_out[...] = place

    lineage = ones_where(iota((COARSE, CELLS), 0) == parent[...])
    coarse = 0.25 * exact_dot(state[...], lineage, 1)
    sun_rows = jnp.where(iota((8, COARSE), 0) == 0, sun[...], 0.0)
    columns = jnp.concatenate([coarse, sun_rows], axis=0)
    placed = ones_where(iota((DOMAINS * SLOT_COLS, COARSE), 0) == place)
    packed = exact_dot(columns, placed, 1)
    for tile in range(DOMAINS // PER_TILE):
        part = packed[:, tile * LANES : (tile + 1) * LANES]
        for e in range(PER_TILE):
            first = (tile * PER_TILE + e) * LINES
            pieces = [part[a * SPAN : (a + 1) * SPAN] for a in range(PER_TILE)]
            message[first : first + SPAN, :] = regroup(pieces, lambda a: a - e)
            moved = pltpu.roll(part[ROWS:], ((-e) % PER_TILE) * SLOT_COLS, 1) if e else part[ROWS:]
            message[first + SPAN : first + LINES, :] = moved[0:1]


def radiation_weights(gas, ext, ssa, ray, solar, weights, solar_out):
    band = jnp.where(iota((GPOINTS, 16), 0) // 8 == iota((GPOINTS, 16), 1), 1.0, 0.0)
    spot = iota((GPOINTS, 16), 1)
    ext_col, ssa_col, ray_col = column(ext[...]), column(ssa[...]), column(ray[...])
    scatter_w = jnp.where(spot == BANDS, ray_col, jnp.where(spot == BANDS + 1, ssa_col * ext_col, 0.0))
    optical_w = jnp.where(spot == BANDS, ray_col, jnp.where(spot == BANDS + 1, ext_col, band))
    gas_hi, gas_lo = halves(gas[...].T)
    opt_hi, opt_lo = halves(optical_w)
    sca_hi, sca_lo = halves(scatter_w)
    none = jnp.zeros((GPOINTS, 16), F32)
    wide = jnp.zeros((GPOINTS, NODES), F32)
    upper = [gas_hi, gas_lo, gas_hi, opt_hi, opt_lo, opt_hi, none, none]
    lower = [wide, wide, wide, sca_hi, sca_lo, sca_hi, band, band]
    weights[0:GPOINTS, :] = (-jnp.concatenate([p.astype(F32) for p in upper], axis=1)).astype(BF16)
    weights[GPOINTS:, :] = jnp.concatenate([p.astype(F32) for p in lower], axis=1).astype(BF16)
    solar_out[...] = jnp.broadcast_to(column(solar[...]), (GPOINTS, LANES))


def diffuse_kernel(
    role, state, kappa, near, left, right, _, out, fields, rates, goal, chosen,
):
    @pl.when(role[0] == SLOTS - 1)
    def _():
        out[...] = jnp.zeros_like(out)

    @pl.when(role[0] != SLOTS - 1)
    def _():
        for ref, start, width, shift in (
            (left, 0, LANES, LANES - HALO - CELLS),
            (right, LANES + CELLS, LANES, LANES - HALO + CELLS),
        ):
            fields[:, start : start + width] = ref[0:ROWS, :]
            rates[:, start : start + width] = ref[ROWS : ROWS + 1, :]
            goal[0:3, start : start + width] = ref[ROWS + 1 : ROWS + 4, :].astype(I32) + shift
        fields[:, LANES : LANES + CELLS] = state[...]
        rates[:, LANES : LANES + CELLS] = kappa[...]
        for n in range(3):
            goal[n : n + 1, LANES : LANES + CELLS] = near[n] + (LANES - HALO)
        window = 3 * LANES
        rows = iota((window, LANES), 0)

        def spread(tile):
            first = min(max(tile - 1, 0), TILES - 1)
            return first * LANES

        results = []
        for tile in range(TILES + 2):
            here = slice(tile * LANES, (tile + 1) * LANES)
            place = rows + spread(tile)
            count = jnp.zeros((window, LANES), F32)
            for n in range(3):
                count = count + jnp.where(place == goal[n : n + 1, here], 1.0, 0.0)
            picked = count.astype(BF16)
            chosen[tile] = picked
            own = fields[:, here]
            total = exact_dot(fields[:, spread(tile) : spread(tile) + window], picked, 0)
            results.append(own + rates[:, here] * (total - 3.0 * own))
        for tile, value in enumerate(results):
            fields[:, tile * LANES : (tile + 1) * LANES] = value
        for tile in range(1, TILES + 1):
            here = slice(tile * LANES, (tile + 1) * LANES)
            own = fields[:, here]
            total = exact_dot(fields[:, spread(tile) : spread(tile) + window], chosen[tile], 0)
            value = own + rates[:, here] * (total - 3.0 * own)
            out[:, (tile - 1) * LANES : tile * LANES] = value


def radiation_kernel(
    role, weights, solar, received, from_first, from_second, from_moved, _left, _right, depth, ssa, albedo,
    aero_two, early, late,
    profile, columns, aero, optics, scatter_q, decay, beam, glow, net, sems,
):
    step = pl.program_id(0)
    steps = pl.num_programs(0)
    is_third, is_last = role[0] == SLOTS - 2, role[0] == SLOTS - 1
    ahead = DOMAINS // UNIT_SENDERS
    active = is_last | (is_third & (step < ahead + MOVED // UNIT_SENDERS))

    def copies(unit, slot):
        two = jnp.where(unit < ahead, unit + MOVED // UNIT_SENDERS, unit - ahead) * UNIT
        third, fourth = [], []
        for tile in range(UNIT // LANES):
            lanes = pl.ds(pl.multiple_of(two + tile * LANES, LANES), LANES)
            third.append(
                pltpu.make_async_copy(
                    aero_two.at[:, :, lanes],
                    aero.at[slot, tile, pl.ds(0, 2 * BANDS + 1), pl.ds(0, LEVELS)],
                    sems.at[slot, tile, 0],
                )
            )
            fourth += aerosol_copies(
                depth, ssa, albedo, aero.at[slot, tile],
                pl.multiple_of(unit * UNIT + tile * LANES, LANES), LANES, sems.at[slot, tile],
            )
        return (is_third, third), (is_last, fourth)

    def begin(unit, slot):
        for chosen, descriptors in copies(unit, slot):
            @pl.when(chosen & (is_last | (unit < ahead + MOVED // UNIT_SENDERS)))
            def _():
                for descriptor in descriptors:
                    descriptor.start()

    slot = step % 2

    @pl.when(step == 0)
    def _():
        begin(step, slot)

    @pl.when(step + 1 < steps)
    def _():
        begin(step + 1, 1 - slot)

    for chosen, ref, first in (
        (is_third & (step < ahead), received, 0),
        (is_last & (step < ahead), from_first, 0),
        (is_last & (step >= ahead), from_second, ahead),
        (active & is_third & (step >= ahead), from_moved, ahead),
    ):
        @pl.when(chosen)
        def _():
            height = UNIT_SENDERS * LINES
            profile[...] = ref[pl.ds(pl.multiple_of((step - first) * height, 8), height), :]

    @pl.when(active)
    def _():
        for tile in range(UNIT // LANES):
            lanes = slice(tile * LANES, (tile + 1) * LANES)
            starts = [(tile * PER_TILE + e) * LINES for e in range(PER_TILE)]
            parts = [profile[start : start + SPAN, :] for start in starts]
            for a in range(PER_TILE):
                columns[a * SPAN : (a + 1) * SPAN, lanes] = regroup(parts, lambda e: e - a)
            suns = [profile[start + SPAN : start + LINES, :] for start in starts]
            columns[ROWS : ROWS + 1, lanes] = regroup(suns, lambda e: e)
        for chosen, descriptors in copies(step, slot):
            @pl.when(chosen)
            def _():
                for descriptor in descriptors:
                    descriptor.wait()
        radiate(weights, solar, columns, aero, slot, optics, scatter_q, decay, beam, glow, net)
        heat = (net[0:LEVELS] - net[1 : LEVELS + 1]).sum(axis=1) * (LEVELS / GPOINTS)
        span = LEVELS // PER_TILE
        messages = []
        for tile in range(UNIT // LANES):
            part = heat[:, tile * LANES : (tile + 1) * LANES]
            pieces = [part[a * span : (a + 1) * span] for a in range(PER_TILE)]
            messages += [regroup(pieces, lambda a: a - e) for e in range(PER_TILE)]

        @pl.when(step < ahead)
        def _():
            for e, message in enumerate(messages):
                early[e] = message

        @pl.when(step >= ahead)
        def _():
            for e, message in enumerate(messages):
                late[e] = message


def over_groups(x):
    return x.reshape(x.shape[0] // 8, 8, LANES).sum(axis=0)


def radiate(weights, solar, columns, aero, slot, optics, scatter_q, decay, beam, glow, net):
    cosine = columns[ROWS : ROWS + 1, :]
    path = jnp.maximum(cosine, 0.1)
    scale = LOG2E / path
    beam[...] = solar[:, 0:1] * (0.5 * jnp.maximum(cosine, 0.0))
    glow[...] = jnp.zeros_like(glow)
    node = iota((NODES, UNIT), 0).astype(F32)
    spot = iota((16, UNIT), 0)
    half = GPOINTS // 2

    def bands_of(band, level):
        rows = pl.ds(band * PITCH + level, 16, stride=PITCH)
        tiles = [aero.at[slot, tile].reshape(AERO * PITCH, LANES) for tile in range(UNIT // LANES)]
        return jnp.concatenate([tile[rows, :] for tile in tiles], axis=1)

    def down(block, _):
        first = block * LEVEL_BLOCK
        for j in range(LEVEL_BLOCK):
            level = first + j
            warmth = (columns[pl.ds(level, 1), :] + 4.0) * ((NODES - 1) / 8.0)
            vapour = columns[pl.ds(level + LEVELS, 1), :] * scale
            cloud = columns[pl.ds(level + 2 * LEVELS, 1), :] * scale
            hat = jnp.maximum(0.0, 1.0 - jnp.abs(warmth - node)) * vapour
            depth = bands_of(0, level) * scale
            share = depth * bands_of(BANDS, level)
            hat_hi, hat_lo = halves(hat)
            opt_hi, opt_lo = halves(
                jnp.where(spot < BANDS, depth, jnp.where(spot == BANDS, scale, cloud))
            )
            sca_hi, sca_lo = halves(jnp.where(spot < BANDS, share, 0.0))
            stacked = jnp.concatenate(
                [hat_hi, hat_hi, hat_lo, opt_hi, opt_hi, opt_lo, sca_hi, sca_lo], axis=0
            )
            optics[j] = jnp.dot(weights[...], stacked, preferred_element_type=F32)
        for lane in range(0, UNIT, LANES):
            lanes = slice(lane, lane + LANES)
            back = jnp.broadcast_to(1.66 * path[:, lanes], (half, LANES))
            for row in range(0, GPOINTS, half):
                rows = slice(row, row + half)
                straight = beam[rows, lanes]
                spread = glow[rows, lanes]
                for j in range(LEVEL_BLOCK):
                    total = 2.0 * over_groups(straight) + over_groups(spread)
                    if row == 0:
                        net[first + j, :, lanes] = total
                    else:
                        net[first + j, :, lanes] += total
                    loss = optics[j, rows, lanes]
                    part = optics[j, GPOINTS + row : GPOINTS + row + half, lanes]
                    through = straight * jnp.exp2(loss)
                    kept = jnp.exp2(back * (loss + part))
                    source = (through - straight) * (part * pl.reciprocal(loss, approx=True))
                    scatter_q[first + j, rows, lanes] = source
                    decay[first + j, rows, lanes] = kept
                    spread = spread * kept + source
                    straight = through
                beam[rows, lanes] = straight
                glow[rows, lanes] = spread
        return 0

    lax.fori_loop(0, LEVELS // LEVEL_BLOCK, down, 0)
    for lane in range(0, UNIT, LANES):
        lanes = slice(lane, lane + LANES)
        floor = 2.0 * beam[:, lanes] + glow[:, lanes]
        rising = aero[slot, lane // LANES, 2 * BANDS, 0:1, :] * floor
        net[LEVELS, :, lanes] = over_groups(floor - rising)

        def up(i, rising):
            for k in range(8):
                level = LEVELS - 1 - (i * 8 + k)
                rising = rising * decay[level, :, lanes] + scatter_q[level, :, lanes]
                net[level, :, lanes] -= over_groups(rising)
            return rising

        lax.fori_loop(0, LEVELS // 8, up, rising)


def rad_scratch():
    return [
        pltpu.VMEM((ROWS + 8, UNIT), F32),
        pltpu.VMEM((2, UNIT // LANES, AERO, PITCH, LANES), F32),
        pltpu.VMEM((LEVEL_BLOCK, 2 * GPOINTS, UNIT), F32),
        pltpu.VMEM((LEVELS, GPOINTS, UNIT), F32),
        pltpu.VMEM((LEVELS, GPOINTS, UNIT), F32),
        pltpu.VMEM((GPOINTS, UNIT), F32),
        pltpu.VMEM((GPOINTS, UNIT), F32),
        pltpu.VMEM((LEVELS + 1, 8, UNIT), F32),
    ]


def warm_kernel(role, mine, parent, slots_in, stepped, out):
    span = LEVELS // PER_TILE
    tiles = []
    for tile in range(DOMAINS // PER_TILE):
        parts = [mine[tile * PER_TILE + e] for e in range(PER_TILE)]
        tiles.append(
            jnp.concatenate([regroup(parts, lambda e: e - a) for a in range(PER_TILE)], axis=0)
        )
    heat = jnp.concatenate(tiles, axis=1)
    placed = ones_where(iota((DOMAINS * SLOT_COLS, COARSE), 0) == slots_in[...])
    coarse = exact_dot(heat, placed, 0)
    lineage = ones_where(iota((COARSE, CELLS), 0) == parent[...])
    fine = exact_dot(coarse, lineage, 0)
    out[...] = jnp.where(role[0] != SLOTS - 1, stepped[...] + 0.5 * fine, 0.0)


def near_core(x):
    return pltpu.with_memory_space_constraint(x, pltpu.VMEM)


def far(x):
    return pltpu.with_memory_space_constraint(x, pltpu.HBM)


def params():
    return pltpu.CompilerParams(vmem_limit_bytes=VMEM_LIMIT)


SMEM = pl.BlockSpec(memory_space=pltpu.SMEM)
VMEM = pl.BlockSpec(memory_space=pltpu.VMEM)
HBM = pl.BlockSpec(memory_space=pl.ANY)


def per_device(
    state, kappa, neighbours, parent, cos_zenith, routes, rad_albedo, aerosol_depth, aerosol_ssa,
    gas_table, cloud_ext, cloud_ssa, rayleigh, solar_weight,
):
    fields = state.reshape(ROWS, CELLS)
    near = jnp.transpose(neighbours, (1, 0, 2))
    slot = lax.axis_index("grp").astype(I32).reshape(1)
    last = SLOTS - 1
    depth = jnp.transpose(aerosol_depth[0], (1, 0, 2))
    ssa = jnp.transpose(aerosol_ssa[0], (1, 0, 2))

    message, places, edge_low, edge_high, weights, solar, aero_two = pl.pallas_call(
        first_kernel,
        in_specs=[SMEM, SMEM] + [VMEM] * 10 + [HBM] * 3,
        out_specs=[VMEM] * 7,
        out_shape=[
            jax.ShapeDtypeStruct((DOMAINS * LINES, LANES), F32),
            jax.ShapeDtypeStruct((1, COARSE), I32),
            jax.ShapeDtypeStruct((ROWS + 8, LANES), F32),
            jax.ShapeDtypeStruct((ROWS + 8, LANES), F32),
            jax.ShapeDtypeStruct((2 * GPOINTS, 176), BF16),
            jax.ShapeDtypeStruct((GPOINTS, LANES), F32),
            pltpu.VMEM((2 * BANDS + 1, LEVELS, (DOMAINS + MOVED) * SLOT_COLS), F32),
        ],
        scratch_shapes=[pltpu.SemaphoreType.DMA((3,))],
        compiler_params=params(),
        name="first",
    )(
        slot, far(jnp.transpose(routes, (0, 2, 1))), far(fields), far(parent), far(cos_zenith),
        far(kappa), far(near), far(gas_table.T), far(cloud_ext[None]), far(cloud_ssa[None]),
        far(rayleigh[None]), far(solar_weight[None]), far(depth), far(ssa), far(rad_albedo),
    )
    aero_two = lax.ppermute(aero_two, "grp", [(last, last - 1)])

    forward = [
        (s * DOMAINS + i, s * DOMAINS + (i + 1) % DOMAINS) for s in range(last) for i in range(DOMAINS)
    ]
    backward = [(target, source) for source, target in forward]
    left = lax.ppermute(edge_high, ("grp", "dom"), forward)
    right = lax.ppermute(edge_low, ("grp", "dom"), backward)

    received = lax.all_to_all(
        message.reshape(DOMAINS, 1, LINES * LANES), "dom", 0, 0, tiled=True
    ).reshape(DOMAINS * LINES, LANES)
    from_first = lax.ppermute(received, "grp", [(0, last)])
    from_second = lax.ppermute(received[: STAY * LINES], "grp", [(1, last)])
    from_moved = lax.ppermute(received[STAY * LINES :], "grp", [(1, 2)])

    ahead = DOMAINS // UNIT_SENDERS
    units = ahead + STAY // UNIT_SENDERS

    early, late = pl.pallas_call(
        radiation_kernel,
        grid_spec=pltpu.PrefetchScalarGridSpec(
            num_scalar_prefetch=1,
            grid=(units,),
            in_specs=[
                pl.BlockSpec((2 * GPOINTS, 176), lambda i, role: (0, 0)),
                pl.BlockSpec((GPOINTS, LANES), lambda i, role: (0, 0)),
                VMEM, VMEM, VMEM, VMEM, VMEM, VMEM, HBM, HBM, HBM, VMEM,
            ],
            out_specs=[
                pl.BlockSpec(
                    (UNIT_SENDERS, 8, LANES), lambda i, role: (jnp.minimum(i, ahead - 1), 0, 0)
                ),
                pl.BlockSpec(
                    (UNIT_SENDERS, 8, LANES), lambda i, role: (jnp.maximum(i - ahead, 0), 0, 0)
                ),
            ],
            scratch_shapes=[
                pltpu.VMEM((UNIT_SENDERS * LINES, LANES), F32),
                *rad_scratch(),
                pltpu.SemaphoreType.DMA((2, UNIT // LANES, 3)),
            ],
        ),
        out_shape=[
            jax.ShapeDtypeStruct((ahead * UNIT_SENDERS, 8, LANES), F32),
            jax.ShapeDtypeStruct(((units - ahead) * UNIT_SENDERS, 8, LANES), F32),
        ],
        compiler_params=params(),
        name="radiation",
    )(
        slot, weights, solar, near_core(received), near_core(from_first), near_core(from_second),
        near_core(from_moved), near_core(left), near_core(right), far(depth), far(ssa), far(rad_albedo),
        near_core(aero_two),
    )

    extended = CELLS + 2 * LANES
    stepped = pl.pallas_call(
        diffuse_kernel,
        in_specs=[SMEM] + [VMEM] * 5 + [HBM],
        out_specs=VMEM,
        out_shape=jax.ShapeDtypeStruct((ROWS, CELLS), F32),
        scratch_shapes=[
            pltpu.VMEM((ROWS, extended), F32),
            pltpu.VMEM((1, extended), F32),
            pltpu.VMEM((8, extended), I32),
            pltpu.VMEM((TILES + 2, 3 * LANES, LANES), BF16),
        ],
        compiler_params=params(),
        name="diffuse",
    )(slot, far(fields), far(kappa), far(near), near_core(left), near_core(right), early)

    to_first = lax.ppermute(early, "grp", [(last, 0)])
    to_second = lax.ppermute(late, "grp", [(last, 1)])
    moved_back = lax.ppermute(late, "grp", [(2, 1)])
    away = to_first + jnp.concatenate([to_second, moved_back[:MOVED]], axis=0)
    returning = jnp.where(slot[0] == last - 1, early, away)
    mine = lax.all_to_all(returning, "dom", 0, 0, tiled=True)

    warmed = pl.pallas_call(
        warm_kernel,
        grid=(1,),
        in_specs=[
            SMEM,
            VMEM,
            pl.BlockSpec((1, CELLS), lambda i: (0, 0)),
            pl.BlockSpec((1, COARSE), lambda i: (0, 0)),
            pl.BlockSpec((LEVELS, CELLS), lambda i: (0, 0)),
        ],
        out_specs=pl.BlockSpec((LEVELS, CELLS), lambda i: (0, 0)),
        out_shape=jax.ShapeDtypeStruct((ROWS, CELLS), F32),
        input_output_aliases={4: 0},
        compiler_params=params(),
        name="warm",
    )(slot, near_core(mine), far(parent), places, stepped)
    return warmed.reshape(1, FIELDS, LEVELS, CELLS)


def solution(mesh):
    return jax.shard_map(
        per_device,
        mesh=mesh,
        in_specs=(
            P("grp", None, None, "dom"),
            P("grp", "dom"),
            P("grp", None, "dom"),
            P("grp", "dom"),
            P("grp", "dom"),
            P(("grp", "dom"), None, None),
            P("grp", "dom"),
            P("grp", None, None, "dom"),
            P("grp", None, None, "dom"),
            P(),
            P(),
            P(),
            P(),
            P(),
        ),
        out_specs=P("grp", None, None, "dom"),
        check_vma=False,
    )
```

```python
import jax
import jax.numpy as jnp
from jax import lax
from jax.experimental import pallas as pl
from jax.experimental.pallas import tpu as pltpu
from jax.sharding import PartitionSpec as P

F32 = jnp.float32
BF16 = jnp.bfloat16
I32 = jnp.int32
HALO = 32
FIELDS, LEVELS, GPOINTS, BANDS, NODES = 3, 32, 112, 14, 32
ROWS = FIELDS * LEVELS
CELLS, COARSE = 2048, 512
LANES = 128
BLOCKS, BLOCK_COLS, MOST = 32, 16, 2
DOMAINS, SLOTS = 32, 4
SLOT_COLS = BLOCK_COLS * MOST
SPAN = ROWS // (LANES // SLOT_COLS)
LINES = SPAN + 1
PER_TILE = LANES // SLOT_COLS
TILES = CELLS // LANES
UNIT = 256
UNIT_SENDERS = UNIT // SLOT_COLS
STAY = 16
MOVED = DOMAINS - STAY
SOON = max(STAY, MOVED) // UNIT_SENDERS
LATER = DOMAINS // UNIT_SENDERS
LEVEL_BLOCK = 8
AERO = 2 * BANDS + 2
PITCH = LEVELS + 8
LOG2E = 1.4426950408889634
VMEM_LIMIT = 28 * 1024 * 1024


def halves(x):
    high = x.astype(BF16)
    return high, (x - high.astype(F32)).astype(BF16)


def thirds(x):
    high = x.astype(BF16)
    rest = x - high.astype(F32)
    middle = rest.astype(BF16)
    return high, middle, (rest - middle.astype(F32)).astype(BF16)


def exact_dot(x, chosen, contract):
    rows = x.shape[0]
    stacked = jnp.concatenate(thirds(x), axis=0)
    product = lax.dot_general(
        stacked, chosen, (((1,), (contract,)), ((), ())), preferred_element_type=F32
    )
    return product[:rows] + product[rows : 2 * rows] + product[2 * rows :]


def iota(shape, dim):
    return lax.broadcasted_iota(I32, shape, dim)


def ones_where(mask):
    return jnp.where(mask, 1.0, 0.0).astype(BF16)


def regroup(pieces, shift_of):
    group = iota(pieces[0].shape, 1) // SLOT_COLS
    result = None
    for k, piece in enumerate(pieces):
        shift = (shift_of(k) % PER_TILE) * SLOT_COLS
        moved = pltpu.roll(piece, shift, 1) if shift else piece
        result = moved if result is None else jnp.where(group == k, moved, result)
    return result


def column(row):
    n = row.shape[1]
    return jnp.sum(jnp.where(iota((n, n), 0) == iota((n, n), 1), row, 0.0), axis=1, keepdims=True)


def aerosol_copies(depth, ssa, albedo, target, begin, count, sems):
    lanes = pl.ds(begin, count)
    levels = pl.ds(0, LEVELS)
    return [
        pltpu.make_async_copy(
            depth.at[:, :, lanes], target.at[pl.ds(0, BANDS), levels], sems.at[0]
        ),
        pltpu.make_async_copy(
            ssa.at[:, :, lanes], target.at[pl.ds(BANDS, BANDS), levels], sems.at[1]
        ),
        pltpu.make_async_copy(
            albedo.at[:, lanes], target.at[2 * BANDS, pl.ds(0, 1)], sems.at[2]
        ),
    ]


def first_kernel(
    role, routes, state, parent, sun, kappa, near, gas, ext, ssa, ray, solar,
    aero_depth, aero_ssa, albedo,
    message, slots_out, edge_pair, edge_next, weights, solar_out, aero_two, sems,
):
    is_last = role[0] == SLOTS - 1

    @pl.when(jnp.logical_not(is_last))
    def _():
        for parity, above, below in ((0, edge_pair, edge_next), (1, edge_next, edge_pair)):
            @pl.when(role[1] == parity)
            def _():
                for edge, start in ((above, CELLS - LANES), (below, 0)):
                    here = slice(start, start + LANES)
                    edge[0:ROWS, :] = state[:, here]
                    others = [near[n, :, here].astype(F32) for n in range(3)]
                    edge[ROWS : ROWS + 8, :] = jnp.concatenate(
                        [kappa[:, here]] + others + [jnp.zeros((4, LANES), F32)], axis=0
                    )

        pack_columns(routes, state, parent, sun, message, slots_out)

    @pl.when(role[0] == SLOTS - 2)
    def _():
        radiation_weights(gas, ext, ssa, ray, solar, weights, solar_out)

    @pl.when(is_last)
    def _():
        start, count = DOMAINS * SLOT_COLS, (DOMAINS + STAY) * SLOT_COLS
        copies = aerosol_copies(aero_depth, aero_ssa, albedo, aero_two, start, count, sems)
        for copy in copies:
            copy.start()
        radiation_weights(gas, ext, ssa, ray, solar, weights, solar_out)
        for copy in copies:
            copy.wait()


def pack_columns(routes, state, parent, sun, message, slots_out):
    block = iota((1, COARSE), 1) // BLOCK_COLS
    target = jnp.zeros((1, COARSE), I32)
    for b in range(BLOCKS):
        target = jnp.where(block == b, routes[0, 0, b], target)
    arrival = jnp.zeros((1, COARSE), I32)
    for b in range(BLOCKS):
        same = (target == routes[0, 0, b]) & (block > b)
        arrival = arrival + jnp.where(same, 1, 0)
    place = (target * MOST + arrival) * BLOCK_COLS + iota((1, COARSE), 1) % BLOCK_COLS
    slots_out[...] = place

    lineage = ones_where(iota((COARSE, CELLS), 0) == parent[...])
    coarse = 0.25 * exact_dot(state[...], lineage, 1)
    sun_rows = jnp.where(iota((8, COARSE), 0) == 0, sun[...], 0.0)
    columns = jnp.concatenate([coarse, sun_rows], axis=0)
    placed = ones_where(iota((DOMAINS * SLOT_COLS, COARSE), 0) == place)
    packed = exact_dot(columns, placed, 1)
    for tile in range(DOMAINS // PER_TILE):
        part = packed[:, tile * LANES : (tile + 1) * LANES]
        for e in range(PER_TILE):
            first = (tile * PER_TILE + e) * LINES
            pieces = [part[a * SPAN : (a + 1) * SPAN] for a in range(PER_TILE)]
            message[first : first + SPAN, :] = regroup(pieces, lambda a: a - e)
            moved = pltpu.roll(part[ROWS:], ((-e) % PER_TILE) * SLOT_COLS, 1) if e else part[ROWS:]
            message[first + SPAN : first + LINES, :] = moved[0:1]


def radiation_weights(gas, ext, ssa, ray, solar, weights, solar_out):
    band = jnp.where(iota((GPOINTS, 16), 0) // 8 == iota((GPOINTS, 16), 1), 1.0, 0.0)
    spot = iota((GPOINTS, 16), 1)
    ext_col, ssa_col, ray_col = column(ext[...]), column(ssa[...]), column(ray[...])
    scatter_w = jnp.where(spot == BANDS, ray_col, jnp.where(spot == BANDS + 1, ssa_col * ext_col, 0.0))
    optical_w = jnp.where(spot == BANDS, ray_col, jnp.where(spot == BANDS + 1, ext_col, band))
    gas_hi, gas_lo = halves(gas[...].T)
    opt_hi, opt_lo = halves(optical_w)
    sca_hi, sca_lo = halves(scatter_w)
    none = jnp.zeros((GPOINTS, 16), F32)
    wide = jnp.zeros((GPOINTS, NODES), F32)
    upper = [gas_hi, gas_lo, gas_hi, opt_hi, opt_lo, opt_hi, none, none]
    lower = [wide, wide, wide, sca_hi, sca_lo, sca_hi, band, band]
    weights[0:GPOINTS, :] = (-jnp.concatenate([p.astype(F32) for p in upper], axis=1)).astype(BF16)
    weights[GPOINTS:, :] = jnp.concatenate([p.astype(F32) for p in lower], axis=1).astype(BF16)
    solar_out[...] = jnp.broadcast_to(column(solar[...]), (GPOINTS, LANES))


def diffuse_kernel(
    role, state, kappa, near, of_pair, of_next, _, out, fields, rates, goal, chosen,
):
    @pl.when(role[0] == SLOTS - 1)
    def _():
        out[...] = jnp.zeros_like(out)

    @pl.when(role[0] != SLOTS - 1)
    def _():
        even = role[1] == 0
        for edge, start, shift in (
            (jnp.where(even, of_next[...], of_pair[...]), 0, LANES - HALO - CELLS),
            (jnp.where(even, of_pair[...], of_next[...]), LANES + CELLS, LANES - HALO + CELLS),
        ):
            here = slice(start, start + LANES)
            fields[:, here] = edge[0:ROWS]
            rates[:, here] = edge[ROWS : ROWS + 1]
            goal[0:3, here] = edge[ROWS + 1 : ROWS + 4].astype(I32) + shift
        fields[:, LANES : LANES + CELLS] = state[...]
        rates[:, LANES : LANES + CELLS] = kappa[...]
        for n in range(3):
            goal[n : n + 1, LANES : LANES + CELLS] = near[n] + (LANES - HALO)
        window = 3 * LANES
        rows = iota((window, LANES), 0)

        def spread(tile):
            first = min(max(tile - 1, 0), TILES - 1)
            return first * LANES

        results = []
        for tile in range(TILES + 2):
            here = slice(tile * LANES, (tile + 1) * LANES)
            place = rows + spread(tile)
            count = jnp.zeros((window, LANES), F32)
            for n in range(3):
                count = count + jnp.where(place == goal[n : n + 1, here], 1.0, 0.0)
            picked = count.astype(BF16)
            chosen[tile] = picked
            own = fields[:, here]
            total = exact_dot(fields[:, spread(tile) : spread(tile) + window], picked, 0)
            results.append(own + rates[:, here] * (total - 3.0 * own))
        for tile, value in enumerate(results):
            fields[:, tile * LANES : (tile + 1) * LANES] = value
        for tile in range(1, TILES + 1):
            here = slice(tile * LANES, (tile + 1) * LANES)
            own = fields[:, here]
            total = exact_dot(fields[:, spread(tile) : spread(tile) + window], chosen[tile], 0)
            value = own + rates[:, here] * (total - 3.0 * own)
            out[:, (tile - 1) * LANES : tile * LANES] = value


def soon_kernel(
    role, weights, solar, received, from_third, depth, ssa, albedo, aero_two, out, *scratch
):
    is_third, is_last = role[0] == SLOTS - 2, role[0] == SLOTS - 1
    radiate_unit(
        (is_third, received, STAY // UNIT_SENDERS, DOMAINS // UNIT_SENDERS),
        (is_last, from_third, MOVED // UNIT_SENDERS, (2 * DOMAINS + STAY) // UNIT_SENDERS),
        weights, solar, depth, ssa, albedo, aero_two, out, *scratch,
    )


def later_kernel(
    role, weights, solar, arrived, _pair, _next, _soon, depth, ssa, albedo, aero_two, out, *scratch
):
    is_third, is_last = role[0] == SLOTS - 2, role[0] == SLOTS - 1
    radiate_unit(
        (is_third, arrived, LATER, 0), (is_last, arrived, LATER, 0),
        weights, solar, depth, ssa, albedo, aero_two, out, *scratch,
    )


def radiate_unit(
    third, last, weights, solar, depth, ssa, albedo, aero_two, out,
    profile, columns, aero, optics, scatter_q, decay, beam, glow, net, sems,
):
    step = pl.program_id(0)
    steps = pl.num_programs(0)
    is_third, third_profiles, third_units, third_first = third
    is_last, last_profiles, last_units, last_first = last

    def taken(unit):
        return (is_third & (unit < third_units)) | (is_last & (unit < last_units))

    active = taken(step)

    def copies(unit, slot):
        here, there = [], []
        for tile in range(UNIT // LANES):
            offset = tile * LANES
            lanes = pl.ds(pl.multiple_of((third_first + unit) * UNIT + offset, LANES), LANES)
            here.append(
                pltpu.make_async_copy(
                    aero_two.at[:, :, lanes],
                    aero.at[slot, tile, pl.ds(0, 2 * BANDS + 1), pl.ds(0, LEVELS)],
                    sems.at[slot, tile, 0],
                )
            )
            there += aerosol_copies(
                depth, ssa, albedo, aero.at[slot, tile],
                pl.multiple_of((last_first + unit) * UNIT + offset, LANES), LANES, sems.at[slot, tile],
            )
        return (is_third, here), (is_last, there)

    def begin(unit, slot):
        for chosen, descriptors in copies(unit, slot):
            @pl.when(chosen & taken(unit))
            def _():
                for descriptor in descriptors:
                    descriptor.start()

    slot = step % 2

    @pl.when(step == 0)
    def _():
        begin(step, slot)

    @pl.when(step + 1 < steps)
    def _():
        begin(step + 1, 1 - slot)

    for chosen, ref in ((is_third, third_profiles), (is_last, last_profiles)):
        @pl.when(chosen & active)
        def _():
            height = UNIT_SENDERS * LINES
            profile[...] = ref[pl.ds(pl.multiple_of(step * height, 8), height), :]

    @pl.when(active)
    def _():
        for tile in range(UNIT // LANES):
            lanes = slice(tile * LANES, (tile + 1) * LANES)
            starts = [(tile * PER_TILE + e) * LINES for e in range(PER_TILE)]
            parts = [profile[start : start + SPAN, :] for start in starts]
            for a in range(PER_TILE):
                columns[a * SPAN : (a + 1) * SPAN, lanes] = regroup(parts, lambda e: e - a)
            suns = [profile[start + SPAN : start + LINES, :] for start in starts]
            columns[ROWS : ROWS + 1, lanes] = regroup(suns, lambda e: e)
        for chosen, descriptors in copies(step, slot):
            @pl.when(chosen)
            def _():
                for descriptor in descriptors:
                    descriptor.wait()
        radiate(weights, solar, columns, aero, slot, optics, scatter_q, decay, beam, glow, net)
        heat = (net[0:LEVELS] - net[1 : LEVELS + 1]).sum(axis=1) * (LEVELS / GPOINTS)
        span = LEVELS // PER_TILE
        messages = []
        for tile in range(UNIT // LANES):
            part = heat[:, tile * LANES : (tile + 1) * LANES]
            pieces = [part[a * span : (a + 1) * span] for a in range(PER_TILE)]
            messages += [regroup(pieces, lambda a: a - e) for e in range(PER_TILE)]

        for e, message in enumerate(messages):
            out[e] = message


def over_groups(x):
    return x.reshape(x.shape[0] // 8, 8, LANES).sum(axis=0)


def radiate(weights, solar, columns, aero, slot, optics, scatter_q, decay, beam, glow, net):
    cosine = columns[ROWS : ROWS + 1, :]
    path = jnp.maximum(cosine, 0.1)
    scale = LOG2E / path
    beam[...] = solar[:, 0:1] * (0.5 * jnp.maximum(cosine, 0.0))
    glow[...] = jnp.zeros_like(glow)
    node = iota((NODES, UNIT), 0).astype(F32)
    spot = iota((16, UNIT), 0)
    half = GPOINTS // 2

    def bands_of(band, level):
        rows = pl.ds(band * PITCH + level, 16, stride=PITCH)
        tiles = [aero.at[slot, tile].reshape(AERO * PITCH, LANES) for tile in range(UNIT // LANES)]
        return jnp.concatenate([tile[rows, :] for tile in tiles], axis=1)

    def down(block, _):
        first = block * LEVEL_BLOCK
        for j in range(LEVEL_BLOCK):
            level = first + j
            warmth = (columns[pl.ds(level, 1), :] + 4.0) * ((NODES - 1) / 8.0)
            vapour = columns[pl.ds(level + LEVELS, 1), :] * scale
            cloud = columns[pl.ds(level + 2 * LEVELS, 1), :] * scale
            hat = jnp.maximum(0.0, 1.0 - jnp.abs(warmth - node)) * vapour
            depth = bands_of(0, level) * scale
            share = depth * bands_of(BANDS, level)
            hat_hi, hat_lo = halves(hat)
            opt_hi, opt_lo = halves(
                jnp.where(spot < BANDS, depth, jnp.where(spot == BANDS, scale, cloud))
            )
            sca_hi, sca_lo = halves(jnp.where(spot < BANDS, share, 0.0))
            stacked = jnp.concatenate(
                [hat_hi, hat_hi, hat_lo, opt_hi, opt_hi, opt_lo, sca_hi, sca_lo], axis=0
            )
            optics[j] = jnp.dot(weights[...], stacked, preferred_element_type=F32)
        for lane in range(0, UNIT, LANES):
            lanes = slice(lane, lane + LANES)
            back = jnp.broadcast_to(1.66 * path[:, lanes], (half, LANES))
            for row in range(0, GPOINTS, half):
                rows = slice(row, row + half)
                straight = beam[rows, lanes]
                spread = glow[rows, lanes]
                for j in range(LEVEL_BLOCK):
                    total = 2.0 * over_groups(straight) + over_groups(spread)
                    if row == 0:
                        net[first + j, :, lanes] = total
                    else:
                        net[first + j, :, lanes] += total
                    loss = optics[j, rows, lanes]
                    part = optics[j, GPOINTS + row : GPOINTS + row + half, lanes]
                    through = straight * jnp.exp2(loss)
                    kept = jnp.exp2(back * (loss + part))
                    source = (through - straight) * (part * pl.reciprocal(loss, approx=True))
                    scatter_q[first + j, rows, lanes] = source
                    decay[first + j, rows, lanes] = kept
                    spread = spread * kept + source
                    straight = through
                beam[rows, lanes] = straight
                glow[rows, lanes] = spread
        return 0

    lax.fori_loop(0, LEVELS // LEVEL_BLOCK, down, 0)
    for lane in range(0, UNIT, LANES):
        lanes = slice(lane, lane + LANES)
        floor = 2.0 * beam[:, lanes] + glow[:, lanes]
        rising = aero[slot, lane // LANES, 2 * BANDS, 0:1, :] * floor
        net[LEVELS, :, lanes] = over_groups(floor - rising)

        def up(i, rising):
            for k in range(8):
                level = LEVELS - 1 - (i * 8 + k)
                rising = rising * decay[level, :, lanes] + scatter_q[level, :, lanes]
                net[level, :, lanes] -= over_groups(rising)
            return rising

        lax.fori_loop(0, LEVELS // 8, up, rising)


def rad_scratch():
    return [
        pltpu.VMEM((ROWS + 8, UNIT), F32),
        pltpu.VMEM((2, UNIT // LANES, AERO, PITCH, LANES), F32),
        pltpu.VMEM((LEVEL_BLOCK, 2 * GPOINTS, UNIT), F32),
        pltpu.VMEM((LEVELS, GPOINTS, UNIT), F32),
        pltpu.VMEM((LEVELS, GPOINTS, UNIT), F32),
        pltpu.VMEM((GPOINTS, UNIT), F32),
        pltpu.VMEM((GPOINTS, UNIT), F32),
        pltpu.VMEM((LEVELS + 1, 8, UNIT), F32),
    ]


def warm_kernel(role, mine, parent, slots_in, stepped, out):
    span = LEVELS // PER_TILE
    tiles = []
    for tile in range(DOMAINS // PER_TILE):
        parts = [mine[tile * PER_TILE + e] for e in range(PER_TILE)]
        tiles.append(
            jnp.concatenate([regroup(parts, lambda e: e - a) for a in range(PER_TILE)], axis=0)
        )
    heat = jnp.concatenate(tiles, axis=1)
    placed = ones_where(iota((DOMAINS * SLOT_COLS, COARSE), 0) == slots_in[...])
    coarse = exact_dot(heat, placed, 0)
    lineage = ones_where(iota((COARSE, CELLS), 0) == parent[...])
    fine = exact_dot(coarse, lineage, 0)
    out[...] = jnp.where(role[0] != SLOTS - 1, stepped[...] + 0.5 * fine, 0.0)


def near_core(x):
    return pltpu.with_memory_space_constraint(x, pltpu.VMEM)


def far(x):
    return pltpu.with_memory_space_constraint(x, pltpu.HBM)


def params():
    return pltpu.CompilerParams(vmem_limit_bytes=VMEM_LIMIT)


SMEM = pl.BlockSpec(memory_space=pltpu.SMEM)
VMEM = pl.BlockSpec(memory_space=pltpu.VMEM)
HBM = pl.BlockSpec(memory_space=pl.ANY)


def per_device(
    state, kappa, neighbours, parent, cos_zenith, routes, rad_albedo, aerosol_depth, aerosol_ssa,
    gas_table, cloud_ext, cloud_ssa, rayleigh, solar_weight,
):
    fields = state.reshape(ROWS, CELLS)
    near = jnp.transpose(neighbours, (1, 0, 2))
    slot = jnp.stack([lax.axis_index("grp"), lax.axis_index("dom") % 2]).astype(I32)
    last = SLOTS - 1
    depth = jnp.transpose(aerosol_depth[0], (1, 0, 2))
    ssa = jnp.transpose(aerosol_ssa[0], (1, 0, 2))

    message, places, edge_pair, edge_next, weights, solar, aero_two = pl.pallas_call(
        first_kernel,
        in_specs=[SMEM, SMEM] + [VMEM] * 10 + [HBM] * 3,
        out_specs=[VMEM] * 7,
        out_shape=[
            jax.ShapeDtypeStruct((DOMAINS * LINES, LANES), F32),
            jax.ShapeDtypeStruct((1, COARSE), I32),
            jax.ShapeDtypeStruct((ROWS + 8, LANES), F32),
            jax.ShapeDtypeStruct((ROWS + 8, LANES), F32),
            jax.ShapeDtypeStruct((2 * GPOINTS, 176), BF16),
            jax.ShapeDtypeStruct((GPOINTS, LANES), F32),
            pltpu.VMEM((2 * BANDS + 1, LEVELS, (DOMAINS + STAY) * SLOT_COLS), F32),
        ],
        scratch_shapes=[pltpu.SemaphoreType.DMA((3,))],
        compiler_params=params(),
        name="first",
    )(
        slot, far(jnp.transpose(routes, (0, 2, 1))), far(fields), far(parent), far(cos_zenith),
        far(kappa), far(near), far(gas_table.T), far(cloud_ext[None]), far(cloud_ssa[None]),
        far(rayleigh[None]), far(solar_weight[None]), far(depth), far(ssa), far(rad_albedo),
    )
    aero_two = lax.ppermute(aero_two, "grp", [(last, last - 1)])

    received = lax.all_to_all(
        message.reshape(DOMAINS, 1, LINES * LANES), "dom", 0, 0, tiled=True
    ).reshape(DOMAINS * LINES, LANES)
    from_third = lax.ppermute(received[STAY * LINES :], "grp", [(last - 1, last)])
    arrived = lax.ppermute(received, "grp", [(0, last), (1, last - 1)])

    heat_block = (UNIT_SENDERS, 8, LANES)
    fixed = [
        pl.BlockSpec((2 * GPOINTS, 176), lambda i, role: (0, 0)),
        pl.BlockSpec((GPOINTS, LANES), lambda i, role: (0, 0)),
    ]
    common = (far(depth), far(ssa), far(rad_albedo), near_core(aero_two))
    scratch = [
        pltpu.VMEM((UNIT_SENDERS * LINES, LANES), F32),
        *rad_scratch(),
        pltpu.SemaphoreType.DMA((2, UNIT // LANES, 3)),
    ]
    def swap(edge, offset):
        pairs = [
            (s * DOMAINS + (i + offset) % DOMAINS, s * DOMAINS + (i + 1 + offset) % DOMAINS)
            for s in range(last)
            for i in range(0, DOMAINS, 2)
        ]
        return lax.ppermute(edge, ("grp", "dom"), pairs + [(b, a) for a, b in pairs])

    of_pair = swap(edge_pair, 0)
    of_next = swap(edge_next, 1)

    def radiation(kernel, name, units, extra, *operands):
        return pl.pallas_call(
            kernel,
            grid_spec=pltpu.PrefetchScalarGridSpec(
                num_scalar_prefetch=1,
                grid=(units,),
                in_specs=fixed + [VMEM] * (len(operands) - extra) + [HBM] * (extra + 3) + [VMEM],
                out_specs=pl.BlockSpec(heat_block, lambda i, role: (i, 0, 0)),
                scratch_shapes=scratch,
            ),
            out_shape=jax.ShapeDtypeStruct((units * UNIT_SENDERS, 8, LANES), F32),
            compiler_params=params(),
            name=name,
        )(slot, weights, solar, *operands, *common)

    soon = radiation(soon_kernel, "soon", SOON, 0, near_core(received), near_core(from_third))
    later = radiation(
        later_kernel, "later", LATER, 1, near_core(arrived), near_core(of_pair), near_core(of_next), soon
    )

    extended = CELLS + 2 * LANES
    stepped = pl.pallas_call(
        diffuse_kernel,
        in_specs=[SMEM] + [VMEM] * 5 + [HBM],
        out_specs=VMEM,
        out_shape=jax.ShapeDtypeStruct((ROWS, CELLS), F32),
        scratch_shapes=[
            pltpu.VMEM((ROWS, extended), F32),
            pltpu.VMEM((1, extended), F32),
            pltpu.VMEM((8, extended), I32),
            pltpu.VMEM((TILES + 2, 3 * LANES, LANES), BF16),
        ],
        compiler_params=params(),
        name="diffuse",
    )(slot, far(fields), far(kappa), far(near), near_core(of_pair), near_core(of_next), later)

    third_back = lax.ppermute(soon, "grp", [(last, last - 1)])
    back = lax.ppermute(later, "grp", [(last, 0), (last - 1, 1)])
    own = jnp.concatenate([soon[:STAY], third_back[:MOVED]], axis=0)
    returning = jnp.where(slot[0] == last - 1, own, back)
    mine = lax.all_to_all(returning, "dom", 0, 0, tiled=True)

    warmed = pl.pallas_call(
        warm_kernel,
        grid=(1,),
        in_specs=[
            SMEM,
            VMEM,
            pl.BlockSpec((1, CELLS), lambda i: (0, 0)),
            pl.BlockSpec((1, COARSE), lambda i: (0, 0)),
            pl.BlockSpec((LEVELS, CELLS), lambda i: (0, 0)),
        ],
        out_specs=pl.BlockSpec((LEVELS, CELLS), lambda i: (0, 0)),
        out_shape=jax.ShapeDtypeStruct((ROWS, CELLS), F32),
        input_output_aliases={4: 0},
        compiler_params=params(),
        name="warm",
    )(slot, near_core(mine), far(parent), places, stepped)
    return warmed.reshape(1, FIELDS, LEVELS, CELLS)


def solution(mesh):
    return jax.shard_map(
        per_device,
        mesh=mesh,
        in_specs=(
            P("grp", None, None, "dom"),
            P("grp", "dom"),
            P("grp", None, "dom"),
            P("grp", "dom"),
            P("grp", "dom"),
            P(("grp", "dom"), None, None),
            P("grp", "dom"),
            P("grp", None, None, "dom"),
            P("grp", None, None, "dom"),
            P(),
            P(),
            P(),
            P(),
            P(),
        ),
        out_specs=P("grp", None, None, "dom"),
        check_vma=False,
    )
```

```python
import jax
import jax.numpy as jnp
from jax import lax
from jax.experimental import pallas as pl
from jax.experimental.pallas import tpu as pltpu
from jax.sharding import PartitionSpec as P

F32 = jnp.float32
BF16 = jnp.bfloat16
I32 = jnp.int32
HALO = 32
FIELDS, LEVELS, GPOINTS, BANDS, NODES = 3, 32, 112, 14, 32
ROWS = FIELDS * LEVELS
CELLS, COARSE = 2048, 512
LANES = 128
BLOCKS, BLOCK_COLS, MOST = 32, 16, 2
DOMAINS, SLOTS = 32, 4
SLOT_COLS = BLOCK_COLS * MOST
SPAN = ROWS // (LANES // SLOT_COLS)
LINES = SPAN + 1
PER_TILE = LANES // SLOT_COLS
TILES = CELLS // LANES
UNIT = 256
UNIT_SENDERS = UNIT // SLOT_COLS
STAY = 16
MOVED = DOMAINS - STAY
SOON = max(STAY, MOVED) // UNIT_SENDERS
LATER = DOMAINS // UNIT_SENDERS
LEVEL_BLOCK = 8
AERO = 2 * BANDS + 2
PITCH = LEVELS + 8
LOG2E = 1.4426950408889634
VMEM_LIMIT = 28 * 1024 * 1024


def halves(x):
    high = x.astype(BF16)
    return high, (x - high.astype(F32)).astype(BF16)


def thirds(x):
    high = x.astype(BF16)
    rest = x - high.astype(F32)
    middle = rest.astype(BF16)
    return high, middle, (rest - middle.astype(F32)).astype(BF16)


def exact_dot(x, chosen, contract):
    rows = x.shape[0]
    stacked = jnp.concatenate(thirds(x), axis=0)
    product = lax.dot_general(
        stacked, chosen, (((1,), (contract,)), ((), ())), preferred_element_type=F32
    )
    return product[:rows] + product[rows : 2 * rows] + product[2 * rows :]


def iota(shape, dim):
    return lax.broadcasted_iota(I32, shape, dim)


def ones_where(mask):
    return jnp.where(mask, 1.0, 0.0).astype(BF16)


def regroup(pieces, shift_of):
    group = iota(pieces[0].shape, 1) // SLOT_COLS
    result = None
    for k, piece in enumerate(pieces):
        shift = (shift_of(k) % PER_TILE) * SLOT_COLS
        moved = pltpu.roll(piece, shift, 1) if shift else piece
        result = moved if result is None else jnp.where(group == k, moved, result)
    return result


def column(row):
    n = row.shape[1]
    return jnp.sum(jnp.where(iota((n, n), 0) == iota((n, n), 1), row, 0.0), axis=1, keepdims=True)


def aerosol_copies(depth, ssa, albedo, target, begin, count, sems):
    lanes = pl.ds(begin, count)
    levels = pl.ds(0, LEVELS)
    return [
        pltpu.make_async_copy(
            depth.at[:, :, lanes], target.at[pl.ds(0, BANDS), levels], sems.at[0]
        ),
        pltpu.make_async_copy(
            ssa.at[:, :, lanes], target.at[pl.ds(BANDS, BANDS), levels], sems.at[1]
        ),
        pltpu.make_async_copy(
            albedo.at[:, lanes], target.at[2 * BANDS, pl.ds(0, 1)], sems.at[2]
        ),
    ]


def first_kernel(
    role, routes, state, parent, sun, kappa, near, gas, ext, ssa, ray, solar,
    aero_depth, aero_ssa, albedo,
    message, slots_out, edge_pair, edge_next, weights, solar_out, aero_two, sems,
):
    is_last = role[0] == SLOTS - 1

    @pl.when(jnp.logical_not(is_last))
    def _():
        for parity, above, below in ((0, edge_pair, edge_next), (1, edge_next, edge_pair)):
            @pl.when(role[1] == parity)
            def _():
                for edge, start in ((above, CELLS - LANES), (below, 0)):
                    here = slice(start, start + LANES)
                    edge[0:ROWS, :] = state[:, here]
                    others = [near[n, :, here].astype(F32) for n in range(3)]
                    edge[ROWS : ROWS + 8, :] = jnp.concatenate(
                        [kappa[:, here]] + others + [jnp.zeros((4, LANES), F32)], axis=0
                    )

        pack_columns(routes, state, parent, sun, message, slots_out)

    @pl.when(role[0] == SLOTS - 2)
    def _():
        radiation_weights(gas, ext, ssa, ray, solar, weights, solar_out)

    @pl.when(is_last)
    def _():
        start, count = DOMAINS * SLOT_COLS, (DOMAINS + STAY) * SLOT_COLS
        copies = aerosol_copies(aero_depth, aero_ssa, albedo, aero_two, start, count, sems)
        for copy in copies:
            copy.start()
        radiation_weights(gas, ext, ssa, ray, solar, weights, solar_out)
        for copy in copies:
            copy.wait()


def pack_columns(routes, state, parent, sun, message, slots_out):
    block = iota((1, COARSE), 1) // BLOCK_COLS
    target = jnp.zeros((1, COARSE), I32)
    for b in range(BLOCKS):
        target = jnp.where(block == b, routes[0, 0, b], target)
    arrival = jnp.zeros((1, COARSE), I32)
    for b in range(BLOCKS):
        same = (target == routes[0, 0, b]) & (block > b)
        arrival = arrival + jnp.where(same, 1, 0)
    place = (target * MOST + arrival) * BLOCK_COLS + iota((1, COARSE), 1) % BLOCK_COLS
    slots_out[...] = place

    lineage = ones_where(iota((COARSE, CELLS), 0) == parent[...])
    coarse = 0.25 * exact_dot(state[...], lineage, 1)
    sun_rows = jnp.where(iota((8, COARSE), 0) == 0, sun[...], 0.0)
    columns = jnp.concatenate([coarse, sun_rows], axis=0)
    placed = ones_where(iota((DOMAINS * SLOT_COLS, COARSE), 0) == place)
    packed = exact_dot(columns, placed, 1)
    for tile in range(DOMAINS // PER_TILE):
        part = packed[:, tile * LANES : (tile + 1) * LANES]
        for e in range(PER_TILE):
            first = (tile * PER_TILE + e) * LINES
            pieces = [part[a * SPAN : (a + 1) * SPAN] for a in range(PER_TILE)]
            message[first : first + SPAN, :] = regroup(pieces, lambda a: a - e)
            moved = pltpu.roll(part[ROWS:], ((-e) % PER_TILE) * SLOT_COLS, 1) if e else part[ROWS:]
            message[first + SPAN : first + LINES, :] = moved[0:1]


def radiation_weights(gas, ext, ssa, ray, solar, weights, solar_out):
    band = jnp.where(iota((GPOINTS, 16), 0) // 8 == iota((GPOINTS, 16), 1), 1.0, 0.0)
    spot = iota((GPOINTS, 16), 1)
    ext_col, ssa_col, ray_col = column(ext[...]), column(ssa[...]), column(ray[...])
    scatter_w = jnp.where(spot == BANDS, ray_col, jnp.where(spot == BANDS + 1, ssa_col * ext_col, 0.0))
    optical_w = jnp.where(spot == BANDS, ray_col, jnp.where(spot == BANDS + 1, ext_col, band))
    gas_hi, gas_lo = halves(gas[...].T)
    opt_hi, opt_lo = halves(optical_w)
    sca_hi, sca_lo = halves(scatter_w)
    none = jnp.zeros((GPOINTS, 16), F32)
    wide = jnp.zeros((GPOINTS, NODES), F32)
    upper = [gas_hi, gas_lo, gas_hi, opt_hi, opt_lo, opt_hi, none, none]
    lower = [wide, wide, wide, sca_hi, sca_lo, sca_hi, band, band]
    weights[0:GPOINTS, :] = (-jnp.concatenate([p.astype(F32) for p in upper], axis=1)).astype(BF16)
    weights[GPOINTS:, :] = jnp.concatenate([p.astype(F32) for p in lower], axis=1).astype(BF16)
    solar_out[...] = jnp.broadcast_to(column(solar[...]), (GPOINTS, LANES))


def diffuse_kernel(
    role, state, kappa, near, of_pair, of_next, _, out, fields, rates, goal, chosen,
):
    @pl.when(role[0] == SLOTS - 1)
    def _():
        out[...] = jnp.zeros_like(out)

    @pl.when(role[0] != SLOTS - 1)
    def _():
        even = role[1] == 0
        for edge, start, shift in (
            (jnp.where(even, of_next[...], of_pair[...]), 0, LANES - HALO - CELLS),
            (jnp.where(even, of_pair[...], of_next[...]), LANES + CELLS, LANES - HALO + CELLS),
        ):
            here = slice(start, start + LANES)
            fields[:, here] = edge[0:ROWS]
            rates[:, here] = edge[ROWS : ROWS + 1]
            goal[0:3, here] = edge[ROWS + 1 : ROWS + 4].astype(I32) + shift
        fields[:, LANES : LANES + CELLS] = state[...]
        rates[:, LANES : LANES + CELLS] = kappa[...]
        for n in range(3):
            goal[n : n + 1, LANES : LANES + CELLS] = near[n] + (LANES - HALO)
        window = 3 * LANES
        rows = iota((window, LANES), 0)

        def spread(tile):
            first = min(max(tile - 1, 0), TILES - 1)
            return first * LANES

        results = []
        for tile in range(TILES + 2):
            here = slice(tile * LANES, (tile + 1) * LANES)
            place = rows + spread(tile)
            count = jnp.zeros((window, LANES), F32)
            for n in range(3):
                count = count + jnp.where(place == goal[n : n + 1, here], 1.0, 0.0)
            picked = count.astype(BF16)
            chosen[tile] = picked
            own = fields[:, here]
            total = exact_dot(fields[:, spread(tile) : spread(tile) + window], picked, 0)
            results.append(own + rates[:, here] * (total - 3.0 * own))
        for tile, value in enumerate(results):
            fields[:, tile * LANES : (tile + 1) * LANES] = value
        for tile in range(1, TILES + 1):
            here = slice(tile * LANES, (tile + 1) * LANES)
            own = fields[:, here]
            total = exact_dot(fields[:, spread(tile) : spread(tile) + window], chosen[tile], 0)
            value = own + rates[:, here] * (total - 3.0 * own)
            out[:, (tile - 1) * LANES : tile * LANES] = value


def soon_kernel(
    role, weights, solar, received, from_third, depth, ssa, albedo, aero_two, out, *scratch
):
    is_third, is_last = role[0] == SLOTS - 2, role[0] == SLOTS - 1
    radiate_unit(
        (is_third, received, STAY // UNIT_SENDERS, DOMAINS // UNIT_SENDERS),
        (is_last, from_third, MOVED // UNIT_SENDERS, (2 * DOMAINS + STAY) // UNIT_SENDERS),
        weights, solar, depth, ssa, albedo, aero_two, out, *scratch,
    )


def later_kernel(
    role, weights, solar, arrived, _pair, _next, _soon, depth, ssa, albedo, aero_two, out, *scratch
):
    is_third, is_last = role[0] == SLOTS - 2, role[0] == SLOTS - 1
    radiate_unit(
        (is_third, arrived, LATER, 0), (is_last, arrived, LATER, 0),
        weights, solar, depth, ssa, albedo, aero_two, out, *scratch,
    )


def radiate_unit(
    third, last, weights, solar, depth, ssa, albedo, aero_two, out,
    profile, columns, aero, optics, scatter_q, decay, beam, glow, net, sems,
):
    step = pl.program_id(0)
    steps = pl.num_programs(0)
    is_third, third_profiles, third_units, third_first = third
    is_last, last_profiles, last_units, last_first = last

    def taken(unit):
        return (is_third & (unit < third_units)) | (is_last & (unit < last_units))

    active = taken(step)

    def copies(unit, slot):
        here, there = [], []
        for tile in range(UNIT // LANES):
            offset = tile * LANES
            lanes = pl.ds(pl.multiple_of((third_first + unit) * UNIT + offset, LANES), LANES)
            here.append(
                pltpu.make_async_copy(
                    aero_two.at[:, :, lanes],
                    aero.at[slot, tile, pl.ds(0, 2 * BANDS + 1), pl.ds(0, LEVELS)],
                    sems.at[slot, tile, 0],
                )
            )
            there += aerosol_copies(
                depth, ssa, albedo, aero.at[slot, tile],
                pl.multiple_of((last_first + unit) * UNIT + offset, LANES), LANES, sems.at[slot, tile],
            )
        return (is_third, here), (is_last, there)

    def begin(unit, slot):
        for chosen, descriptors in copies(unit, slot):
            @pl.when(chosen & taken(unit))
            def _():
                for descriptor in descriptors:
                    descriptor.start()

    slot = step % 2

    @pl.when(step == 0)
    def _():
        begin(step, slot)

    @pl.when(step + 1 < steps)
    def _():
        begin(step + 1, 1 - slot)

    for chosen, ref in ((is_third, third_profiles), (is_last, last_profiles)):
        @pl.when(chosen & active)
        def _():
            height = UNIT_SENDERS * LINES
            profile[...] = ref[pl.ds(pl.multiple_of(step * height, 8), height), :]

    @pl.when(active)
    def _():
        for tile in range(UNIT // LANES):
            lanes = slice(tile * LANES, (tile + 1) * LANES)
            starts = [(tile * PER_TILE + e) * LINES for e in range(PER_TILE)]
            parts = [profile[start : start + SPAN, :] for start in starts]
            for a in range(PER_TILE):
                columns[a * SPAN : (a + 1) * SPAN, lanes] = regroup(parts, lambda e: e - a)
            suns = [profile[start + SPAN : start + LINES, :] for start in starts]
            columns[ROWS : ROWS + 1, lanes] = regroup(suns, lambda e: e)
        for chosen, descriptors in copies(step, slot):
            @pl.when(chosen)
            def _():
                for descriptor in descriptors:
                    descriptor.wait()
        radiate(weights, solar, columns, aero, slot, optics, scatter_q, decay, beam, glow, net)
        heat = (net[0:LEVELS] - net[1 : LEVELS + 1]).sum(axis=1) * (LEVELS / GPOINTS)
        span = LEVELS // PER_TILE
        messages = []
        for tile in range(UNIT // LANES):
            part = heat[:, tile * LANES : (tile + 1) * LANES]
            pieces = [part[a * span : (a + 1) * span] for a in range(PER_TILE)]
            messages += [regroup(pieces, lambda a: a - e) for e in range(PER_TILE)]

        for e, message in enumerate(messages):
            out[e] = message


def over_groups(x):
    return x.reshape(x.shape[0] // 8, 8, LANES).sum(axis=0)


def radiate(weights, solar, columns, aero, slot, optics, scatter_q, decay, beam, glow, net):
    cosine = columns[ROWS : ROWS + 1, :]
    path = jnp.maximum(cosine, 0.1)
    scale = LOG2E / path
    beam[...] = solar[:, 0:1] * (0.5 * jnp.maximum(cosine, 0.0))
    glow[...] = jnp.zeros_like(glow)
    node = iota((NODES, UNIT), 0).astype(F32)
    spot = iota((16, UNIT), 0)
    half = GPOINTS // 2

    def bands_of(band, level):
        rows = pl.ds(band * PITCH + level, 16, stride=PITCH)
        tiles = [aero.at[slot, tile].reshape(AERO * PITCH, LANES) for tile in range(UNIT // LANES)]
        return jnp.concatenate([tile[rows, :] for tile in tiles], axis=1)

    def down(block, _):
        first = block * LEVEL_BLOCK
        for j in range(LEVEL_BLOCK):
            level = first + j
            warmth = (columns[pl.ds(level, 1), :] + 4.0) * ((NODES - 1) / 8.0)
            vapour = columns[pl.ds(level + LEVELS, 1), :] * scale
            cloud = columns[pl.ds(level + 2 * LEVELS, 1), :] * scale
            hat = jnp.maximum(0.0, 1.0 - jnp.abs(warmth - node)) * vapour
            depth = bands_of(0, level) * scale
            share = depth * bands_of(BANDS, level)
            hat_hi, hat_lo = halves(hat)
            opt_hi, opt_lo = halves(
                jnp.where(spot < BANDS, depth, jnp.where(spot == BANDS, scale, cloud))
            )
            sca_hi, sca_lo = halves(jnp.where(spot < BANDS, share, 0.0))
            stacked = jnp.concatenate(
                [hat_hi, hat_hi, hat_lo, opt_hi, opt_hi, opt_lo, sca_hi, sca_lo], axis=0
            )
            optics[j] = jnp.dot(weights[...], stacked, preferred_element_type=F32)
        for lane in range(0, UNIT, LANES):
            lanes = slice(lane, lane + LANES)
            back = jnp.broadcast_to(1.66 * path[:, lanes], (half, LANES))
            for row in range(0, GPOINTS, half):
                rows = slice(row, row + half)
                straight = beam[rows, lanes]
                spread = glow[rows, lanes]
                for j in range(LEVEL_BLOCK):
                    total = 2.0 * over_groups(straight) + over_groups(spread)
                    if row == 0:
                        net[first + j, :, lanes] = total
                    else:
                        net[first + j, :, lanes] += total
                    loss = optics[j, rows, lanes]
                    part = optics[j, GPOINTS + row : GPOINTS + row + half, lanes]
                    through = straight * jnp.exp2(loss)
                    kept = jnp.exp2(back * (loss + part))
                    source = (through - straight) * (part * pl.reciprocal(loss, approx=True))
                    scatter_q[first + j, rows, lanes] = source
                    decay[first + j, rows, lanes] = kept
                    spread = spread * kept + source
                    straight = through
                beam[rows, lanes] = straight
                glow[rows, lanes] = spread
        return 0

    lax.fori_loop(0, LEVELS // LEVEL_BLOCK, down, 0)
    for lane in range(0, UNIT, LANES):
        lanes = slice(lane, lane + LANES)
        floor = 2.0 * beam[:, lanes] + glow[:, lanes]
        rising = aero[slot, lane // LANES, 2 * BANDS, 0:1, :] * floor
        net[LEVELS, :, lanes] = over_groups(floor - rising)

        def up(i, rising):
            for k in range(8):
                level = LEVELS - 1 - (i * 8 + k)
                rising = rising * decay[level, :, lanes] + scatter_q[level, :, lanes]
                net[level, :, lanes] -= over_groups(rising)
            return rising

        lax.fori_loop(0, LEVELS // 8, up, rising)


def rad_scratch():
    return [
        pltpu.VMEM((ROWS + 8, UNIT), F32),
        pltpu.VMEM((2, UNIT // LANES, AERO, PITCH, LANES), F32),
        pltpu.VMEM((LEVEL_BLOCK, 2 * GPOINTS, UNIT), F32),
        pltpu.VMEM((LEVELS, GPOINTS, UNIT), F32),
        pltpu.VMEM((LEVELS, GPOINTS, UNIT), F32),
        pltpu.VMEM((GPOINTS, UNIT), F32),
        pltpu.VMEM((GPOINTS, UNIT), F32),
        pltpu.VMEM((LEVELS + 1, 8, UNIT), F32),
    ]


def columns_at(table, index):
    shape = (table.shape[0], LANES)
    tiles = []
    for start in range(0, index.shape[1], LANES):
        here = jnp.broadcast_to(index[:, start : start + LANES], shape)
        source, lane = here // LANES, here % LANES
        result = None
        for k in range(table.shape[1] // LANES):
            part = table[:, k * LANES : (k + 1) * LANES]
            found = jnp.take_along_axis(part, lane, axis=1, mode="promise_in_bounds")
            result = found if result is None else jnp.where(source == k, found, result)
        tiles.append(result)
    return jnp.concatenate(tiles, axis=1)


def warm_kernel(role, mine, parent, slots_in, stepped, out):
    span = LEVELS // PER_TILE
    tiles = []
    for tile in range(DOMAINS // PER_TILE):
        parts = [mine[tile * PER_TILE + e] for e in range(PER_TILE)]
        tiles.append(
            jnp.concatenate([regroup(parts, lambda e: e - a) for a in range(PER_TILE)], axis=0)
        )
    heat = jnp.concatenate(tiles, axis=1)
    coarse = columns_at(heat, slots_in[...])
    fine = columns_at(coarse, parent[...])
    out[...] = jnp.where(role[0] != SLOTS - 1, stepped[...] + 0.5 * fine, 0.0)


def near_core(x):
    return pltpu.with_memory_space_constraint(x, pltpu.VMEM)


def far(x):
    return pltpu.with_memory_space_constraint(x, pltpu.HBM)


def params():
    return pltpu.CompilerParams(vmem_limit_bytes=VMEM_LIMIT)


SMEM = pl.BlockSpec(memory_space=pltpu.SMEM)
VMEM = pl.BlockSpec(memory_space=pltpu.VMEM)
HBM = pl.BlockSpec(memory_space=pl.ANY)


def per_device(
    state, kappa, neighbours, parent, cos_zenith, routes, rad_albedo, aerosol_depth, aerosol_ssa,
    gas_table, cloud_ext, cloud_ssa, rayleigh, solar_weight,
):
    fields = state.reshape(ROWS, CELLS)
    near = jnp.transpose(neighbours, (1, 0, 2))
    slot = jnp.stack([lax.axis_index("grp"), lax.axis_index("dom") % 2]).astype(I32)
    last = SLOTS - 1
    depth = jnp.transpose(aerosol_depth[0], (1, 0, 2))
    ssa = jnp.transpose(aerosol_ssa[0], (1, 0, 2))

    message, places, edge_pair, edge_next, weights, solar, aero_two = pl.pallas_call(
        first_kernel,
        in_specs=[SMEM, SMEM] + [VMEM] * 10 + [HBM] * 3,
        out_specs=[VMEM] * 7,
        out_shape=[
            pltpu.VMEM((DOMAINS * LINES, LANES), F32),
            jax.ShapeDtypeStruct((1, COARSE), I32),
            pltpu.VMEM((ROWS + 8, LANES), F32),
            pltpu.VMEM((ROWS + 8, LANES), F32),
            jax.ShapeDtypeStruct((2 * GPOINTS, 176), BF16),
            jax.ShapeDtypeStruct((GPOINTS, LANES), F32),
            pltpu.VMEM((2 * BANDS + 1, LEVELS, (DOMAINS + STAY) * SLOT_COLS), F32),
        ],
        scratch_shapes=[pltpu.SemaphoreType.DMA((3,))],
        compiler_params=params(),
        name="first",
    )(
        slot, far(jnp.transpose(routes, (0, 2, 1))), far(fields), far(parent), far(cos_zenith),
        far(kappa), far(near), far(gas_table.T), far(cloud_ext[None]), far(cloud_ssa[None]),
        far(rayleigh[None]), far(solar_weight[None]), far(depth), far(ssa), far(rad_albedo),
    )
    aero_two = lax.ppermute(aero_two, "grp", [(last, last - 1)])

    received = lax.all_to_all(
        message.reshape(DOMAINS, 1, LINES * LANES), "dom", 0, 0, tiled=True
    ).reshape(DOMAINS * LINES, LANES)
    from_third = lax.ppermute(received[STAY * LINES :], "grp", [(last - 1, last)])
    arrived = lax.ppermute(received, "grp", [(0, last), (1, last - 1)])

    heat_block = (UNIT_SENDERS, 8, LANES)
    fixed = [
        pl.BlockSpec((2 * GPOINTS, 176), lambda i, role: (0, 0)),
        pl.BlockSpec((GPOINTS, LANES), lambda i, role: (0, 0)),
    ]
    common = (far(depth), far(ssa), far(rad_albedo), near_core(aero_two))
    scratch = [
        pltpu.VMEM((UNIT_SENDERS * LINES, LANES), F32),
        *rad_scratch(),
        pltpu.SemaphoreType.DMA((2, UNIT // LANES, 3)),
    ]
    def swap(edge, offset):
        pairs = [
            (s * DOMAINS + (i + offset) % DOMAINS, s * DOMAINS + (i + 1 + offset) % DOMAINS)
            for s in range(last)
            for i in range(0, DOMAINS, 2)
        ]
        return lax.ppermute(edge, ("grp", "dom"), pairs + [(b, a) for a, b in pairs])

    of_pair = swap(edge_pair, 0)
    of_next = swap(edge_next, 1)

    def radiation(kernel, name, units, extra, *operands):
        return pl.pallas_call(
            kernel,
            grid_spec=pltpu.PrefetchScalarGridSpec(
                num_scalar_prefetch=1,
                grid=(units,),
                in_specs=fixed + [VMEM] * (len(operands) - extra) + [HBM] * (extra + 3) + [VMEM],
                out_specs=pl.BlockSpec(heat_block, lambda i, role: (i, 0, 0)),
                scratch_shapes=scratch,
            ),
            out_shape=jax.ShapeDtypeStruct((units * UNIT_SENDERS, 8, LANES), F32),
            compiler_params=params(),
            name=name,
        )(slot, weights, solar, *operands, *common)

    soon = radiation(soon_kernel, "soon", SOON, 0, near_core(received), near_core(from_third))
    later = radiation(
        later_kernel, "later", LATER, 1, near_core(arrived), near_core(of_pair), near_core(of_next), soon
    )

    extended = CELLS + 2 * LANES
    stepped = pl.pallas_call(
        diffuse_kernel,
        in_specs=[SMEM] + [VMEM] * 5 + [HBM],
        out_specs=VMEM,
        out_shape=jax.ShapeDtypeStruct((ROWS, CELLS), F32),
        scratch_shapes=[
            pltpu.VMEM((ROWS, extended), F32),
            pltpu.VMEM((1, extended), F32),
            pltpu.VMEM((8, extended), I32),
            pltpu.VMEM((TILES + 2, 3 * LANES, LANES), BF16),
        ],
        compiler_params=params(),
        name="diffuse",
    )(slot, far(fields), far(kappa), far(near), near_core(of_pair), near_core(of_next), later)

    third_back = lax.ppermute(soon, "grp", [(last, last - 1)])
    back = lax.ppermute(later, "grp", [(last, 0), (last - 1, 1)])
    own = jnp.concatenate([soon[:STAY], third_back[:MOVED]], axis=0)
    returning = jnp.where(slot[0] == last - 1, own, back)
    mine = lax.all_to_all(returning, "dom", 0, 0, tiled=True)

    warmed = pl.pallas_call(
        warm_kernel,
        grid=(1,),
        in_specs=[
            SMEM,
            VMEM,
            pl.BlockSpec((1, CELLS), lambda i: (0, 0)),
            pl.BlockSpec((1, COARSE), lambda i: (0, 0)),
            pl.BlockSpec((LEVELS, CELLS), lambda i: (0, 0)),
        ],
        out_specs=pl.BlockSpec((LEVELS, CELLS), lambda i: (0, 0)),
        out_shape=jax.ShapeDtypeStruct((ROWS, CELLS), F32),
        input_output_aliases={4: 0},
        compiler_params=params(),
        name="warm",
    )(slot, near_core(mine), far(parent), places, stepped)
    return warmed.reshape(1, FIELDS, LEVELS, CELLS)


def solution(mesh):
    return jax.shard_map(
        per_device,
        mesh=mesh,
        in_specs=(
            P("grp", None, None, "dom"),
            P("grp", "dom"),
            P("grp", None, "dom"),
            P("grp", "dom"),
            P("grp", "dom"),
            P(("grp", "dom"), None, None),
            P("grp", "dom"),
            P("grp", None, None, "dom"),
            P("grp", None, None, "dom"),
            P(),
            P(),
            P(),
            P(),
            P(),
        ),
        out_specs=P("grp", None, None, "dom"),
        check_vma=False,
    )
```

```python
import jax
import jax.numpy as jnp
from jax import lax
from jax.experimental import pallas as pl
from jax.experimental.pallas import tpu as pltpu
from jax.sharding import PartitionSpec as P

F32 = jnp.float32
BF16 = jnp.bfloat16
I32 = jnp.int32
HALO = 32
FIELDS, LEVELS, GPOINTS, BANDS, NODES = 3, 32, 112, 14, 32
ROWS = FIELDS * LEVELS
CELLS, COARSE = 2048, 512
LANES = 128
BLOCKS, BLOCK_COLS, MOST = 32, 16, 2
DOMAINS, SLOTS = 32, 4
SLOT_COLS = BLOCK_COLS * MOST
SPAN = ROWS // (LANES // SLOT_COLS)
LINES = SPAN + 1
PER_TILE = LANES // SLOT_COLS
TILES = CELLS // LANES
UNIT = 256
UNIT_SENDERS = UNIT // SLOT_COLS
STAY = 8
MOVED = DOMAINS - STAY
SOON = max(STAY, MOVED) // UNIT_SENDERS
LATER = DOMAINS // UNIT_SENDERS
LEVEL_BLOCK = 8
AERO = 2 * BANDS + 2
PITCH = LEVELS + 8
LOG2E = 1.4426950408889634
VMEM_LIMIT = 28 * 1024 * 1024


def halves(x):
    high = x.astype(BF16)
    return high, (x - high.astype(F32)).astype(BF16)


def thirds(x):
    high = x.astype(BF16)
    rest = x - high.astype(F32)
    middle = rest.astype(BF16)
    return high, middle, (rest - middle.astype(F32)).astype(BF16)


def exact_dot(x, chosen, contract):
    rows = x.shape[0]
    stacked = jnp.concatenate(thirds(x), axis=0)
    product = lax.dot_general(
        stacked, chosen, (((1,), (contract,)), ((), ())), preferred_element_type=F32
    )
    return product[:rows] + product[rows : 2 * rows] + product[2 * rows :]


def iota(shape, dim):
    return lax.broadcasted_iota(I32, shape, dim)


def ones_where(mask):
    return jnp.where(mask, 1.0, 0.0).astype(BF16)


def regroup(pieces, shift_of):
    group = iota(pieces[0].shape, 1) // SLOT_COLS
    result = None
    for k, piece in enumerate(pieces):
        shift = (shift_of(k) % PER_TILE) * SLOT_COLS
        moved = pltpu.roll(piece, shift, 1) if shift else piece
        result = moved if result is None else jnp.where(group == k, moved, result)
    return result


def column(row):
    n = row.shape[1]
    return jnp.sum(jnp.where(iota((n, n), 0) == iota((n, n), 1), row, 0.0), axis=1, keepdims=True)


def aerosol_copies(depth, ssa, albedo, target, begin, count, sems):
    lanes = pl.ds(begin, count)
    levels = pl.ds(0, LEVELS)
    return [
        pltpu.make_async_copy(
            depth.at[:, :, lanes], target.at[pl.ds(0, BANDS), levels], sems.at[0]
        ),
        pltpu.make_async_copy(
            ssa.at[:, :, lanes], target.at[pl.ds(BANDS, BANDS), levels], sems.at[1]
        ),
        pltpu.make_async_copy(
            albedo.at[:, lanes], target.at[2 * BANDS, pl.ds(0, 1)], sems.at[2]
        ),
    ]


def first_kernel(
    role, routes, state, parent, sun, kappa, near, gas, ext, ssa, ray, solar,
    aero_depth, aero_ssa, albedo,
    message, slots_out, edge_pair, edge_next, weights, solar_out, aero_two, sems,
):
    is_last = role[0] == SLOTS - 1

    @pl.when(jnp.logical_not(is_last))
    def _():
        for parity, above, below in ((0, edge_pair, edge_next), (1, edge_next, edge_pair)):
            @pl.when(role[1] == parity)
            def _():
                for edge, start in ((above, CELLS - LANES), (below, 0)):
                    here = slice(start, start + LANES)
                    edge[0:ROWS, :] = state[:, here]
                    others = [near[n, :, here].astype(F32) for n in range(3)]
                    edge[ROWS : ROWS + 8, :] = jnp.concatenate(
                        [kappa[:, here]] + others + [jnp.zeros((4, LANES), F32)], axis=0
                    )

        pack_columns(routes, state, parent, sun, message, slots_out)

    @pl.when(role[0] == SLOTS - 2)
    def _():
        radiation_weights(gas, ext, ssa, ray, solar, weights, solar_out)

    @pl.when(is_last)
    def _():
        start, count = DOMAINS * SLOT_COLS, (DOMAINS + STAY) * SLOT_COLS
        copies = aerosol_copies(aero_depth, aero_ssa, albedo, aero_two, start, count, sems)
        for copy in copies:
            copy.start()
        radiation_weights(gas, ext, ssa, ray, solar, weights, solar_out)
        for copy in copies:
            copy.wait()


def pack_columns(routes, state, parent, sun, message, slots_out):
    block = iota((1, COARSE), 1) // BLOCK_COLS
    target = jnp.zeros((1, COARSE), I32)
    for b in range(BLOCKS):
        target = jnp.where(block == b, routes[0, 0, b], target)
    arrival = jnp.zeros((1, COARSE), I32)
    for b in range(BLOCKS):
        same = (target == routes[0, 0, b]) & (block > b)
        arrival = arrival + jnp.where(same, 1, 0)
    place = (target * MOST + arrival) * BLOCK_COLS + iota((1, COARSE), 1) % BLOCK_COLS
    slots_out[...] = place

    lineage = ones_where(iota((COARSE, CELLS), 0) == parent[...])
    coarse = 0.25 * exact_dot(state[...], lineage, 1)
    sun_rows = jnp.where(iota((8, COARSE), 0) == 0, sun[...], 0.0)
    columns = jnp.concatenate([coarse, sun_rows], axis=0)
    placed = ones_where(iota((DOMAINS * SLOT_COLS, COARSE), 0) == place)
    packed = exact_dot(columns, placed, 1)
    for tile in range(DOMAINS // PER_TILE):
        part = packed[:, tile * LANES : (tile + 1) * LANES]
        for e in range(PER_TILE):
            first = (tile * PER_TILE + e) * LINES
            pieces = [part[a * SPAN : (a + 1) * SPAN] for a in range(PER_TILE)]
            message[first : first + SPAN, :] = regroup(pieces, lambda a: a - e)
            moved = pltpu.roll(part[ROWS:], ((-e) % PER_TILE) * SLOT_COLS, 1) if e else part[ROWS:]
            message[first + SPAN : first + LINES, :] = moved[0:1]


def radiation_weights(gas, ext, ssa, ray, solar, weights, solar_out):
    band = jnp.where(iota((GPOINTS, 16), 0) // 8 == iota((GPOINTS, 16), 1), 1.0, 0.0)
    spot = iota((GPOINTS, 16), 1)
    ext_col, ssa_col, ray_col = column(ext[...]), column(ssa[...]), column(ray[...])
    scatter_w = jnp.where(spot == BANDS, ray_col, jnp.where(spot == BANDS + 1, ssa_col * ext_col, 0.0))
    optical_w = jnp.where(spot == BANDS, ray_col, jnp.where(spot == BANDS + 1, ext_col, band))
    gas_hi, gas_lo = halves(gas[...].T)
    opt_hi, opt_lo = halves(optical_w)
    sca_hi, sca_lo = halves(scatter_w)
    none = jnp.zeros((GPOINTS, 16), F32)
    wide = jnp.zeros((GPOINTS, NODES), F32)
    upper = [gas_hi, gas_lo, gas_hi, opt_hi, opt_lo, opt_hi, none, none]
    lower = [wide, wide, wide, sca_hi, sca_lo, sca_hi, band, band]
    weights[0:GPOINTS, :] = (-jnp.concatenate([p.astype(F32) for p in upper], axis=1)).astype(BF16)
    weights[GPOINTS:, :] = jnp.concatenate([p.astype(F32) for p in lower], axis=1).astype(BF16)
    solar_out[...] = jnp.broadcast_to(column(solar[...]), (GPOINTS, LANES))


def diffuse_kernel(
    role, state, kappa, near, of_pair, of_next, _, out, fields, rates, goal, chosen,
):
    @pl.when(role[0] == SLOTS - 1)
    def _():
        out[...] = jnp.zeros_like(out)

    @pl.when(role[0] != SLOTS - 1)
    def _():
        even = role[1] == 0
        for edge, start, shift in (
            (jnp.where(even, of_next[...], of_pair[...]), 0, LANES - HALO - CELLS),
            (jnp.where(even, of_pair[...], of_next[...]), LANES + CELLS, LANES - HALO + CELLS),
        ):
            here = slice(start, start + LANES)
            fields[:, here] = edge[0:ROWS]
            rates[:, here] = edge[ROWS : ROWS + 1]
            goal[0:3, here] = edge[ROWS + 1 : ROWS + 4].astype(I32) + shift
        fields[:, LANES : LANES + CELLS] = state[...]
        rates[:, LANES : LANES + CELLS] = kappa[...]
        for n in range(3):
            goal[n : n + 1, LANES : LANES + CELLS] = near[n] + (LANES - HALO)
        window = 3 * LANES
        rows = iota((window, LANES), 0)

        def spread(tile):
            first = min(max(tile - 1, 0), TILES - 1)
            return first * LANES

        results = []
        for tile in range(TILES + 2):
            here = slice(tile * LANES, (tile + 1) * LANES)
            place = rows + spread(tile)
            count = jnp.zeros((window, LANES), F32)
            for n in range(3):
                count = count + jnp.where(place == goal[n : n + 1, here], 1.0, 0.0)
            picked = count.astype(BF16)
            chosen[tile] = picked
            own = fields[:, here]
            total = exact_dot(fields[:, spread(tile) : spread(tile) + window], picked, 0)
            results.append(own + rates[:, here] * (total - 3.0 * own))
        for tile, value in enumerate(results):
            fields[:, tile * LANES : (tile + 1) * LANES] = value
        for tile in range(1, TILES + 1):
            here = slice(tile * LANES, (tile + 1) * LANES)
            own = fields[:, here]
            total = exact_dot(fields[:, spread(tile) : spread(tile) + window], chosen[tile], 0)
            value = own + rates[:, here] * (total - 3.0 * own)
            out[:, (tile - 1) * LANES : tile * LANES] = value


def soon_kernel(
    role, weights, solar, received, from_third, depth, ssa, albedo, aero_two, out, *scratch
):
    is_third, is_last = role[0] == SLOTS - 2, role[0] == SLOTS - 1
    radiate_unit(
        (is_third, received, STAY // UNIT_SENDERS, DOMAINS // UNIT_SENDERS),
        (is_last, from_third, MOVED // UNIT_SENDERS, (2 * DOMAINS + STAY) // UNIT_SENDERS),
        weights, solar, depth, ssa, albedo, aero_two, out, *scratch,
    )


def later_kernel(
    role, weights, solar, arrived, _pair, _next, _soon, depth, ssa, albedo, aero_two, out, *scratch
):
    is_third, is_last = role[0] == SLOTS - 2, role[0] == SLOTS - 1
    radiate_unit(
        (is_third, arrived, LATER, 0), (is_last, arrived, LATER, 0),
        weights, solar, depth, ssa, albedo, aero_two, out, *scratch,
    )


def radiate_unit(
    third, last, weights, solar, depth, ssa, albedo, aero_two, out,
    profile, columns, aero, optics, scatter_q, decay, beam, glow, net, sems,
):
    step = pl.program_id(0)
    steps = pl.num_programs(0)
    is_third, third_profiles, third_units, third_first = third
    is_last, last_profiles, last_units, last_first = last

    def taken(unit):
        return (is_third & (unit < third_units)) | (is_last & (unit < last_units))

    active = taken(step)

    def copies(unit, slot):
        here, there = [], []
        for tile in range(UNIT // LANES):
            offset = tile * LANES
            lanes = pl.ds(pl.multiple_of((third_first + unit) * UNIT + offset, LANES), LANES)
            here.append(
                pltpu.make_async_copy(
                    aero_two.at[:, :, lanes],
                    aero.at[slot, tile, pl.ds(0, 2 * BANDS + 1), pl.ds(0, LEVELS)],
                    sems.at[slot, tile, 0],
                )
            )
            there += aerosol_copies(
                depth, ssa, albedo, aero.at[slot, tile],
                pl.multiple_of((last_first + unit) * UNIT + offset, LANES), LANES, sems.at[slot, tile],
            )
        return (is_third, here), (is_last, there)

    def begin(unit, slot):
        for chosen, descriptors in copies(unit, slot):
            @pl.when(chosen & taken(unit))
            def _():
                for descriptor in descriptors:
                    descriptor.start()

    slot = step % 2

    @pl.when(step == 0)
    def _():
        begin(step, slot)

    @pl.when(step + 1 < steps)
    def _():
        begin(step + 1, 1 - slot)

    for chosen, ref in ((is_third, third_profiles), (is_last, last_profiles)):
        @pl.when(chosen & active)
        def _():
            height = UNIT_SENDERS * LINES
            profile[...] = ref[pl.ds(pl.multiple_of(step * height, 8), height), :]

    @pl.when(active)
    def _():
        for tile in range(UNIT // LANES):
            lanes = slice(tile * LANES, (tile + 1) * LANES)
            starts = [(tile * PER_TILE + e) * LINES for e in range(PER_TILE)]
            parts = [profile[start : start + SPAN, :] for start in starts]
            for a in range(PER_TILE):
                columns[a * SPAN : (a + 1) * SPAN, lanes] = regroup(parts, lambda e: e - a)
            suns = [profile[start + SPAN : start + LINES, :] for start in starts]
            columns[ROWS : ROWS + 1, lanes] = regroup(suns, lambda e: e)
        for chosen, descriptors in copies(step, slot):
            @pl.when(chosen)
            def _():
                for descriptor in descriptors:
                    descriptor.wait()
        radiate(weights, solar, columns, aero, slot, optics, scatter_q, decay, beam, glow, net)
        heat = (net[0:LEVELS] - net[1 : LEVELS + 1]).sum(axis=1) * (LEVELS / GPOINTS)
        span = LEVELS // PER_TILE
        messages = []
        for tile in range(UNIT // LANES):
            part = heat[:, tile * LANES : (tile + 1) * LANES]
            pieces = [part[a * span : (a + 1) * span] for a in range(PER_TILE)]
            messages += [regroup(pieces, lambda a: a - e) for e in range(PER_TILE)]

        for e, message in enumerate(messages):
            out[e] = message


def over_groups(x):
    return x.reshape(x.shape[0] // 8, 8, LANES).sum(axis=0)


def radiate(weights, solar, columns, aero, slot, optics, scatter_q, decay, beam, glow, net):
    cosine = columns[ROWS : ROWS + 1, :]
    path = jnp.maximum(cosine, 0.1)
    scale = LOG2E / path
    beam[...] = solar[:, 0:1] * (0.5 * jnp.maximum(cosine, 0.0))
    glow[...] = jnp.zeros_like(glow)
    node = iota((NODES, UNIT), 0).astype(F32)
    spot = iota((16, UNIT), 0)
    half = GPOINTS // 2

    def bands_of(band, level):
        rows = pl.ds(band * PITCH + level, 16, stride=PITCH)
        tiles = [aero.at[slot, tile].reshape(AERO * PITCH, LANES) for tile in range(UNIT // LANES)]
        return jnp.concatenate([tile[rows, :] for tile in tiles], axis=1)

    def down(block, _):
        first = block * LEVEL_BLOCK
        for j in range(LEVEL_BLOCK):
            level = first + j
            warmth = (columns[pl.ds(level, 1), :] + 4.0) * ((NODES - 1) / 8.0)
            vapour = columns[pl.ds(level + LEVELS, 1), :] * scale
            cloud = columns[pl.ds(level + 2 * LEVELS, 1), :] * scale
            hat = jnp.maximum(0.0, 1.0 - jnp.abs(warmth - node)) * vapour
            depth = bands_of(0, level) * scale
            share = depth * bands_of(BANDS, level)
            hat_hi, hat_lo = halves(hat)
            opt_hi, opt_lo = halves(
                jnp.where(spot < BANDS, depth, jnp.where(spot == BANDS, scale, cloud))
            )
            sca_hi, sca_lo = halves(jnp.where(spot < BANDS, share, 0.0))
            stacked = jnp.concatenate(
                [hat_hi, hat_hi, hat_lo, opt_hi, opt_hi, opt_lo, sca_hi, sca_lo], axis=0
            )
            optics[j] = jnp.dot(weights[...], stacked, preferred_element_type=F32)
        for lane in range(0, UNIT, LANES):
            lanes = slice(lane, lane + LANES)
            back = jnp.broadcast_to(1.66 * path[:, lanes], (half, LANES))
            for row in range(0, GPOINTS, half):
                rows = slice(row, row + half)
                straight = beam[rows, lanes]
                spread = glow[rows, lanes]
                for j in range(LEVEL_BLOCK):
                    total = 2.0 * over_groups(straight) + over_groups(spread)
                    if row == 0:
                        net[first + j, :, lanes] = total
                    else:
                        net[first + j, :, lanes] += total
                    loss = optics[j, rows, lanes]
                    part = optics[j, GPOINTS + row : GPOINTS + row + half, lanes]
                    through = straight * jnp.exp2(loss)
                    kept = jnp.exp2(back * (loss + part))
                    source = (through - straight) * (part * pl.reciprocal(loss, approx=True))
                    scatter_q[first + j, rows, lanes] = source
                    decay[first + j, rows, lanes] = kept
                    spread = spread * kept + source
                    straight = through
                beam[rows, lanes] = straight
                glow[rows, lanes] = spread
        return 0

    lax.fori_loop(0, LEVELS // LEVEL_BLOCK, down, 0)
    for lane in range(0, UNIT, LANES):
        lanes = slice(lane, lane + LANES)
        floor = 2.0 * beam[:, lanes] + glow[:, lanes]
        rising = aero[slot, lane // LANES, 2 * BANDS, 0:1, :] * floor
        net[LEVELS, :, lanes] = over_groups(floor - rising)

        def up(i, rising):
            for k in range(8):
                level = LEVELS - 1 - (i * 8 + k)
                rising = rising * decay[level, :, lanes] + scatter_q[level, :, lanes]
                net[level, :, lanes] -= over_groups(rising)
            return rising

        lax.fori_loop(0, LEVELS // 8, up, rising)


def rad_scratch():
    return [
        pltpu.VMEM((ROWS + 8, UNIT), F32),
        pltpu.VMEM((2, UNIT // LANES, AERO, PITCH, LANES), F32),
        pltpu.VMEM((LEVEL_BLOCK, 2 * GPOINTS, UNIT), F32),
        pltpu.VMEM((LEVELS, GPOINTS, UNIT), F32),
        pltpu.VMEM((LEVELS, GPOINTS, UNIT), F32),
        pltpu.VMEM((GPOINTS, UNIT), F32),
        pltpu.VMEM((GPOINTS, UNIT), F32),
        pltpu.VMEM((LEVELS + 1, 8, UNIT), F32),
    ]


def columns_at(table, index):
    shape = (table.shape[0], LANES)
    tiles = []
    for start in range(0, index.shape[1], LANES):
        here = jnp.broadcast_to(index[:, start : start + LANES], shape)
        source, lane = here // LANES, here % LANES
        result = None
        for k in range(table.shape[1] // LANES):
            part = table[:, k * LANES : (k + 1) * LANES]
            found = jnp.take_along_axis(part, lane, axis=1, mode="promise_in_bounds")
            result = found if result is None else jnp.where(source == k, found, result)
        tiles.append(result)
    return jnp.concatenate(tiles, axis=1)


def warm_kernel(role, mine, parent, slots_in, stepped, out):
    span = LEVELS // PER_TILE
    tiles = []
    for tile in range(DOMAINS // PER_TILE):
        parts = [mine[tile * PER_TILE + e] for e in range(PER_TILE)]
        tiles.append(
            jnp.concatenate([regroup(parts, lambda e: e - a) for a in range(PER_TILE)], axis=0)
        )
    heat = jnp.concatenate(tiles, axis=1)
    coarse = columns_at(heat, slots_in[...])
    fine = columns_at(coarse, parent[...])
    out[...] = jnp.where(role[0] != SLOTS - 1, stepped[...] + 0.5 * fine, 0.0)


def near_core(x):
    return pltpu.with_memory_space_constraint(x, pltpu.VMEM)


def far(x):
    return pltpu.with_memory_space_constraint(x, pltpu.HBM)


def params():
    return pltpu.CompilerParams(vmem_limit_bytes=VMEM_LIMIT)


SMEM = pl.BlockSpec(memory_space=pltpu.SMEM)
VMEM = pl.BlockSpec(memory_space=pltpu.VMEM)
HBM = pl.BlockSpec(memory_space=pl.ANY)


def per_device(
    state, kappa, neighbours, parent, cos_zenith, routes, rad_albedo, aerosol_depth, aerosol_ssa,
    gas_table, cloud_ext, cloud_ssa, rayleigh, solar_weight,
):
    fields = state.reshape(ROWS, CELLS)
    near = jnp.transpose(neighbours, (1, 0, 2))
    slot = jnp.stack([lax.axis_index("grp"), lax.axis_index("dom") % 2]).astype(I32)
    last = SLOTS - 1
    depth = jnp.transpose(aerosol_depth[0], (1, 0, 2))
    ssa = jnp.transpose(aerosol_ssa[0], (1, 0, 2))

    message, places, edge_pair, edge_next, weights, solar, aero_two = pl.pallas_call(
        first_kernel,
        in_specs=[SMEM, SMEM] + [VMEM] * 10 + [HBM] * 3,
        out_specs=[VMEM] * 7,
        out_shape=[
            pltpu.VMEM((DOMAINS * LINES, LANES), F32),
            jax.ShapeDtypeStruct((1, COARSE), I32),
            pltpu.VMEM((ROWS + 8, LANES), F32),
            pltpu.VMEM((ROWS + 8, LANES), F32),
            jax.ShapeDtypeStruct((2 * GPOINTS, 176), BF16),
            jax.ShapeDtypeStruct((GPOINTS, LANES), F32),
            pltpu.VMEM((2 * BANDS + 1, LEVELS, (DOMAINS + STAY) * SLOT_COLS), F32),
        ],
        scratch_shapes=[pltpu.SemaphoreType.DMA((3,))],
        compiler_params=params(),
        name="first",
    )(
        slot, far(jnp.transpose(routes, (0, 2, 1))), far(fields), far(parent), far(cos_zenith),
        far(kappa), far(near), far(gas_table.T), far(cloud_ext[None]), far(cloud_ssa[None]),
        far(rayleigh[None]), far(solar_weight[None]), far(depth), far(ssa), far(rad_albedo),
    )
    aero_two = lax.ppermute(aero_two, "grp", [(last, last - 1)])

    received = lax.all_to_all(
        message.reshape(DOMAINS, 1, LINES * LANES), "dom", 0, 0, tiled=True
    ).reshape(DOMAINS * LINES, LANES)
    from_third = lax.ppermute(received[STAY * LINES :], "grp", [(last - 1, last)])
    arrived = lax.ppermute(received, "grp", [(0, last), (1, last - 1)])

    heat_block = (UNIT_SENDERS, 8, LANES)
    fixed = [
        pl.BlockSpec((2 * GPOINTS, 176), lambda i, role: (0, 0)),
        pl.BlockSpec((GPOINTS, LANES), lambda i, role: (0, 0)),
    ]
    common = (far(depth), far(ssa), far(rad_albedo), near_core(aero_two))
    scratch = [
        pltpu.VMEM((UNIT_SENDERS * LINES, LANES), F32),
        *rad_scratch(),
        pltpu.SemaphoreType.DMA((2, UNIT // LANES, 3)),
    ]
    def swap(edge, offset):
        pairs = [
            (s * DOMAINS + (i + offset) % DOMAINS, s * DOMAINS + (i + 1 + offset) % DOMAINS)
            for s in range(last)
            for i in range(0, DOMAINS, 2)
        ]
        return lax.ppermute(edge, ("grp", "dom"), pairs + [(b, a) for a, b in pairs])

    of_pair = swap(edge_pair, 0)
    of_next = swap(edge_next, 1)

    def radiation(kernel, name, units, extra, *operands):
        return pl.pallas_call(
            kernel,
            grid_spec=pltpu.PrefetchScalarGridSpec(
                num_scalar_prefetch=1,
                grid=(units,),
                in_specs=fixed + [VMEM] * (len(operands) - extra) + [HBM] * (extra + 3) + [VMEM],
                out_specs=pl.BlockSpec(heat_block, lambda i, role: (i, 0, 0)),
                scratch_shapes=scratch,
            ),
            out_shape=jax.ShapeDtypeStruct((units * UNIT_SENDERS, 8, LANES), F32),
            compiler_params=params(),
            name=name,
        )(slot, weights, solar, *operands, *common)

    soon = radiation(soon_kernel, "soon", SOON, 0, near_core(received), near_core(from_third))
    later = radiation(
        later_kernel, "later", LATER, 1, near_core(arrived), near_core(of_pair), near_core(of_next), soon
    )

    extended = CELLS + 2 * LANES
    stepped = pl.pallas_call(
        diffuse_kernel,
        in_specs=[SMEM] + [VMEM] * 5 + [HBM],
        out_specs=VMEM,
        out_shape=jax.ShapeDtypeStruct((ROWS, CELLS), F32),
        scratch_shapes=[
            pltpu.VMEM((ROWS, extended), F32),
            pltpu.VMEM((1, extended), F32),
            pltpu.VMEM((8, extended), I32),
            pltpu.VMEM((TILES + 2, 3 * LANES, LANES), BF16),
        ],
        compiler_params=params(),
        name="diffuse",
    )(slot, far(fields), far(kappa), far(near), near_core(of_pair), near_core(of_next), later)

    third_back = lax.ppermute(soon, "grp", [(last, last - 1)])
    back = lax.ppermute(later, "grp", [(last, 0), (last - 1, 1)])
    own = jnp.concatenate([soon[:STAY], third_back[:MOVED]], axis=0)
    returning = jnp.where(slot[0] == last - 1, own, back)
    mine = lax.all_to_all(returning, "dom", 0, 0, tiled=True)

    warmed = pl.pallas_call(
        warm_kernel,
        grid=(1,),
        in_specs=[
            SMEM,
            VMEM,
            pl.BlockSpec((1, CELLS), lambda i: (0, 0)),
            pl.BlockSpec((1, COARSE), lambda i: (0, 0)),
            pl.BlockSpec((LEVELS, CELLS), lambda i: (0, 0)),
        ],
        out_specs=pl.BlockSpec((LEVELS, CELLS), lambda i: (0, 0)),
        out_shape=jax.ShapeDtypeStruct((ROWS, CELLS), F32),
        input_output_aliases={4: 0},
        compiler_params=params(),
        name="warm",
    )(slot, near_core(mine), far(parent), places, stepped)
    return warmed.reshape(1, FIELDS, LEVELS, CELLS)


def solution(mesh):
    return jax.shard_map(
        per_device,
        mesh=mesh,
        in_specs=(
            P("grp", None, None, "dom"),
            P("grp", "dom"),
            P("grp", None, "dom"),
            P("grp", "dom"),
            P("grp", "dom"),
            P(("grp", "dom"), None, None),
            P("grp", "dom"),
            P("grp", None, None, "dom"),
            P("grp", None, None, "dom"),
            P(),
            P(),
            P(),
            P(),
            P(),
        ),
        out_specs=P("grp", None, None, "dom"),
        check_vma=False,
    )
```

```python
import jax
import jax.numpy as jnp
from jax import lax
from jax.experimental import pallas as pl
from jax.experimental.pallas import tpu as pltpu
from jax.sharding import PartitionSpec as P

F32 = jnp.float32
BF16 = jnp.bfloat16
I32 = jnp.int32
HALO = 32
FIELDS, LEVELS, GPOINTS, BANDS, NODES = 3, 32, 112, 14, 32
ROWS = FIELDS * LEVELS
CELLS, COARSE = 2048, 512
LANES = 128
BLOCKS, BLOCK_COLS, MOST = 32, 16, 2
DOMAINS, SLOTS = 32, 4
SLOT_COLS = BLOCK_COLS * MOST
SPAN = ROWS // (LANES // SLOT_COLS)
LINES = SPAN + 1
PER_TILE = LANES // SLOT_COLS
TILES = CELLS // LANES
UNIT = 256
UNIT_SENDERS = UNIT // SLOT_COLS
STAY = 8
MOVED = DOMAINS - STAY
SOON = max(STAY, MOVED) // UNIT_SENDERS
LATER = DOMAINS // UNIT_SENDERS
LEVEL_BLOCK = 8
AERO = 2 * BANDS + 3
PITCH = LEVELS + 8
LOG2E = 1.4426950408889634
VMEM_LIMIT = 28 * 1024 * 1024


def halves(x):
    high = x.astype(BF16)
    return high, (x - high.astype(F32)).astype(BF16)


def thirds(x):
    high = x.astype(BF16)
    rest = x - high.astype(F32)
    middle = rest.astype(BF16)
    return high, middle, (rest - middle.astype(F32)).astype(BF16)


def exact_dot(x, chosen, contract):
    rows = x.shape[0]
    stacked = jnp.concatenate(thirds(x), axis=0)
    product = lax.dot_general(
        stacked, chosen, (((1,), (contract,)), ((), ())), preferred_element_type=F32
    )
    return product[:rows] + product[rows : 2 * rows] + product[2 * rows :]


def iota(shape, dim):
    return lax.broadcasted_iota(I32, shape, dim)


def ones_where(mask):
    return jnp.where(mask, 1.0, 0.0).astype(BF16)


def regroup(pieces, shift_of):
    group = iota(pieces[0].shape, 1) // SLOT_COLS
    result = None
    for k, piece in enumerate(pieces):
        shift = (shift_of(k) % PER_TILE) * SLOT_COLS
        moved = pltpu.roll(piece, shift, 1) if shift else piece
        result = moved if result is None else jnp.where(group == k, moved, result)
    return result


def column(row):
    n = row.shape[1]
    return jnp.sum(jnp.where(iota((n, n), 0) == iota((n, n), 1), row, 0.0), axis=1, keepdims=True)


def aerosol_copies(depth, ssa, albedo, target, begin, count, sems):
    lanes = pl.ds(begin, count)
    levels = pl.ds(0, LEVELS)
    return [
        pltpu.make_async_copy(
            depth.at[:, :, lanes], target.at[pl.ds(0, BANDS), levels], sems.at[0]
        ),
        pltpu.make_async_copy(
            ssa.at[:, :, lanes], target.at[pl.ds(BANDS, BANDS), levels], sems.at[1]
        ),
        pltpu.make_async_copy(
            albedo.at[:, lanes], target.at[2 * BANDS, pl.ds(0, 1)], sems.at[2]
        ),
    ]


def first_kernel(
    role, routes, state, parent, sun, kappa, near, gas, ext, ssa, ray, solar,
    aero_depth, aero_ssa, albedo,
    message, slots_out, edge_pair, edge_next, weights, solar_out, aero_two, sems,
):
    is_last = role[0] == SLOTS - 1

    @pl.when(jnp.logical_not(is_last))
    def _():
        for parity, above, below in ((0, edge_pair, edge_next), (1, edge_next, edge_pair)):
            @pl.when(role[1] == parity)
            def _():
                for edge, start in ((above, CELLS - LANES), (below, 0)):
                    here = slice(start, start + LANES)
                    edge[0:ROWS, :] = state[:, here]
                    others = [near[n, :, here].astype(F32) for n in range(3)]
                    edge[ROWS : ROWS + 8, :] = jnp.concatenate(
                        [kappa[:, here]] + others + [jnp.zeros((4, LANES), F32)], axis=0
                    )

        pack_columns(routes, state, parent, sun, message, slots_out)

    @pl.when(role[0] == SLOTS - 2)
    def _():
        radiation_weights(gas, ext, ssa, ray, solar, weights, solar_out)

    @pl.when(is_last)
    def _():
        start, count = DOMAINS * SLOT_COLS, (DOMAINS + STAY) * SLOT_COLS
        copies = aerosol_copies(aero_depth, aero_ssa, albedo, aero_two, start, count, sems)
        for copy in copies:
            copy.start()
        radiation_weights(gas, ext, ssa, ray, solar, weights, solar_out)
        for copy in copies:
            copy.wait()


def pack_columns(routes, state, parent, sun, message, slots_out):
    block = iota((1, COARSE), 1) // BLOCK_COLS
    target = jnp.zeros((1, COARSE), I32)
    for b in range(BLOCKS):
        target = jnp.where(block == b, routes[0, 0, b], target)
    arrival = jnp.zeros((1, COARSE), I32)
    for b in range(BLOCKS):
        same = (target == routes[0, 0, b]) & (block > b)
        arrival = arrival + jnp.where(same, 1, 0)
    place = (target * MOST + arrival) * BLOCK_COLS + iota((1, COARSE), 1) % BLOCK_COLS
    slots_out[...] = place

    lineage = ones_where(iota((COARSE, CELLS), 0) == parent[...])
    coarse = 0.25 * exact_dot(state[...], lineage, 1)
    sun_rows = jnp.where(iota((8, COARSE), 0) == 0, sun[...], 0.0)
    columns = jnp.concatenate([coarse, sun_rows], axis=0)
    placed = ones_where(iota((DOMAINS * SLOT_COLS, COARSE), 0) == place)
    packed = exact_dot(columns, placed, 1)
    for tile in range(DOMAINS // PER_TILE):
        part = packed[:, tile * LANES : (tile + 1) * LANES]
        for e in range(PER_TILE):
            first = (tile * PER_TILE + e) * LINES
            pieces = [part[a * SPAN : (a + 1) * SPAN] for a in range(PER_TILE)]
            message[first : first + SPAN, :] = regroup(pieces, lambda a: a - e)
            moved = pltpu.roll(part[ROWS:], ((-e) % PER_TILE) * SLOT_COLS, 1) if e else part[ROWS:]
            message[first + SPAN : first + LINES, :] = moved[0:1]


def radiation_weights(gas, ext, ssa, ray, solar, weights, solar_out):
    band = jnp.where(iota((GPOINTS, 16), 0) // 8 == iota((GPOINTS, 16), 1), 1.0, 0.0)
    spot = iota((GPOINTS, 16), 1)
    ext_col, ssa_col, ray_col = column(ext[...]), column(ssa[...]), column(ray[...])
    scatter_w = jnp.where(spot == BANDS, ray_col, jnp.where(spot == BANDS + 1, ssa_col * ext_col, 0.0))
    optical_w = jnp.where(spot == BANDS, ray_col, jnp.where(spot == BANDS + 1, ext_col, band))
    gas_hi, gas_lo = halves(gas[...].T)
    opt_hi, opt_lo = halves(optical_w)
    sca_hi, sca_lo = halves(scatter_w)
    none = jnp.zeros((GPOINTS, 16), F32)
    wide = jnp.zeros((GPOINTS, NODES), F32)
    upper = [gas_hi, gas_lo, gas_hi, opt_hi, opt_lo, opt_hi, none, none]
    lower = [wide, wide, wide, sca_hi, sca_lo, sca_hi, band, band]
    weights[0:GPOINTS, :] = (-jnp.concatenate([p.astype(F32) for p in upper], axis=1)).astype(BF16)
    weights[GPOINTS:, :] = jnp.concatenate([p.astype(F32) for p in lower], axis=1).astype(BF16)
    solar_out[...] = jnp.broadcast_to(column(solar[...]), (GPOINTS, LANES))


def diffuse_kernel(
    role, state, kappa, near, of_pair, of_next, _, out, fields, rates, goal, chosen,
):
    @pl.when(role[0] == SLOTS - 1)
    def _():
        out[...] = jnp.zeros_like(out)

    @pl.when(role[0] != SLOTS - 1)
    def _():
        even = role[1] == 0
        for edge, start, shift in (
            (jnp.where(even, of_next[...], of_pair[...]), 0, LANES - HALO - CELLS),
            (jnp.where(even, of_pair[...], of_next[...]), LANES + CELLS, LANES - HALO + CELLS),
        ):
            here = slice(start, start + LANES)
            fields[:, here] = edge[0:ROWS]
            rates[:, here] = edge[ROWS : ROWS + 1]
            goal[0:3, here] = edge[ROWS + 1 : ROWS + 4].astype(I32) + shift
        fields[:, LANES : LANES + CELLS] = state[...]
        rates[:, LANES : LANES + CELLS] = kappa[...]
        for n in range(3):
            goal[n : n + 1, LANES : LANES + CELLS] = near[n] + (LANES - HALO)
        window = 3 * LANES
        rows = iota((window, LANES), 0)

        def spread(tile):
            first = min(max(tile - 1, 0), TILES - 1)
            return first * LANES

        results = []
        for tile in range(TILES + 2):
            here = slice(tile * LANES, (tile + 1) * LANES)
            place = rows + spread(tile)
            count = jnp.zeros((window, LANES), F32)
            for n in range(3):
                count = count + jnp.where(place == goal[n : n + 1, here], 1.0, 0.0)
            picked = count.astype(BF16)
            chosen[tile] = picked
            own = fields[:, here]
            total = exact_dot(fields[:, spread(tile) : spread(tile) + window], picked, 0)
            results.append(own + rates[:, here] * (total - 3.0 * own))
        for tile, value in enumerate(results):
            fields[:, tile * LANES : (tile + 1) * LANES] = value
        for tile in range(1, TILES + 1):
            here = slice(tile * LANES, (tile + 1) * LANES)
            own = fields[:, here]
            total = exact_dot(fields[:, spread(tile) : spread(tile) + window], chosen[tile], 0)
            value = own + rates[:, here] * (total - 3.0 * own)
            out[:, (tile - 1) * LANES : tile * LANES] = value


def soon_kernel(
    role, weights, solar, received, from_third, depth, ssa, albedo, aero_two, out, *scratch
):
    is_third, is_last = role[0] == SLOTS - 2, role[0] == SLOTS - 1
    radiate_unit(
        (is_third, received, STAY // UNIT_SENDERS, DOMAINS // UNIT_SENDERS),
        (is_last, from_third, MOVED // UNIT_SENDERS, (2 * DOMAINS + STAY) // UNIT_SENDERS),
        weights, solar, depth, ssa, albedo, aero_two, out, *scratch,
    )


def later_kernel(
    role, weights, solar, arrived, _pair, _next, _soon, depth, ssa, albedo, aero_two, out, *scratch
):
    is_third, is_last = role[0] == SLOTS - 2, role[0] == SLOTS - 1
    radiate_unit(
        (is_third, arrived, LATER, 0), (is_last, arrived, LATER, 0),
        weights, solar, depth, ssa, albedo, aero_two, out, *scratch,
    )


def radiate_unit(
    third, last, weights, solar, depth, ssa, albedo, aero_two, out,
    profile, columns, aero, optics, scatter_q, decay, beam, glow, net, sems,
):
    step = pl.program_id(0)
    steps = pl.num_programs(0)
    is_third, third_profiles, third_units, third_first = third
    is_last, last_profiles, last_units, last_first = last

    def taken(unit):
        return (is_third & (unit < third_units)) | (is_last & (unit < last_units))

    active = taken(step)

    def copies(unit, slot):
        here, there = [], []
        for tile in range(UNIT // LANES):
            offset = tile * LANES
            lanes = pl.ds(pl.multiple_of((third_first + unit) * UNIT + offset, LANES), LANES)
            here.append(
                pltpu.make_async_copy(
                    aero_two.at[:, :, lanes],
                    aero.at[slot, tile, pl.ds(0, 2 * BANDS + 1), pl.ds(0, LEVELS)],
                    sems.at[slot, tile, 0],
                )
            )
            there += aerosol_copies(
                depth, ssa, albedo, aero.at[slot, tile],
                pl.multiple_of((last_first + unit) * UNIT + offset, LANES), LANES, sems.at[slot, tile],
            )
        return (is_third, here), (is_last, there)

    def begin(unit, slot):
        for chosen, descriptors in copies(unit, slot):
            @pl.when(chosen & taken(unit))
            def _():
                for descriptor in descriptors:
                    descriptor.start()

    slot = step % 2

    @pl.when(step == 0)
    def _():
        begin(step, slot)

    @pl.when(step + 1 < steps)
    def _():
        begin(step + 1, 1 - slot)

    for chosen, ref in ((is_third, third_profiles), (is_last, last_profiles)):
        @pl.when(chosen & active)
        def _():
            height = UNIT_SENDERS * LINES
            profile[...] = ref[pl.ds(pl.multiple_of(step * height, 8), height), :]

    @pl.when(active)
    def _():
        for tile in range(UNIT // LANES):
            lanes = slice(tile * LANES, (tile + 1) * LANES)
            starts = [(tile * PER_TILE + e) * LINES for e in range(PER_TILE)]
            parts = [profile[start : start + SPAN, :] for start in starts]
            for a in range(PER_TILE):
                columns[a * SPAN : (a + 1) * SPAN, lanes] = regroup(parts, lambda e: e - a)
            suns = [profile[start + SPAN : start + LINES, :] for start in starts]
            columns[ROWS : ROWS + 1, lanes] = regroup(suns, lambda e: e)
        for chosen, descriptors in copies(step, slot):
            @pl.when(chosen)
            def _():
                for descriptor in descriptors:
                    descriptor.wait()
        radiate(weights, solar, columns, aero, slot, optics, scatter_q, decay, beam, glow, net)
        heat = (net[0:LEVELS] - net[1 : LEVELS + 1]).sum(axis=1) * (LEVELS / GPOINTS)
        span = LEVELS // PER_TILE
        messages = []
        for tile in range(UNIT // LANES):
            part = heat[:, tile * LANES : (tile + 1) * LANES]
            pieces = [part[a * span : (a + 1) * span] for a in range(PER_TILE)]
            messages += [regroup(pieces, lambda a: a - e) for e in range(PER_TILE)]

        for e, message in enumerate(messages):
            out[e] = message


def over_groups(x):
    return x.reshape(x.shape[0] // 8, 8, LANES).sum(axis=0)


def radiate(weights, solar, columns, aero, slot, optics, scatter_q, decay, beam, glow, net):
    cosine = columns[ROWS : ROWS + 1, :]
    path = jnp.maximum(cosine, 0.1)
    scale = LOG2E / path
    beam[...] = solar[:, 0:1] * (0.5 * jnp.maximum(cosine, 0.0))
    glow[...] = jnp.zeros_like(glow)
    node = iota((NODES, UNIT), 0).astype(F32)
    spot = iota((16, UNIT), 0)
    half = GPOINTS // 2

    def bands_of(band, level):
        rows = pl.ds(band * PITCH + level, 16, stride=PITCH)
        tiles = [aero.at[slot, tile].reshape(AERO * PITCH, LANES) for tile in range(UNIT // LANES)]
        return jnp.concatenate([tile[rows, :] for tile in tiles], axis=1)

    def down(block, _):
        first = block * LEVEL_BLOCK
        for j in range(LEVEL_BLOCK):
            level = first + j
            warmth = (columns[pl.ds(level, 1), :] + 4.0) * ((NODES - 1) / 8.0)
            vapour = columns[pl.ds(level + LEVELS, 1), :] * scale
            cloud = columns[pl.ds(level + 2 * LEVELS, 1), :] * scale
            hat = jnp.maximum(0.0, 1.0 - jnp.abs(warmth - node)) * vapour
            depth = bands_of(0, level) * scale
            share = depth * bands_of(BANDS, level)
            hat_hi, hat_lo = halves(hat)
            opt_hi, opt_lo = halves(
                jnp.where(spot < BANDS, depth, jnp.where(spot == BANDS, scale, cloud))
            )
            sca_hi, sca_lo = halves(jnp.where(spot < BANDS, share, 0.0))
            stacked = jnp.concatenate(
                [hat_hi, hat_hi, hat_lo, opt_hi, opt_hi, opt_lo, sca_hi, sca_lo], axis=0
            )
            optics[j] = jnp.dot(weights[...], stacked, preferred_element_type=F32)
        for lane in range(0, UNIT, LANES):
            lanes = slice(lane, lane + LANES)
            back = jnp.broadcast_to(1.66 * path[:, lanes], (half, LANES))
            for row in range(0, GPOINTS, half):
                rows = slice(row, row + half)
                straight = beam[rows, lanes]
                spread = glow[rows, lanes]
                for j in range(LEVEL_BLOCK):
                    total = 2.0 * over_groups(straight) + over_groups(spread)
                    if row == 0:
                        net[first + j, :, lanes] = total
                    else:
                        net[first + j, :, lanes] += total
                    loss = optics[j, rows, lanes]
                    part = optics[j, GPOINTS + row : GPOINTS + row + half, lanes]
                    through = straight * jnp.exp2(loss)
                    kept = jnp.exp2(back * (loss + part))
                    source = (through - straight) * (part * pl.reciprocal(loss, approx=True))
                    scatter_q[first + j, rows, lanes] = source
                    decay[first + j, rows, lanes] = kept
                    spread = spread * kept + source
                    straight = through
                beam[rows, lanes] = straight
                glow[rows, lanes] = spread
        return 0

    lax.fori_loop(0, LEVELS // LEVEL_BLOCK, down, 0)
    for lane in range(0, UNIT, LANES):
        lanes = slice(lane, lane + LANES)
        floor = 2.0 * beam[:, lanes] + glow[:, lanes]
        rising = aero[slot, lane // LANES, 2 * BANDS, 0:1, :] * floor
        net[LEVELS, :, lanes] = over_groups(floor - rising)

        def up(i, rising):
            for k in range(8):
                level = LEVELS - 1 - (i * 8 + k)
                rising = rising * decay[level, :, lanes] + scatter_q[level, :, lanes]
                net[level, :, lanes] -= over_groups(rising)
            return rising

        lax.fori_loop(0, LEVELS // 8, up, rising)


def rad_scratch():
    return [
        pltpu.VMEM((ROWS + 8, UNIT), F32),
        pltpu.VMEM((2, UNIT // LANES, AERO, PITCH, LANES), F32),
        pltpu.VMEM((LEVEL_BLOCK, 2 * GPOINTS, UNIT), F32),
        pltpu.VMEM((LEVELS, GPOINTS, UNIT), F32),
        pltpu.VMEM((LEVELS, GPOINTS, UNIT), F32),
        pltpu.VMEM((GPOINTS, UNIT), F32),
        pltpu.VMEM((GPOINTS, UNIT), F32),
        pltpu.VMEM((LEVELS + 1, 8, UNIT), F32),
    ]


def columns_at(table, index):
    shape = (table.shape[0], LANES)
    tiles = []
    for start in range(0, index.shape[1], LANES):
        here = jnp.broadcast_to(index[:, start : start + LANES], shape)
        source, lane = here // LANES, here % LANES
        result = None
        for k in range(table.shape[1] // LANES):
            part = table[:, k * LANES : (k + 1) * LANES]
            found = jnp.take_along_axis(part, lane, axis=1, mode="promise_in_bounds")
            result = found if result is None else jnp.where(source == k, found, result)
        tiles.append(result)
    return jnp.concatenate(tiles, axis=1)


def warm_kernel(role, mine, parent, slots_in, stepped, out):
    span = LEVELS // PER_TILE
    tiles = []
    for tile in range(DOMAINS // PER_TILE):
        parts = [mine[tile * PER_TILE + e] for e in range(PER_TILE)]
        tiles.append(
            jnp.concatenate([regroup(parts, lambda e: e - a) for a in range(PER_TILE)], axis=0)
        )
    heat = jnp.concatenate(tiles, axis=1)
    coarse = columns_at(heat, slots_in[...])
    fine = columns_at(coarse, parent[...])
    out[...] = jnp.where(role[0] != SLOTS - 1, stepped[...] + 0.5 * fine, 0.0)


def near_core(x):
    return pltpu.with_memory_space_constraint(x, pltpu.VMEM)


def far(x):
    return pltpu.with_memory_space_constraint(x, pltpu.HBM)


def params():
    return pltpu.CompilerParams(vmem_limit_bytes=VMEM_LIMIT)


SMEM = pl.BlockSpec(memory_space=pltpu.SMEM)
VMEM = pl.BlockSpec(memory_space=pltpu.VMEM)
HBM = pl.BlockSpec(memory_space=pl.ANY)


def per_device(
    state, kappa, neighbours, parent, cos_zenith, routes, rad_albedo, aerosol_depth, aerosol_ssa,
    gas_table, cloud_ext, cloud_ssa, rayleigh, solar_weight,
):
    fields = state.reshape(ROWS, CELLS)
    near = jnp.transpose(neighbours, (1, 0, 2))
    slot = jnp.stack([lax.axis_index("grp"), lax.axis_index("dom") % 2]).astype(I32)
    last = SLOTS - 1
    depth = jnp.transpose(aerosol_depth[0], (1, 0, 2))
    ssa = jnp.transpose(aerosol_ssa[0], (1, 0, 2))

    message, places, edge_pair, edge_next, weights, solar, aero_two = pl.pallas_call(
        first_kernel,
        in_specs=[SMEM, SMEM] + [VMEM] * 10 + [HBM] * 3,
        out_specs=[VMEM] * 7,
        out_shape=[
            pltpu.VMEM((DOMAINS * LINES, LANES), F32),
            jax.ShapeDtypeStruct((1, COARSE), I32),
            pltpu.VMEM((ROWS + 8, LANES), F32),
            pltpu.VMEM((ROWS + 8, LANES), F32),
            jax.ShapeDtypeStruct((2 * GPOINTS, 176), BF16),
            jax.ShapeDtypeStruct((GPOINTS, LANES), F32),
            pltpu.VMEM((2 * BANDS + 1, LEVELS, (DOMAINS + STAY) * SLOT_COLS), F32),
        ],
        scratch_shapes=[pltpu.SemaphoreType.DMA((3,))],
        compiler_params=params(),
        name="first",
    )(
        slot, far(jnp.transpose(routes, (0, 2, 1))), far(fields), far(parent), far(cos_zenith),
        far(kappa), far(near), far(gas_table.T), far(cloud_ext[None]), far(cloud_ssa[None]),
        far(rayleigh[None]), far(solar_weight[None]), far(depth), far(ssa), far(rad_albedo),
    )
    aero_two = lax.ppermute(aero_two, "grp", [(last, last - 1)])

    received = lax.all_to_all(
        message.reshape(DOMAINS, 1, LINES * LANES), "dom", 0, 0, tiled=True
    ).reshape(DOMAINS * LINES, LANES)
    from_third = lax.ppermute(received[STAY * LINES :], "grp", [(last - 1, last)])
    arrived = lax.ppermute(received, "grp", [(0, last), (1, last - 1)])

    heat_block = (UNIT_SENDERS, 8, LANES)
    fixed = [
        pl.BlockSpec((2 * GPOINTS, 176), lambda i, role: (0, 0)),
        pl.BlockSpec((GPOINTS, LANES), lambda i, role: (0, 0)),
    ]
    common = (far(depth), far(ssa), far(rad_albedo), near_core(aero_two))
    scratch = [
        pltpu.VMEM((UNIT_SENDERS * LINES, LANES), F32),
        *rad_scratch(),
        pltpu.SemaphoreType.DMA((2, UNIT // LANES, 3)),
    ]
    def swap(edge, offset):
        pairs = [
            (s * DOMAINS + (i + offset) % DOMAINS, s * DOMAINS + (i + 1 + offset) % DOMAINS)
            for s in range(last)
            for i in range(0, DOMAINS, 2)
        ]
        return lax.ppermute(edge, ("grp", "dom"), pairs + [(b, a) for a, b in pairs])

    of_pair = swap(edge_pair, 0)
    of_next = swap(edge_next, 1)

    def radiation(kernel, name, units, extra, *operands):
        return pl.pallas_call(
            kernel,
            grid_spec=pltpu.PrefetchScalarGridSpec(
                num_scalar_prefetch=1,
                grid=(units,),
                in_specs=fixed + [VMEM] * (len(operands) - extra) + [HBM] * (extra + 3) + [VMEM],
                out_specs=pl.BlockSpec(heat_block, lambda i, role: (i, 0, 0)),
                scratch_shapes=scratch,
            ),
            out_shape=jax.ShapeDtypeStruct((units * UNIT_SENDERS, 8, LANES), F32),
            compiler_params=params(),
            name=name,
        )(slot, weights, solar, *operands, *common)

    soon = radiation(soon_kernel, "soon", SOON, 0, near_core(received), near_core(from_third))
    later = radiation(
        later_kernel, "later", LATER, 1, near_core(arrived), near_core(of_pair), near_core(of_next), soon
    )

    extended = CELLS + 2 * LANES
    stepped = pl.pallas_call(
        diffuse_kernel,
        in_specs=[SMEM] + [VMEM] * 5 + [HBM],
        out_specs=VMEM,
        out_shape=jax.ShapeDtypeStruct((ROWS, CELLS), F32),
        scratch_shapes=[
            pltpu.VMEM((ROWS, extended), F32),
            pltpu.VMEM((1, extended), F32),
            pltpu.VMEM((8, extended), I32),
            pltpu.VMEM((TILES + 2, 3 * LANES, LANES), BF16),
        ],
        compiler_params=params(),
        name="diffuse",
    )(slot, far(fields), far(kappa), far(near), near_core(of_pair), near_core(of_next), later)

    third_back = lax.ppermute(soon, "grp", [(last, last - 1)])
    back = lax.ppermute(later, "grp", [(last, 0), (last - 1, 1)])
    own = jnp.concatenate([soon[:STAY], third_back[:MOVED]], axis=0)
    returning = jnp.where(slot[0] == last - 1, own, back)
    mine = lax.all_to_all(returning, "dom", 0, 0, tiled=True)

    warmed = pl.pallas_call(
        warm_kernel,
        grid=(1,),
        in_specs=[
            SMEM,
            VMEM,
            pl.BlockSpec((1, CELLS), lambda i: (0, 0)),
            pl.BlockSpec((1, COARSE), lambda i: (0, 0)),
            pl.BlockSpec((LEVELS, CELLS), lambda i: (0, 0)),
        ],
        out_specs=pl.BlockSpec((LEVELS, CELLS), lambda i: (0, 0)),
        out_shape=jax.ShapeDtypeStruct((ROWS, CELLS), F32),
        input_output_aliases={4: 0},
        compiler_params=params(),
        name="warm",
    )(slot, near_core(mine), far(parent), places, stepped)
    return warmed.reshape(1, FIELDS, LEVELS, CELLS)


def solution(mesh):
    return jax.shard_map(
        per_device,
        mesh=mesh,
        in_specs=(
            P("grp", None, None, "dom"),
            P("grp", "dom"),
            P("grp", None, "dom"),
            P("grp", "dom"),
            P("grp", "dom"),
            P(("grp", "dom"), None, None),
            P("grp", "dom"),
            P("grp", None, None, "dom"),
            P("grp", None, None, "dom"),
            P(),
            P(),
            P(),
            P(),
            P(),
        ),
        out_specs=P("grp", None, None, "dom"),
        check_vma=False,
    )
```
